128 devices in a mesh: ctx: 16 (over z, y_hi, core), shard: 8 (over x, y_lo).
Axes of the slice: x: 4, y: 4 (y_hi: 2, y_lo: 2; y = y_hi * 2 + y_lo), z: 4, core: 2. Of those that a mesh axis runs over, the one named last changes fastest.
Arguments:
- tokens: bfloat16 [16, 16, 64, 1024], P('ctx', 'shard'), may hold values from -6 to 6
- lengths: int32 [16], P('shard'), may hold values from 256 to 1024, as said below
- block_pairs: int32 [16], replicated, may hold values from 0 to 15, each once
- ln1_gain: bfloat16 [1024], P('shard'), may hold values from 0.5 to 1.5
- ln1_bias: bfloat16 [1024], P('shard'), may hold values from -1.1953125 to 1.1953125
- w_qkv: bfloat16 [1024, 3072], P('shard'), may hold values from -0.1875 to 0.1875
- query_bias: bfloat16 [1024], P('shard'), may hold values from -1.796875 to 1.796875
- value_bias: bfloat16 [1024], P('shard'), may hold values from -0.59765625 to 0.59765625
- w_out: bfloat16 [1024, 1024], P('shard'), may hold values from -0.75 to 0.75
- out_bias: bfloat16 [1024], P('shard'), may hold values from -0.59765625 to 0.59765625
- ln2_gain: bfloat16 [1024], P('shard'), may hold values from 0.5 to 1.5
- ln2_bias: bfloat16 [1024], P('shard'), may hold values from -1.1953125 to 1.1953125
- w_fc1: bfloat16 [1024, 4096], P('shard'), may hold values from -0.1875 to 0.1875
- fc1_bias: bfloat16 [4096], P('shard'), may hold values from -1.796875 to 1.796875
- w_fc2: bfloat16 [4096, 1024], P('shard'), may hold values from -0.09375 to 0.09375
- fc2_bias: bfloat16 [1024], P('shard'), may hold values from -0.59765625 to 0.59765625
- out_cotangent: bfloat16 [16, 16, 64, 1024], P('ctx', 'shard'), may hold values from -6 to 6
Outputs:
- layer_out: bfloat16 [16, 16, 64, 1024], P('ctx', 'shard')
- input_grad: bfloat16 [16, 16, 64, 1024], P('ctx', 'shard')
- grad_ln1_gain: float32 [1024], P(('ctx', 'shard'))
- grad_ln1_bias: float32 [1024], P(('ctx', 'shard'))
- grad_w_qkv: float32 [1024, 3072], P(('ctx', 'shard'))
- grad_query_bias: float32 [1024], P(('ctx', 'shard'))
- grad_value_bias: float32 [1024], P(('ctx', 'shard'))
- grad_w_out: float32 [1024, 1024], P(('ctx', 'shard'))
- grad_out_bias: float32 [1024], P(('ctx', 'shard'))
- grad_ln2_gain: float32 [1024], P(('ctx', 'shard'))
- grad_ln2_bias: float32 [1024], P(('ctx', 'shard'))
- grad_w_fc1: float32 [1024, 4096], P(('ctx', 'shard'))
- grad_fc1_bias: float32 [4096], P(('ctx', 'shard'))
- grad_w_fc2: float32 [4096, 1024], P(('ctx', 'shard'))
- grad_fc2_bias: float32 [1024], P(('ctx', 'shard'))
The draws below stay inside these ranges and needn't reach their ends.
Inputs may be any that keep to these rules, and one draw needn't show every extreme that they name: `lengths`: of the two slots on each index of shard, one, drawn from the seed, is full with 1024 valid tokens; the other has a drawn length, and some slot has exactly 256. Index c of ctx holds causal blocks block_pairs[c] and 31 - block_pairs[c] of every slot; each lower block is held once.
All inputs are finite; a program needn't handle non-finite values.
Results may differ from the reference program's by a relative error of at most 0.019.
Values may be sent and summed in bfloat16 or wider, within the bound.
A program may use at most 192 MiB of HBM per device.

```python
import jax
import jax.numpy as jnp
from jax import lax

D = 1024
HEADS = 16
HEAD_DIM = 64
FF = 4096
SEQ_LEN = 1024
SLOTS = 16
BLOCKS = 32
BLK = 32
TOK_SLOT = 64
N_CTX = 16


def draw_lengths(key, part):
    key = jax.random.fold_in(key, 7)
    key_short, key_pick, key_side = jax.random.split(key, 3)
    groups = SLOTS // 2
    shorter = jax.random.randint(key_short, (groups,), SEQ_LEN // 4, SEQ_LEN + 1)
    picked = jax.random.randint(key_pick, (), 0, groups)
    shorter = jnp.where(jnp.arange(groups) == picked, SEQ_LEN // 4, shorter)
    full_side = jax.random.randint(key_side, (groups,), 0, 2)
    first_slot = jnp.where(full_side == 0, SEQ_LEN, shorter)
    second_slot = jnp.where(full_side == 0, shorter, SEQ_LEN)
    return jnp.stack([first_slot, second_slot], axis=1).reshape(SLOTS).astype(jnp.int32)


def levels(own_key, dims, cuts, low, largest):
    loudness, own = 1.0, jax.random.fold_in(own_key, 6)
    for dim, shards_of in cuts:
        steps = jnp.exp(jax.random.uniform(jax.random.fold_in(own, dim), (shards_of,), jnp.float32, low / len(cuts), largest / len(cuts)))
        loudness = loudness * jnp.repeat(steps, dims[dim] // shards_of).reshape([-1 if axis == dim else 1 for axis in range(len(dims))])
    return loudness


def normal_values(stream_key, extent, width, bound, shards=(), dtype=jnp.bfloat16):
    entries = width * jax.random.normal(stream_key, extent, jnp.float32)
    if shards:
        entries = entries * levels(stream_key, extent, shards, -0.22, 0.18)
    return jnp.clip(entries, -bound, bound).astype(dtype)


def setup_inputs(seed: int = 0) -> dict:
    arg_keys = jax.random.split(jax.random.key(seed), 18)
    tokens = normal_values(arg_keys[0], (N_CTX, SLOTS, TOK_SLOT, D), 1.0, 6.0, ((0, 16), (1, 8)))
    lengths = draw_lengths(jax.random.fold_in(arg_keys[17], 71), 0)
    block_pairs = jax.random.permutation(arg_keys[2], N_CTX).astype(jnp.int32)
    ln1_gain = jnp.clip(1.0 + 0.1 * jax.random.normal(arg_keys[3], (D,), jnp.float32), 0.5, 1.5).astype(jnp.bfloat16)
    ln1_bias = normal_values(arg_keys[4], (D,), 0.2, 1.1953125, ((0, 8),))
    w_qkv = normal_values(arg_keys[5], (D, 3 * D), D ** -0.5, 0.1875, ((0, 8),))
    query_bias = normal_values(arg_keys[6], (D,), 0.3, 1.796875, ((0, 8),))
    value_bias = normal_values(arg_keys[7], (D,), 0.1, 0.59765625, ((0, 8),))
    w_out = normal_values(arg_keys[8], (D, D), (D // 16) ** -0.5, 0.75, ((0, 8),))
    out_bias = normal_values(arg_keys[9], (D,), 0.1, 0.59765625, ((0, 8),))
    ln2_gain = jnp.clip(1.0 + 0.1 * jax.random.normal(arg_keys[10], (D,), jnp.float32), 0.5, 1.5).astype(jnp.bfloat16)
    ln2_bias = normal_values(arg_keys[11], (D,), 0.2, 1.1953125, ((0, 8),))
    w_fc1 = normal_values(arg_keys[12], (D, FF), D ** -0.5, 0.1875, ((0, 8),))
    fc1_bias = normal_values(arg_keys[13], (FF,), 0.3, 1.796875, ((0, 8),))
    w_fc2 = normal_values(arg_keys[14], (FF, D), FF ** -0.5, 0.09375, ((0, 8),))
    fc2_bias = normal_values(arg_keys[15], (D,), 0.1, 0.59765625, ((0, 8),))
    out_cotangent = normal_values(arg_keys[16], (N_CTX, SLOTS, TOK_SLOT, D), 1.0, 6.0, ((0, 16), (1, 8)))
    return {"tokens": tokens, "lengths": lengths, "block_pairs": block_pairs, "ln1_gain": ln1_gain, "ln1_bias": ln1_bias, "w_qkv": w_qkv, "query_bias": query_bias, "value_bias": value_bias, "w_out": w_out, "out_bias": out_bias, "ln2_gain": ln2_gain, "ln2_bias": ln2_bias, "w_fc1": w_fc1, "fc1_bias": fc1_bias, "w_fc2": w_fc2, "fc2_bias": fc2_bias, "out_cotangent": out_cotangent}


@jax.custom_vjp
def low(v):
    return lax.optimization_barrier(v.astype(jnp.bfloat16)).astype(jnp.float32)

@jax.custom_vjp
def low_back(v):
    return v

def low_keep(v):
    return (low(v), None)

def low_pass(kept, grad):
    return (grad,)

def back_keep(v):
    return (v, None)

def back_low(kept, grad):
    return (low(grad),)
low.defvjp(low_keep, low_pass)
low_back.defvjp(back_keep, back_low)
eps_norm = 1e-05
negative = -1e+30

def exact_gelu(inputs):
    return jax.nn.gelu(inputs, approximate=False)

def layer_norm(inputs, gain, shift):
    centre = inputs - lax.optimization_barrier(jnp.mean(inputs, axis=-1, keepdims=True))
    spread = lax.optimization_barrier(jnp.mean(centre * centre, axis=-1, keepdims=True))
    return centre * lax.rsqrt(spread + eps_norm) * gain + shift

def matmul(left, right):
    return jnp.dot(left, right, precision=lax.Precision.HIGHEST, preferred_element_type=jnp.float32)

def slot_forward(weights, inputs, length, position):
    gain_one, bias_one, qkv_weight, bias_query, bias_value, out_weight, bias_out, gain_two, bias_two, up_weight, bias_up, down_weight, bias_down = weights
    attn_in = low(layer_norm(inputs, gain_one, bias_one))
    qkv_dot = low_back(matmul(attn_in, qkv_weight))
    query_low = low(qkv_dot[:, :D] + bias_query).reshape(SEQ_LEN, HEADS, HEAD_DIM)
    key_low = low(qkv_dot[:, D:2 * D]).reshape(SEQ_LEN, HEADS, HEAD_DIM)
    value_low = low(qkv_dot[:, 2 * D:] + bias_value).reshape(SEQ_LEN, HEADS, HEAD_DIM)
    key_valid = position < length
    block_size = min(512, SEQ_LEN)

    def attend(item_pair):
        query_block, place_rows = item_pair
        raw_scores = jnp.einsum('qhd,khd->hqk', query_block, key_low, precision=lax.Precision.HIGHEST)
        scores = low_back(raw_scores * HEAD_DIM ** (-0.5))
        allowed = key_valid[None, :] & (position[None, :] <= place_rows[:, None])
        scores = jnp.where(allowed[None], scores, negative)
        row_max = lax.optimization_barrier(jnp.max(scores, axis=-1, keepdims=True))
        powers = jnp.exp(scores - row_max)
        probs = powers / lax.optimization_barrier(jnp.sum(powers, axis=-1, keepdims=True))
        mixed_block = jnp.einsum('hqk,khd->qhd', low(probs), value_low, precision=lax.Precision.HIGHEST)
        return mixed_block.reshape(block_size, D)
    mixed = lax.map(jax.checkpoint(attend), (query_low.reshape(SEQ_LEN // block_size, block_size, HEADS, HEAD_DIM), position.reshape(SEQ_LEN // block_size, block_size)))
    mixed = low(low_back(mixed.reshape(SEQ_LEN, D)))
    hidden = inputs + (low_back(matmul(mixed, out_weight)) + bias_out)
    mlp_in = low(layer_norm(hidden, gain_two, bias_two))
    pre_act = low_back(matmul(mlp_in, up_weight)) + bias_up
    activated = low(exact_gelu(pre_act))
    mlp_out = low_back(matmul(activated, down_weight)) + bias_down
    row_valid = (position < length).astype(jnp.float32)[:, None]
    return row_valid * (hidden + mlp_out)

def reference(tokens, lengths, block_pairs, ln1_gain, ln1_bias, w_qkv, query_bias, value_bias, w_out, out_bias, ln2_gain, ln2_bias, w_fc1, fc1_bias, w_fc2, fc2_bias, out_cotangent):
    weights = tuple((param.astype(jnp.float32) for param in (ln1_gain, ln1_bias, w_qkv, query_bias, value_bias, w_out, out_bias, ln2_gain, ln2_bias, w_fc1, fc1_bias, w_fc2, fc2_bias)))
    row_index = jnp.arange(TOK_SLOT)
    half_index = row_index // BLK
    within = row_index % BLK
    blocks = jnp.where(half_index[None, :] == 0, block_pairs[:, None], BLOCKS - 1 - block_pairs[:, None])
    position = (blocks * BLK + within[None, :]).reshape(SEQ_LEN).astype(jnp.int32)
    slot_inputs = jnp.swapaxes(tokens.astype(jnp.float32), 0, 1).reshape(SLOTS, SEQ_LEN, D)
    slot_cot = jnp.swapaxes(out_cotangent.astype(jnp.float32), 0, 1).reshape(SLOTS, SEQ_LEN, D)

    def forward(params, inputs):

        def slot_step(carry_in, item_pair):
            values, length = item_pair
            return (carry_in, slot_forward(params, values, length, position))
        return lax.scan(slot_step, jnp.zeros((), jnp.float32), (inputs, lengths))[1]
    outputs, pull_back = jax.vjp(forward, weights, slot_inputs)
    grads, input_grads = pull_back(slot_cot)

    def unslot(values):
        return jnp.swapaxes(values.reshape(SLOTS, N_CTX, TOK_SLOT, D), 0, 1).astype(jnp.bfloat16)
    return (unslot(outputs), unslot(input_grads), grads[0], grads[1], grads[2], grads[3], grads[4], grads[5], grads[6], grads[7], grads[8], grads[9], grads[10], grads[11], grads[12])
```

```python
import jax
import jax.numpy as jnp
from jax import lax
from jax.experimental import pallas as pl
from jax.experimental.pallas import tpu as pltpu
from jax.sharding import PartitionSpec as P

HEADS = 16
HEAD_DIM = 64
MESH = pl.DeviceIdType.MESH
ANY = pl.ANY
VMEM = pltpu.VMEM
F32 = jnp.float32
BF16 = jnp.bfloat16

eps_norm = 1e-05
negative = -1e30


def place():
    c, s = lax.axis_index("ctx"), lax.axis_index("shard")
    return c, s, lax.rem(c, 2), s // 2, lax.rem(s, 2)


def sibling(c):
    return c + 1 - 2 * lax.rem(c, 2)


def send(src, dst, sems, idx, device):
    copy = pltpu.make_async_remote_copy(
        src_ref=src,
        dst_ref=dst,
        send_sem=sems[0].at[idx],
        recv_sem=sems[1].at[idx],
        device_id=device,
        device_id_type=MESH,
    )
    copy.start()
    return copy


def arrived(dst, sems, idx, c, s):
    pltpu.make_async_remote_copy(
        src_ref=dst,
        dst_ref=dst,
        send_sem=sems[0].at[idx],
        recv_sem=sems[1].at[idx],
        device_id=(c, s),
        device_id_type=MESH,
    ).wait_recv()


def greet(devices):
    barrier = pltpu.get_barrier_semaphore()
    for device in devices:
        pl.semaphore_signal(barrier, inc=1, device_id=device, device_id_type=MESH)
    pl.semaphore_wait(barrier, len(devices))


def sem_pair(count):
    return [pltpu.SemaphoreType.DMA((count,)), pltpu.SemaphoreType.DMA((count,))]


def comm_call(kernel, name, cid, outs, sems, ins, spaces=None, out_spaces=None, scratch=()):
    scratches = list(scratch)
    for count in sems:
        scratches += sem_pair(count)
    return pl.pallas_call(
        kernel,
        name=name,
        out_shape=[jax.ShapeDtypeStruct(shape, dtype) for shape, dtype in outs],
        in_specs=[pl.BlockSpec(memory_space=space) for space in (spaces or [ANY] * len(ins))],
        out_specs=[
            pl.BlockSpec(memory_space=space) for space in (out_spaces or [ANY] * len(outs))
        ],
        scratch_shapes=scratches + [pltpu.SemaphoreType.DMA((8,))],
        compiler_params=pltpu.CompilerParams(
            collective_id=cid, has_side_effects=True, vmem_limit_bytes=56 << 20
        ),
    )(*ins)


def half_rows(core, rows):
    return pl.ds(pl.multiple_of(core * rows, rows), rows)


def gather_first(tok, wq, small, tok_all, wq_all, small_all, a0, a1, b0, b1, d0, d1, e0, e1, local):
    c, s, core, x, yl = place()
    sib = (sibling(c), s)
    greet([(c, lax.rem(s + k, 8)) for k in range(1, 8)] + [sib])
    rows = half_rows(core, 64)
    out = []
    for k in range(1, 8):
        peer = lax.rem(s + k, 8)
        out.append(send(small, small_all.at[s], (a0, a1), k - 1, (c, peer)))
    for k in range(1, 8):
        peer = lax.rem(s + k, 8)
        out.append(
            send(wq.at[peer // 2, rows], wq_all.at[s, rows], (b0, b1), k - 1, (c, peer))
        )
    for k in range(1, 4):
        peer = lax.rem(x + k, 4)
        out.append(send(tok, tok_all.at[x], (d0, d1), k - 1, (c, 2 * peer + yl)))
    own = [
        pltpu.make_async_copy(tok, tok_all.at[x], local.at[0]),
        pltpu.make_async_copy(wq.at[x], wq_all.at[s], local.at[1]),
        pltpu.make_async_copy(small, small_all.at[s], local.at[2]),
    ]
    for copy in own:
        copy.start()
    for k in range(1, 8):
        origin = lax.rem(s - k + 8, 8)
        block = wq_all.at[origin, rows]
        arrived(block, (b0, b1), k - 1, c, s)
        out.append(send(block, block, (e0, e1), k - 1, sib))
    other = half_rows(1 - core, 64)
    for k in range(1, 8):
        origin = lax.rem(s - k + 8, 8)
        arrived(wq_all.at[origin, other], (e0, e1), k - 1, c, s)
        arrived(small_all.at[origin], (a0, a1), k - 1, c, s)
    for k in range(1, 4):
        arrived(tok_all.at[lax.rem(x - k + 4, 4)], (d0, d1), k - 1, c, s)
    for copy in out:
        copy.wait_send()
    for copy in own:
        copy.wait()


def gather_rest(
    qkv, wo, wf1, wf2, cot,
    parts, wo_all, wf1_all, wf2_all, cot_all,
    a0, a1, b0, b1, d0, d1, e0, e1, f0, f1, g0, g1, h0, h1, i0, i1, local,
):
    c, s, core, x, yl = place()
    sib = (sibling(c), s)
    mate = (c, s + 1 - 2 * yl)
    greet(
        [(lax.rem(c + k, 16), s) for k in range(1, 16)]
        + [(c, lax.rem(s + k, 8)) for k in range(1, 8)]
    )
    out = []
    for k in range(1, 16):
        peer = lax.rem(c + k, 16)
        cols = pl.ds(pl.multiple_of(lax.rem(peer, 2) * 384, 128), 384)
        out.append(send(qkv.at[peer // 2, :, cols], parts.at[c], (a0, a1), k - 1, (peer, s)))
    rows = half_rows(core, 64)
    rows2 = half_rows(core, 256)
    for k in range(1, 8):
        peer = lax.rem(s + k, 8)
        out.append(send(wo.at[rows], wo_all.at[s, rows], (b0, b1), k - 1, (c, peer)))
        cols = pl.ds(pl.multiple_of(peer // 2 * 1024, 128), 1024)
        out.append(send(wf1.at[rows, cols], wf1_all.at[s, rows], (d0, d1), k - 1, (c, peer)))
    out.append(send(wf2.at[rows2], wf2_all.at[yl, rows2], (e0, e1), 0, mate))
    for k in range(1, 4):
        peer = lax.rem(x + k, 4)
        out.append(send(cot, cot_all.at[x], (f0, f1), k - 1, (c, 2 * peer + yl)))
    mine = pl.ds(pl.multiple_of(core * 384, 128), 384)
    quarter = pl.ds(pl.multiple_of(x * 1024, 128), 1024)
    own = [
        pltpu.make_async_copy(qkv.at[c // 2, :, mine], parts.at[c], local.at[0]),
        pltpu.make_async_copy(wo, wo_all.at[s], local.at[1]),
        pltpu.make_async_copy(wf1.at[:, quarter], wf1_all.at[s], local.at[2]),
        pltpu.make_async_copy(wf2, wf2_all.at[yl], local.at[3]),
        pltpu.make_async_copy(cot, cot_all.at[x], local.at[4]),
    ]
    for copy in own:
        copy.start()
    for k in range(1, 8):
        origin = lax.rem(s - k + 8, 8)
        for whole, near, far in ((wo_all, (b0, b1), (g0, g1)), (wf1_all, (d0, d1), (h0, h1))):
            block = whole.at[origin, rows]
            arrived(block, near, k - 1, c, s)
            out.append(send(block, block, far, k - 1, sib))
    block = wf2_all.at[1 - yl, rows2]
    arrived(block, (e0, e1), 0, c, s)
    out.append(send(block, block, (i0, i1), 0, sib))
    other = half_rows(1 - core, 64)
    for k in range(1, 8):
        origin = lax.rem(s - k + 8, 8)
        arrived(wo_all.at[origin, other], (g0, g1), k - 1, c, s)
        arrived(wf1_all.at[origin, other], (h0, h1), k - 1, c, s)
    arrived(wf2_all.at[1 - yl, half_rows(1 - core, 256)], (i0, i1), 0, c, s)
    for k in range(1, 16):
        arrived(parts.at[lax.rem(c - k + 16, 16)], (a0, a1), k - 1, c, s)
    for k in range(1, 4):
        arrived(cot_all.at[lax.rem(x - k + 4, 4)], (f0, f1), k - 1, c, s)
    for copy in out:
        copy.wait_send()
    for copy in own:
        copy.wait()


def head_columns(x, core):
    return pl.ds(pl.multiple_of(x * 256 + core * 128, 128), 128)


def mix_back(mixed, rows_out, a0, a1, local):
    c, s, core, x, yl = place()
    z, yh = c // 4, lax.rem(c // 2, 2)
    barrier = pltpu.get_barrier_semaphore()
    at_home = z == x
    for k in range(16):
        xo = k // 4
        co = x * 4 + k % 4
        so = 2 * xo + yl

        @pl.when(jnp.logical_not((co == c) & (so == s)))
        def _():
            pl.semaphore_signal(barrier, inc=1, device_id=(co, so), device_id_type=MESH)

    pl.semaphore_wait(barrier, 16 - at_home.astype(jnp.int32))
    cols = head_columns(x, core)
    target = 2 * z + yl

    def copy_to(k):
        peer = lax.rem(c + k, 16)
        return pltpu.make_async_remote_copy(
            src_ref=mixed.at[peer],
            dst_ref=rows_out.at[yh, :, cols],
            send_sem=a0.at[k],
            recv_sem=a1.at[x * 4 + yh * 2 + core],
            device_id=(peer, target),
            device_id_type=MESH,
        )

    for k in range(1, 16):
        copy_to(k).start()

    @pl.when(at_home)
    def _():
        copy = pltpu.make_async_copy(mixed.at[c], rows_out.at[yh, :, cols], local.at[0])
        copy.start()
        copy.wait()

    @pl.when(jnp.logical_not(at_home))
    def _():
        copy_to(0).start()

    for k in range(16):
        xo, yo, ko = k // 4, (k // 2) % 2, k % 2
        mine = at_home & (xo == x) & (yo == yh) & (ko == core)

        @pl.when(jnp.logical_not(mine))
        def _():
            arrived(rows_out.at[yo, :, pl.ds(xo * 256 + ko * 128, 128)], (a0, a1), k, c, s)

    for k in range(1, 16):
        copy_to(k).wait_send()

    @pl.when(jnp.logical_not(at_home))
    def _():
        copy_to(0).wait_send()


def mix_forth(rows_in, parts, a0, a1, local):
    c, s, core, x, yl = place()
    z, yh = c // 4, lax.rem(c // 2, 2)
    barrier = pltpu.get_barrier_semaphore()
    at_home = z == x
    source = 2 * z + yl
    for k in range(1, 16):
        pl.semaphore_signal(
            barrier, inc=1, device_id=(lax.rem(c + k, 16), source), device_id_type=MESH
        )

    @pl.when(jnp.logical_not(at_home))
    def _():
        pl.semaphore_signal(barrier, inc=1, device_id=(c, source), device_id_type=MESH)

    pl.semaphore_wait(barrier, 16 - at_home.astype(jnp.int32))

    def copy_to(k):
        xo, yo, ko = k // 4, (k // 2) % 2, k % 2
        return pltpu.make_async_remote_copy(
            src_ref=rows_in.at[yo, :, pl.ds(xo * 256 + ko * 128, 128)],
            dst_ref=parts.at[c],
            send_sem=a0.at[k],
            recv_sem=a1.at[c],
            device_id=(x * 4 + yo * 2 + ko, 2 * xo + yl),
            device_id_type=MESH,
        )

    for k in range(16):
        xo, yo, ko = k // 4, (k // 2) % 2, k % 2
        mine = at_home & (xo == x) & (yo == yh) & (ko == core)

        @pl.when(jnp.logical_not(mine))
        def _():
            copy_to(k).start()

    @pl.when(at_home)
    def _():
        copy = pltpu.make_async_copy(
            rows_in.at[yh, :, head_columns(x, core)], parts.at[c], local.at[0]
        )
        copy.start()
        copy.wait()

    for k in range(1, 16):
        origin = lax.rem(c + k, 16)
        arrived(parts.at[origin], (a0, a1), origin, c, s)

    @pl.when(jnp.logical_not(at_home))
    def _():
        arrived(parts.at[c], (a0, a1), c, c, s)

    for k in range(16):
        xo, yo, ko = k // 4, (k // 2) % 2, k % 2
        mine = at_home & (xo == x) & (yo == yh) & (ko == core)

        @pl.when(jnp.logical_not(mine))
        def _():
            copy_to(k).wait_send()


def gather_x(mine, whole, a0, a1, local):
    c, s, core, x, yl = place()
    greet([(c, 2 * lax.rem(x + k, 4) + yl) for k in range(1, 4)])
    out = []
    for k in range(1, 4):
        peer = lax.rem(x + k, 4)
        out.append(send(mine, whole.at[x], (a0, a1), k - 1, (c, 2 * peer + yl)))
    own = pltpu.make_async_copy(mine, whole.at[x], local.at[0])
    own.start()
    for k in range(1, 4):
        arrived(whole.at[lax.rem(x - k + 4, 4)], (a0, a1), k - 1, c, s)
    for copy in out:
        copy.wait_send()
    own.wait()


def scatter_x(part_one, part_two, got_one, got_two, a0, a1, b0, b1, local):
    c, s, core, x, yl = place()
    greet([(c, 2 * lax.rem(x + k, 4) + yl) for k in range(1, 4)])
    out = []
    for part, got, sems in ((part_one, got_one, (a0, a1)), (part_two, got_two, (b0, b1))):
        for k in range(1, 4):
            peer = lax.rem(x + k, 4)
            out.append(send(part.at[peer], got.at[k - 1], sems, k - 1, (c, 2 * peer + yl)))
    for got, sems in ((got_one, (a0, a1)), (got_two, (b0, b1))):
        for k in range(1, 4):
            arrived(got.at[k - 1], sems, k - 1, c, s)
    for copy in out:
        copy.wait_send()


def heads_back(parts, whole, a0, a1, local):
    c, s, core, x, yl = place()
    greet([(lax.rem(c + k, 16), s) for k in range(1, 16)])
    cols = pl.ds(pl.multiple_of(core * 384, 128), 384)
    out = []
    for k in range(1, 16):
        peer = lax.rem(c + k, 16)
        out.append(send(parts.at[peer], whole.at[c // 2, :, cols], (a0, a1), k - 1, (peer, s)))
    own = pltpu.make_async_copy(parts.at[c], whole.at[c // 2, :, cols], local.at[0])
    own.start()
    for k in range(1, 16):
        origin = lax.rem(c - k + 16, 16)
        place_of = pl.ds(pl.multiple_of(lax.rem(origin, 2) * 384, 128), 384)
        arrived(whole.at[origin // 2, :, place_of], (a0, a1), k - 1, c, s)
    for copy in out:
        copy.wait_send()
    own.wait()


def sum_ctx(
    part, g_qkv, g_out, g_one, g_two, vec,
    got_part, s_qkv, s_out, s_one, s_two, s_vec,
    n_qkv, n_out, n_one, n_two, t_qkv, t_out, t_one, t_two, t_vec,
    p0, p1, a0, a1, b0, b1, v0, v1, local,
):
    c, s, core, x, yl = place()
    sib = (sibling(c), s)
    chip = c // 2
    greet(
        [(lax.rem(c + k, 16), s) for k in range(1, 16)]
        + [(c, 2 * lax.rem(x + k, 4) + yl) for k in range(1, 4)]
    )
    out = []
    for k in range(1, 4):
        peer = lax.rem(x + k, 4)
        out.append(send(part.at[peer], got_part.at[k - 1], (p0, p1), k - 1, (c, 2 * peer + yl)))
    for k in range(1, 16):
        peer = lax.rem(c + k, 16)
        out.append(send(vec.at[peer], t_vec.at[k - 1], (v0, v1), k - 1, (peer, s)))
    grads = (
        (g_two, n_two, t_two, s_two),
        (g_one, n_one, t_one, s_one),
        (g_out, n_out, t_out, s_out),
        (g_qkv, n_qkv, t_qkv, s_qkv),
    )
    for i, (g, near, far, total) in enumerate(grads):
        out.append(send(g.at[:, 1 - core], near, (a0, a1), i, sib))
    for i, (g, near, far, total) in enumerate(grads):
        arrived(near, (a0, a1), i, c, s)

        def add(j, _):
            near[j] = (near[j].astype(F32) + g[j, core].astype(F32)).astype(BF16)
            return 0

        lax.fori_loop(0, 8, add, 0)
        for k in range(1, 8):
            peer = lax.rem(chip + k, 8)
            out.append(
                send(near.at[peer], far.at[k - 1], (b0, b1), 7 * i + k - 1, (2 * peer + core, s))
            )
    for k in range(1, 16):
        arrived(t_vec.at[k - 1], (v0, v1), k - 1, c, s)
    s_vec[...] = vec[c] + jnp.sum(t_vec[...], axis=0)
    for i, (g, near, far, total) in enumerate(grads):
        for k in range(1, 8):
            arrived(far.at[k - 1], (b0, b1), 7 * i + k - 1, c, s)

        def add_rows(j, _):
            rows = pl.ds(pl.multiple_of(j * 16, 16), 16)
            acc = near[chip, rows].astype(F32)
            for k in range(7):
                acc = acc + far[k, rows].astype(F32)
            total[rows] = acc
            return 0

        lax.fori_loop(0, 4, add_rows, 0)
    for k in range(1, 4):
        arrived(got_part.at[k - 1], (p0, p1), k - 1, c, s)
    for copy in out:
        copy.wait_send()


def to_owners(
    s_qkv, s_out, s_one, s_two, s_vec,
    r_qkv, r_out, r_one, r_two, r_vec,
    a0, a1, b0, b1, d0, d1, e0, e1, f0, f1, local,
):
    c, s, core, x, yl = place()
    barrier = pltpu.get_barrier_semaphore()
    low = lax.rem(c, 4)
    to_c, to_x = 4 * x + c // 4, low
    from_c, from_x = 4 * low + x, c // 4
    stays = (to_c == c) & (to_x == x)
    for k in range(1, 8):
        pl.semaphore_signal(
            barrier, inc=1, device_id=(c, lax.rem(s + k, 8)), device_id_type=MESH
        )
    for y in range(2):

        @pl.when(jnp.logical_not(stays & (yl == y)))
        def _():
            pl.semaphore_signal(
                barrier, inc=1, device_id=(from_c, 2 * from_x + y), device_id_type=MESH
            )

    pl.semaphore_wait(barrier, 9 - stays.astype(jnp.int32))
    out = []

    def two_to(y):
        return pltpu.make_async_remote_copy(
            src_ref=s_two.at[y],
            dst_ref=r_two.at[yl],
            send_sem=e0.at[y],
            recv_sem=e1.at[yl],
            device_id=(to_c, 2 * to_x + y),
            device_id_type=MESH,
        )

    for y in range(2):

        @pl.when(jnp.logical_not(stays & (yl == y)))
        def _():
            two_to(y).start()

    @pl.when(stays)
    def _():
        copy = pltpu.make_async_copy(s_two.at[yl], r_two.at[yl], local.at[0])
        copy.start()
        copy.wait()

    triples = ((s_qkv, r_qkv, (a0, a1)), (s_out, r_out, (b0, b1)), (s_one, r_one, (d0, d1)))
    for k in range(1, 8):
        peer = lax.rem(s + k, 8)
        rows = pl.ds(pl.multiple_of(peer * 8, 8), 8)
        for src, dst, sems in triples:
            out.append(send(src.at[rows], dst.at[s], sems, k - 1, (c, peer)))
        out.append(send(s_vec, r_vec.at[s], (f0, f1), k - 1, (c, peer)))
    own_rows = pl.ds(pl.multiple_of(s * 8, 8), 8)
    own = [
        pltpu.make_async_copy(src.at[own_rows], dst.at[s], local.at[1 + i])
        for i, (src, dst, _) in enumerate(triples)
    ] + [pltpu.make_async_copy(s_vec, r_vec.at[s], local.at[4])]
    for copy in own:
        copy.start()
    for k in range(1, 8):
        origin = lax.rem(s - k + 8, 8)
        for _, dst, sems in triples:
            arrived(dst.at[origin], sems, k - 1, c, s)
        arrived(r_vec.at[origin], (f0, f1), k - 1, c, s)
    for y in range(2):

        @pl.when(jnp.logical_not(stays & (yl == y)))
        def _():
            arrived(r_two.at[y], (e0, e1), y, c, s)

    for copy in out:
        copy.wait_send()
    for y in range(2):

        @pl.when(jnp.logical_not(stays & (yl == y)))
        def _():
            two_to(y).wait_send()

    for copy in own:
        copy.wait()


def exact_gelu(inputs):
    return jax.nn.gelu(inputs, approximate=False)


def norm_parts(inputs):
    centre = inputs - jnp.mean(inputs, axis=-1, keepdims=True)
    spread = jnp.mean(centre * centre, axis=-1, keepdims=True)
    inverse = lax.rsqrt(spread + eps_norm)
    return (centre * inverse, inverse)


def norm_back(grad_normed, normed, inverse, gain):
    scaled = grad_normed * gain
    centred = scaled - jnp.mean(scaled, axis=-1, keepdims=True)
    return inverse * (centred - normed * jnp.mean(scaled * normed, axis=-1, keepdims=True))


def dot(left, right):
    return jnp.dot(left, right, preferred_element_type=F32)


def dot_rows(left, right):
    return jnp.einsum("rd,re->de", left, right, preferred_element_type=F32)


def dot_back(left, right):
    return jnp.einsum("re,de->rd", left, right, preferred_element_type=F32)


def shards(
    tokens,
    lengths,
    block_pairs,
    ln1_gain,
    ln1_bias,
    w_qkv,
    query_bias,
    value_bias,
    w_out,
    out_bias,
    ln2_gain,
    ln2_bias,
    w_fc1,
    fc1_bias,
    w_fc2,
    fc2_bias,
    out_cotangent,
):
    c, s = lax.axis_index("ctx"), lax.axis_index("shard")
    core, x, yl = c % 2, s // 2, s % 2
    scale = HEAD_DIM ** (-0.5)
    tok = tokens.reshape(128, 1024)
    cot = out_cotangent.reshape(128, 1024)

    row = jnp.arange(64)
    blocks = jnp.where(row[None, :] < 32, block_pairs[:, None], 31 - block_pairs[:, None])
    places = blocks * 32 + (row % 32)[None, :]
    my_places = lax.dynamic_index_in_dim(places, c, 0, keepdims=False)
    places = places.reshape(1024)

    vectors = [
        p.astype(F32).reshape(-1, 128)
        for p in (
            ln1_gain, ln1_bias, query_bias, value_bias, out_bias, ln2_gain, ln2_bias, fc2_bias, fc1_bias,
        )
    ]
    last = jnp.zeros((4, 128), F32).at[0, :2].set(lengths.astype(F32))
    small = jnp.concatenate(vectors + [last], axis=0)
    wq = w_qkv.reshape(128, 3, 4, 2, 128).transpose(2, 0, 3, 1, 4).reshape(4, 128, 768)
    tok_all, wq_all, small_all = comm_call(
        gather_first,
        "gather_first",
        0,
        [((4, 128, 1024), BF16), ((8, 128, 768), BF16), ((8, 16, 128), F32)],
        [7, 7, 3, 7],
        (tok, wq, small),
    )
    gain_one, bias_one, bias_q, bias_v, bias_out, gain_two, bias_two, bias_down = [
        small_all[:, i].reshape(1024) for i in range(8)
    ]
    bias_up = lax.dynamic_slice_in_dim(small_all[:, 8:12].reshape(4096), x * 1024, 1024)
    len_all = small_all[:, 12, :2].astype(jnp.int32)
    len_x = len_all.reshape(4, 2, 2)
    len_x = jnp.where(yl == 0, len_x[:, 0], len_x[:, 1]).reshape(8)
    my_len = lax.dynamic_index_in_dim(len_x, c // 2, 0, keepdims=False)
    w_q = wq_all.reshape(1024, 768)

    rows_all = tok_all.reshape(512, 1024).astype(F32)
    normed_all, _ = norm_parts(rows_all)
    attn_in = (normed_all * gain_one + bias_one).astype(BF16)
    bq = lax.dynamic_slice_in_dim(bias_q, x * 256, 256).reshape(2, 1, 128)
    bv = lax.dynamic_slice_in_dim(bias_v, x * 256, 256).reshape(2, 1, 128)
    bias768 = jnp.concatenate([bq, jnp.zeros_like(bq), bv], axis=1).reshape(768)
    qkv = (dot(attn_in, w_q) + bias768).astype(BF16).reshape(8, 64, 768)

    parts, wo_all, wf1_all, wf2_all, cot_all = comm_call(
        gather_rest,
        "gather_rest",
        1,
        [
            ((16, 64, 384), BF16),
            ((8, 128, 1024), BF16),
            ((8, 128, 1024), BF16),
            ((2, 512, 1024), BF16),
            ((4, 128, 1024), BF16),
        ],
        [15, 7, 7, 1, 3, 7, 7, 1],
        (qkv, w_out, w_fc1, w_fc2, cot),
    )
    w_o = wo_all.reshape(1024, 1024)
    w_up = wf1_all.reshape(1024, 1024)
    w_down = wf2_all.reshape(1024, 1024)

    parts = parts.reshape(1024, 3, 2, 64)
    q, k, v = parts[:, 0], parts[:, 1], parts[:, 2]
    allowed = (places[None, :] < my_len) & (places[None, :] <= places[:, None])

    def scores_of():
        raw = jnp.einsum("qhd,khd->hqk", q, k, preferred_element_type=F32) * scale
        return jnp.where(allowed[None], raw, negative)

    scores = scores_of()
    row_max = jnp.max(scores, axis=-1, keepdims=True)
    powers = jnp.exp(scores - row_max)
    total = jnp.sum(powers, axis=-1, keepdims=True)
    probs_first = (powers / total).astype(BF16)
    log_total = row_max + jnp.log(total)
    mixed = jnp.einsum("hqk,khd->qhd", probs_first, v, preferred_element_type=F32)
    mixed = mixed.reshape(16, 64, 128).astype(BF16)
    (mix_rows,) = comm_call(mix_back, "mix_back", 2, [((2, 64, 1024), BF16)], [16], (mixed,))
    mix_rows = mix_rows.reshape(128, 1024)

    residual = tok.astype(F32)
    hidden = residual + (dot(mix_rows, w_o) + bias_out)
    normed_two, inverse_two = norm_parts(hidden)
    mlp_in = (normed_two * gain_two + bias_two).astype(BF16)
    (mlp_all,) = comm_call(gather_x, "gather_x", 3, [((4, 128, 1024), BF16)], [3], (mlp_in,))
    mlp_all = mlp_all.reshape(512, 1024)

    pre_act = dot(mlp_all, w_up) + bias_up
    activated, gelu_pull = jax.vjp(exact_gelu, pre_act)
    act_low = activated.astype(BF16)
    mlp_part = dot(act_low, w_down)
    valid_all = (my_places[None, :] < len_x[:, None]).astype(F32).reshape(512, 1)
    g_all = cot_all.reshape(512, 1024).astype(F32) * valid_all
    g_low = g_all.astype(BF16)
    grad_act = dot_back(g_low, w_down)
    grad_pre = gelu_pull(grad_act)[0]
    grad_up_b = jnp.sum(grad_pre, axis=0)
    grad_pre_low = grad_pre.astype(BF16)
    gm_part = dot_back(grad_pre_low, w_up)
    g_two = dot_rows(act_low, g_low).astype(BF16)
    g_one = dot_rows(mlp_all, grad_pre_low).astype(BF16)
    gm_part = gm_part.reshape(4, 128, 1024)
    mlp_part = mlp_part.reshape(4, 128, 1024)
    got_gm, got_out = comm_call(
        scatter_x,
        "scatter_x",
        4,
        [((3, 128, 1024), BF16)] * 2,
        [3, 3],
        (gm_part.astype(BF16), mlp_part.astype(BF16)),
    )

    def own_block(blocks4):
        return lax.dynamic_index_in_dim(blocks4, x, 0, keepdims=False)

    grad_mlp_in = own_block(gm_part) + jnp.sum(got_gm.astype(F32), axis=0)
    mlp_out = own_block(mlp_part) + jnp.sum(got_out.astype(F32), axis=0) + bias_down
    row_valid = own_block(valid_all.reshape(4, 128, 1))
    layer_out = (row_valid * (hidden + mlp_out)).astype(BF16).reshape(tokens.shape)
    grad_out = cot.astype(F32) * row_valid
    grad_down_b = jnp.sum(grad_out, axis=0)
    grad_gain_two = jnp.sum(grad_mlp_in * normed_two, axis=0)
    grad_bias_two = jnp.sum(grad_mlp_in, axis=0)
    grad_hidden = grad_out + norm_back(grad_mlp_in, normed_two, inverse_two, gain_two)
    hidden_low = grad_hidden.astype(BF16)
    grad_out_b = jnp.sum(grad_hidden, axis=0)
    grad_mixed = dot_back(hidden_low, w_o).astype(BF16).reshape(2, 64, 1024)
    g_out = dot_rows(mix_rows, hidden_low).astype(BF16)
    (gm,) = comm_call(mix_forth, "mix_forth", 5, [((16, 64, 128), BF16)], [16], (grad_mixed,))

    gm = gm.reshape(1024, 2, 64)
    probs = jnp.exp(scores_of() - log_total)
    probs_low = probs.astype(BF16)
    grad_probs = jnp.einsum("qhd,khd->hqk", gm, v, preferred_element_type=F32)
    delta = jnp.sum(probs * grad_probs, axis=-1, keepdims=True)
    grad_scores = (probs * (grad_probs - delta)).astype(BF16)
    gq = jnp.einsum("hqk,khd->qhd", grad_scores, k, preferred_element_type=F32) * scale
    gk = jnp.einsum("hqk,qhd->khd", grad_scores, q, preferred_element_type=F32) * scale
    gv = jnp.einsum("hqk,qhd->khd", probs_low, gm, preferred_element_type=F32)
    gq, gk, gv = (g.reshape(1024, 128) for g in (gq, gk, gv))
    grad_bq, grad_bv = jnp.sum(gq, axis=0), jnp.sum(gv, axis=0)
    g_parts = jnp.concatenate([gq, gk, gv], axis=1).astype(BF16).reshape(16, 64, 384)
    (g_qkv,) = comm_call(heads_back, "heads_back", 6, [((8, 64, 768), BF16)], [15], (g_parts,))
    g_qkv = g_qkv.reshape(512, 768)
    ga_part = dot_back(g_qkv, w_q).reshape(4, 128, 1024)
    gw_qkv = dot_rows(attn_in, g_qkv).astype(BF16)

    zeros = jnp.zeros((1024,), F32)
    head_at = x * 256 + core * 128
    full = [
        grad_out_b,
        grad_gain_two,
        grad_bias_two,
        grad_down_b,
        lax.dynamic_update_slice(zeros, grad_bq, (head_at,)),
        lax.dynamic_update_slice(zeros, grad_bv, (head_at,)),
    ]
    up_full = lax.dynamic_update_slice(jnp.zeros((4096,), F32), grad_up_b, (x * 1024,))

    def chunks(vectors, tail):
        body = jnp.stack([v.reshape(16, 64) for v in vectors], axis=1).reshape(16, -1, 128)
        if tail is not None:
            body = jnp.concatenate([body, tail.reshape(16, 2, 128)], axis=1)
        return jnp.pad(body, ((0, 0), (0, 8 - body.shape[1]), (0, 0)))

    vec = chunks(full, up_full)
    sums = comm_call(
        sum_ctx,
        "sum_ctx",
        7,
        [
            ((3, 128, 1024), BF16),
            ((64, 768), F32),
            ((64, 1024), F32),
            ((64, 1024), F32),
            ((64, 1024), F32),
            ((8, 128), F32),
        ],
        [3, 4, 28, 15],
        (
            ga_part.astype(BF16),
            gw_qkv.reshape(8, 2, 64, 768),
            g_out.reshape(8, 2, 64, 1024),
            g_one.reshape(8, 2, 64, 1024),
            g_two.reshape(8, 2, 64, 1024),
            vec,
        ),
        spaces=[ANY, VMEM, VMEM, VMEM, VMEM, VMEM],
        out_spaces=[ANY, VMEM, VMEM, VMEM, VMEM, VMEM],
        scratch=[
            pltpu.VMEM((8, 64, 768), BF16),
            pltpu.VMEM((8, 64, 1024), BF16),
            pltpu.VMEM((8, 64, 1024), BF16),
            pltpu.VMEM((8, 64, 1024), BF16),
            pltpu.VMEM((7, 64, 768), BF16),
            pltpu.VMEM((7, 64, 1024), BF16),
            pltpu.VMEM((7, 64, 1024), BF16),
            pltpu.VMEM((7, 64, 1024), BF16),
            pltpu.VMEM((15, 8, 128), F32),
        ],
    )
    got_ga, s_qkv, s_out, s_one, s_two, s_vec = sums
    normed_one, inverse_one = norm_parts(residual)
    grad_attn_in = own_block(ga_part) + jnp.sum(got_ga.astype(F32), axis=0)
    input_grad = (
        (grad_hidden + norm_back(grad_attn_in, normed_one, inverse_one, gain_one))
        .astype(BF16)
        .reshape(tokens.shape)
    )
    vec_one = chunks([jnp.sum(grad_attn_in * normed_one, axis=0), jnp.sum(grad_attn_in, axis=0)], None)
    (s_vec_one,) = comm_call(
        sum_vec,
        "sum_vec",
        8,
        [((8, 128), F32)],
        [15],
        (vec_one,),
        spaces=[VMEM],
        out_spaces=[VMEM],
        scratch=[pltpu.VMEM((15, 8, 128), F32)],
    )
    s_vec = jnp.concatenate([s_vec, s_vec_one], axis=0)
    r_qkv, r_out, r_one, r_two, r_vec = comm_call(
        to_owners,
        "to_owners",
        9,
        [
            ((8, 8, 768), F32),
            ((8, 8, 1024), F32),
            ((8, 8, 1024), F32),
            ((2, 32, 1024), F32),
            ((8, 16, 128), F32),
        ],
        [7, 7, 7, 2, 7],
        (s_qkv, s_out, s_one, s_two.reshape(2, 32, 1024), s_vec),
    )
    by_x = jnp.sum(r_qkv.reshape(4, 2, 8, 2, 3, 128), axis=1)
    grad_w_qkv = by_x.transpose(1, 3, 0, 2, 4).reshape(8, 3072)
    grad_w_out = jnp.sum(r_out, axis=0)
    one_x = jnp.sum(r_one.reshape(4, 2, 8, 1024), axis=1)
    grad_w_fc1 = one_x.transpose(1, 0, 2).reshape(8, 4096)
    grad_w_fc2 = jnp.sum(r_two, axis=0)
    vec_sum = jnp.sum(r_vec, axis=0)
    small_sums = vec_sum[:3].reshape(6, 8, 8)
    small_sums = lax.dynamic_index_in_dim(small_sums, s, 1, keepdims=False)
    up_sum = lax.dynamic_index_in_dim(vec_sum[3:5].reshape(8, 32), s, 0, keepdims=False)
    one_sums = vec_sum[8:9].reshape(2, 8, 8)
    one_sums = lax.dynamic_index_in_dim(one_sums, s, 1, keepdims=False)
    return (
        layer_out,
        input_grad,
        one_sums[0],
        one_sums[1],
        grad_w_qkv,
        small_sums[4],
        small_sums[5],
        grad_w_out,
        small_sums[0],
        small_sums[1],
        small_sums[2],
        grad_w_fc1,
        up_sum,
        grad_w_fc2,
        small_sums[3],
    )


def sum_vec(vec, total, got, a0, a1, local):
    c, s, core, x, yl = place()
    greet([(lax.rem(c + k, 16), s) for k in range(1, 16)])
    out = []
    for k in range(1, 16):
        peer = lax.rem(c + k, 16)
        out.append(send(vec.at[peer], got.at[k - 1], (a0, a1), k - 1, (peer, s)))
    for k in range(1, 16):
        arrived(got.at[k - 1], (a0, a1), k - 1, c, s)
    total[...] = vec[c] + jnp.sum(got[...], axis=0)
    for copy in out:
        copy.wait_send()


def solution(mesh):
    one, both = P("shard"), P(("ctx", "shard"))
    rows, both_rows = P("shard", None), P(("ctx", "shard"), None)
    whole = P("ctx", "shard", None, None)
    return jax.shard_map(
        shards,
        mesh=mesh,
        in_specs=(
            whole, one, P(), one, one, rows, one, one, rows, one, one, one, rows, one, rows, one, whole,
        ),
        out_specs=(
            whole, whole, both, both, both_rows, both, both, both_rows, both, both, both,
            both_rows, both, both_rows, both,
        ),
        check_vma=False,
    )
```

```python
from types import SimpleNamespace

import jax
import jax.numpy as jnp
from jax import lax
from jax.experimental import pallas as pl
from jax.experimental.pallas import tpu as pltpu
from jax.sharding import PartitionSpec as P

HEADS = 16
HEAD_DIM = 64
MESH = pl.DeviceIdType.MESH
ANY = pl.ANY
VMEM = pltpu.VMEM
F32 = jnp.float32
BF16 = jnp.bfloat16

eps_norm = 1e-05
negative = -1e30


def place():
    c, s = lax.axis_index("ctx"), lax.axis_index("shard")
    return c, s, lax.rem(c, 2), s // 2, lax.rem(s, 2)


def sibling(c):
    return c + 1 - 2 * lax.rem(c, 2)


def send(src, dst, sems, idx, device):
    copy = pltpu.make_async_remote_copy(
        src_ref=src,
        dst_ref=dst,
        send_sem=sems[0].at[idx],
        recv_sem=sems[1].at[idx],
        device_id=device,
        device_id_type=MESH,
    )
    copy.start()
    return copy


def arrived(dst, sems, idx, c, s):
    pltpu.make_async_remote_copy(
        src_ref=dst,
        dst_ref=dst,
        send_sem=sems[0].at[idx],
        recv_sem=sems[1].at[idx],
        device_id=(c, s),
        device_id_type=MESH,
    ).wait_recv()


def greet(devices):
    barrier = pltpu.get_barrier_semaphore()
    for device in devices:
        pl.semaphore_signal(barrier, inc=1, device_id=device, device_id_type=MESH)
    pl.semaphore_wait(barrier, len(devices))


def sem_pair(count):
    return [pltpu.SemaphoreType.DMA((count,)), pltpu.SemaphoreType.DMA((count,))]


def comm_call(kernel, name, cid, outs, sems, ins, spaces=None, out_spaces=None, scratch=()):
    scratches = list(scratch)
    for count in sems:
        scratches += sem_pair(count)
    return pl.pallas_call(
        kernel,
        name=name,
        out_shape=[jax.ShapeDtypeStruct(shape, dtype) for shape, dtype in outs],
        in_specs=[pl.BlockSpec(memory_space=space) for space in (spaces or [ANY] * len(ins))],
        out_specs=[
            pl.BlockSpec(memory_space=space) for space in (out_spaces or [ANY] * len(outs))
        ],
        scratch_shapes=scratches + [pltpu.SemaphoreType.DMA((8,))],
        compiler_params=pltpu.CompilerParams(
            collective_id=cid, has_side_effects=True, vmem_limit_bytes=56 << 20
        ),
    )(*ins)


def half_rows(core, rows):
    return pl.ds(pl.multiple_of(core * rows, rows), rows)


def head_columns(x, core):
    return pl.ds(pl.multiple_of(x * 256 + core * 128, 128), 128)


def pick(value, unit):
    return pl.multiple_of(value * unit, unit)


def loop(count, body, first=0):
    def step(k, carry):
        body(k)
        return carry

    lax.fori_loop(first, count, step, 0)


def remote(src, dst, send_sem, recv_sem, device):
    return pltpu.make_async_remote_copy(
        src_ref=src,
        dst_ref=dst,
        send_sem=send_sem,
        recv_sem=recv_sem,
        device_id=device,
        device_id_type=MESH,
    )


def not_when(condition, body):
    pl.when(jnp.logical_not(condition))(body)


def norm_rows(rows):
    centre = rows - jnp.mean(rows, axis=-1, keepdims=True)
    inverse = lax.rsqrt(jnp.mean(centre * centre, axis=-1, keepdims=True) + eps_norm)
    return centre * inverse, inverse


def dot_nt(left, right):
    return lax.dot_general(left, right, (((1,), (1,)), ((), ())), preferred_element_type=F32)


VECTORS = (
    "ln1_gain", "ln1_bias", "query_bias", "value_bias", "out_bias", "ln2_gain", "ln2_bias", "fc2_bias",
)

FORWARD_IN = (
    ("lengths", pltpu.SMEM),
    ("block_pairs", pltpu.SMEM),
    ("tok", VMEM),
    *[(name, VMEM) for name in VECTORS],
    ("fc1_bias", VMEM),
    ("w_qkv", ANY),
    ("w_out", ANY),
    ("w_fc1", ANY),
    ("w_fc2", ANY),
    ("cot", ANY),
)

FORWARD_OUT = (
    ("attn_all", VMEM, (4, 128, 1024), BF16),
    ("wq_all", VMEM, (8, 128, 768), BF16),
    ("wo_all", VMEM, (8, 128, 1024), BF16),
    ("w1_all", ANY, (8, 128, 1024), BF16),
    ("w2_all", ANY, (2, 512, 1024), BF16),
    ("cot_all", ANY, (4, 128, 1024), BF16),
    ("parts", VMEM, (16, 64, 384), BF16),
    ("probs", VMEM, (2, 1024, 1024), BF16),
    ("mix_t", VMEM, (128, 1024), F32),
    ("mix_rows", VMEM, (2, 64, 1024), BF16),
    ("hidden", VMEM, (128, 1024), F32),
    ("mlp_in", VMEM, (128, 1024), BF16),
    ("small_all", VMEM, (16, 1024), F32),
    ("places", VMEM, (1024, 128), F32),
)

FORWARD_SCRATCH = (
    ("small", pltpu.VMEM((16, 128), F32)),
    ("tok_all", pltpu.VMEM((4, 128, 1024), BF16)),
    ("qkv", pltpu.VMEM((16, 64, 384), BF16)),
    ("mixed", pltpu.VMEM((16, 64, 128), BF16)),
    *[
        (name, pltpu.SemaphoreType.DMA((count,)))
        for name, count in (
            ("local", 16), ("sm_s", 8), ("sm_r", 8), ("wq_s", 24), ("wq_r", 24), ("tk_s", 4), ("tk_r", 4),
            ("wz_s", 4), ("wz_r", 4), ("wc_s", 4), ("wc_r", 4), ("qa_s", 16), ("qa_r", 16),
            ("mx_s", 16), ("mx_r", 16), ("wo_s", 8), ("wo_r", 8), ("woc_s", 8), ("woc_r", 8),
            ("w1_s", 8), ("w1_r", 8), ("w1c_s", 8), ("w1c_r", 8), ("w2_s", 2), ("w2_r", 2), ("w2c_s", 2),
            ("w2c_r", 2), ("ct_s", 4), ("ct_r", 4),
        )
    ],
)


def forward_kernel(*refs):
    names = [n[0] for n in FORWARD_IN] + [n[0] for n in FORWARD_OUT] + [n[0] for n in FORWARD_SCRATCH]
    r = SimpleNamespace(**dict(zip(names, refs, strict=True)))
    c, s, core, x, yl = place()
    z, yh = c // 4, lax.rem(c // 2, 2)
    sib = (sibling(c), s)
    at_home = z == x

    barrier = pltpu.get_barrier_semaphore()

    def hail(device):
        pl.semaphore_signal(barrier, inc=1, device_id=device, device_id_type=MESH)

    loop(8, lambda k: hail((c, lax.rem(s + k, 8))), 1)
    loop(16, lambda k: hail((lax.rem(c + k, 16), s)), 1)

    def hail_source(k):
        co, so = x * 4 + lax.rem(k, 4), 2 * (k // 4) + yl
        not_when((co == c) & (so == s), lambda: hail((co, so)))

    loop(16, hail_source)

    for i, name in enumerate(VECTORS):
        r.small[i : i + 1, :] = getattr(r, name)[...].astype(F32)
    r.small[8:12, :] = r.fc1_bias[...].astype(F32)
    lane = lax.broadcasted_iota(jnp.int32, (4, 128), 1)
    r.small[12:16, :] = jnp.where(
        lane == 0, r.lengths[0].astype(F32), jnp.where(lane == 1, r.lengths[1].astype(F32), 0.0)
    )
    pl.semaphore_wait(barrier, 38 - at_home.astype(jnp.int32))

    def await_block(dst, recv_sem):
        remote(dst, dst, r.local.at[15], recv_sem, sib).wait_recv()

    slice_rows = pl.ds(pick(z * 2 + core, 16), 16)
    columns_of = lambda peer: pl.ds(pick(peer, 128), 128)

    def small_to(k):
        return remote(
            r.small, r.small_all.at[:, columns_of(s)], r.sm_s.at[k], r.sm_r.at[k], (c, lax.rem(s + k, 8))
        )

    def wq_to(k, t):
        peer = lax.rem(s + k, 8)
        cols = pl.ds(pick(t * 4 + peer // 2, 256), 256)
        return remote(
            r.w_qkv.at[slice_rows, cols],
            r.wq_all.at[s, slice_rows, t * 256 : t * 256 + 256],
            r.wq_s.at[3 * k + t],
            r.wq_r.at[3 * k + t],
            (c, peer),
        )

    def tok_to(k):
        peer = 2 * lax.rem(x + k, 4) + yl
        return remote(r.tok, r.tok_all.at[x], r.tk_s.at[k], r.tk_r.at[k], (c, peer))

    loop(8, lambda k: small_to(k).start(), 1)

    def wq_start(k):
        for t in range(3):
            wq_to(k, t).start()

    loop(8, wq_start, 1)
    tok_to(1).start()
    tok_to(3).start()
    tok_to(2).start()
    own = [
        pltpu.make_async_copy(
            r.w_qkv.at[slice_rows, pl.ds(pick(t * 4 + x, 256), 256)],
            r.wq_all.at[s, slice_rows, t * 256 : t * 256 + 256],
            r.local.at[t],
        )
        for t in range(3)
    ]
    for copy in own:
        copy.start()
    r.small_all[:, columns_of(s)] = r.small[...]
    r.tok_all[x] = r.tok[...]

    sub = lax.broadcasted_iota(jnp.int32, (64, 128), 0)

    def set_places(k):
        pair = r.block_pairs[k]
        block = jnp.where(sub < 32, pair, 31 - pair)
        r.places[pl.ds(pick(k, 64), 64), :] = (block * 32 + lax.rem(sub, 32)).astype(F32)

    loop(16, set_places)

    for copy in own:
        copy.wait()

    def wq_arrived(k):
        origin = lax.rem(s - k + 8, 8)
        for t in range(3):
            await_block(r.wq_all.at[origin, slice_rows, t * 256 : t * 256 + 256], r.wq_r.at[3 * k + t])

    loop(8, wq_arrived, 1)

    def slice_of(zp, core_of):
        return r.wq_all.at[:, pl.ds(pick(zp * 2 + core_of, 16), 16)]

    def wq_along(k):
        block = slice_of(z, core)
        return remote(block, block, r.wz_s.at[k], r.wz_r.at[k], (lax.rem(c + 4 * k, 16), s))

    def wq_across(k):
        block = slice_of(lax.rem(z - k + 4, 4), core)
        return remote(block, block, r.wc_s.at[k], r.wc_r.at[k], sib)

    wq_along(1).start()
    wq_along(3).start()
    wq_along(2).start()
    wq_across(0).start()
    loop(
        8,
        lambda k: await_block(r.small_all.at[:, columns_of(lax.rem(s - k + 8, 8))], r.sm_r.at[k]),
        1,
    )
    for k in (1, 3, 2):
        await_block(slice_of(lax.rem(z - k + 4, 4), core), r.wz_r.at[k])
        wq_across(k).start()

    half = lambda which, rows: pl.ds(pick(which, rows), rows)

    def wo_to(k):
        peer = lax.rem(s + k, 8)
        return remote(
            r.w_out.at[half(core, 64)], r.wo_all.at[s, half(core, 64)], r.wo_s.at[k], r.wo_r.at[k], (c, peer)
        )

    def cot_to(k):
        peer = 2 * lax.rem(x + k, 4) + yl
        return remote(r.cot, r.cot_all.at[x], r.ct_s.at[k], r.ct_r.at[k], (c, peer))

    def w1_to(k):
        peer = lax.rem(s + k, 8)
        return remote(
            r.w_fc1.at[half(core, 64), pl.ds(pick(peer // 2, 1024), 1024)],
            r.w1_all.at[s, half(core, 64)],
            r.w1_s.at[k],
            r.w1_r.at[k],
            (c, peer),
        )

    def w2_to():
        mate = (c, s + 1 - 2 * yl)
        rows = half(core, 256)
        return remote(r.w_fc2.at[rows], r.w2_all.at[yl, rows], r.w2_s.at[0], r.w2_r.at[0], mate)

    own = [
        pltpu.make_async_copy(r.w_out, r.wo_all.at[s], r.local.at[4]),
        pltpu.make_async_copy(r.w_fc1.at[:, pl.ds(pick(x, 1024), 1024)], r.w1_all.at[s], r.local.at[5]),
        pltpu.make_async_copy(r.w_fc2, r.w2_all.at[yl], r.local.at[6]),
        pltpu.make_async_copy(r.cot, r.cot_all.at[x], r.local.at[7]),
    ]

    gain_one, bias_one = r.small_all[0:1, :], r.small_all[1:2, :]
    head_cols = pl.ds(pick(x, 256), 256)
    bias_qkv = (r.small_all[2:3, head_cols], None, r.small_all[3:4, head_cols])

    def parts_to(target):
        return remote(
            r.qkv.at[target], r.parts.at[c], r.qa_s.at[target], r.qa_r.at[c], (target, s)
        )

    def qkv_block(k):
        hop = k + (k // 2) * (1 - 2 * lax.rem(k, 2))
        origin = lax.rem(x - hop + 4, 4)

        @pl.when(k > 0)
        def _():
            await_block(r.tok_all.at[origin], r.tk_r.at[hop])

        normed, _ = norm_rows(r.tok_all[origin].astype(F32))
        r.attn_all[origin] = (normed * gain_one + bias_one).astype(BF16)

        @pl.when(k == 0)
        def _():
            for j in range(4):
                await_block(slice_of(lax.rem(z - j + 4, 4), 1 - core), r.wc_r.at[j])

        for t in range(3):
            cols = slice(t * 256, t * 256 + 256)
            acc = dot(r.attn_all[origin], r.wq_all[:, :, cols].reshape(1024, 256))
            if bias_qkv[t] is not None:
                acc = acc + bias_qkv[t]
            acc = acc.astype(BF16)
            for j in range(2):
                for p in range(2):
                    r.qkv[origin * 4 + j * 2 + p, :, t * 128 : t * 128 + 128] = acc[
                        j * 64 : j * 64 + 64, p * 128 : p * 128 + 128
                    ]

        for j in range(4):
            target = origin * 4 + j
            not_when(target == c, lambda: parts_to(target).start())

    loop(4, qkv_block)
    loop(8, lambda k: wo_to(k).start(), 1)
    for k in (1, 3, 2):
        cot_to(k).start()
    for copy in own:
        copy.start()
    r.parts[c] = r.qkv[c]
    loop(16, lambda k: await_block(r.parts.at[lax.rem(c + k, 16)], r.qa_r.at[lax.rem(c + k, 16)]), 1)
    w2_to().start()
    loop(8, lambda k: w1_to(k).start(), 1)

    slot_lane = lax.rem(c // 2, 2)
    row = r.small_all[12:13, columns_of(2 * (c // 4) + yl)]
    lane = lax.broadcasted_iota(jnp.int32, (1, 128), 1)
    length = jnp.sum(jnp.where(lane == slot_lane, row, 0.0), axis=1, keepdims=True)
    head_lane = lax.broadcasted_iota(jnp.int32, (1, 128), 1) // 64
    value_t = r.parts[:, :, 256:384].reshape(1024, 128).T

    def attend(i):
        keys = r.parts[:, :, 128:256].reshape(1024, 128)
        key_place = r.places[:, 0:1]
        query_place = r.places[pl.ds(pick(i, 256), 256), :].T[0:1, :]
        allowed = (key_place < length) & (key_place <= query_place)
        queries = r.parts[pl.ds(i * 4, 4), :, 0:128].reshape(256, 128) * jnp.asarray(0.125, BF16)
        cols = pl.ds(pick(i, 256), 256)
        for h in range(2):
            mine = jnp.where(head_lane == h, queries, jnp.zeros_like(queries))
            scores = jnp.where(allowed, dot_nt(keys, mine), negative)
            powers = jnp.exp(scores - jnp.max(scores, axis=0, keepdims=True))
            low = (powers * (1.0 / jnp.sum(powers, axis=0, keepdims=True))).astype(BF16)
            r.probs[h, :, cols] = low
            r.mix_t[h * 64 : h * 64 + 64, cols] = dot(value_t[h * 64 : h * 64 + 64], low)

    loop(4, attend)
    r.mixed[...] = r.mix_t[...].T.astype(BF16).reshape(16, 64, 128)

    def mix_to(k):
        peer = lax.rem(c + k, 16)
        return remote(
            r.mixed.at[peer],
            r.mix_rows.at[yh, :, head_columns(x, core)],
            r.mx_s.at[k],
            r.mx_r.at[x * 4 + yh * 2 + core],
            (peer, 2 * z + yl),
        )

    loop(16, lambda k: mix_to(k).start(), 1)
    not_when(at_home, lambda: mix_to(0).start())

    @pl.when(at_home)
    def _():
        r.mix_rows[yh, :, head_columns(x, core)] = r.mixed[c]

    def across(whole, recv, send_next, recv_next, rows):
        def body(k):
            block = whole.at[lax.rem(s - k + 8, 8), half(core, rows)]
            await_block(block, recv.at[k])
            remote(block, block, send_next.at[k], recv_next.at[k], sib).start()

        return body

    loop(8, across(r.wo_all, r.wo_r, r.woc_s, r.woc_r, 64), 1)
    loop(
        8,
        lambda k: await_block(r.wo_all.at[lax.rem(s - k + 8, 8), half(1 - core, 64)], r.woc_r.at[k]),
        1,
    )
    own[0].wait()

    def mix_arrived(k):
        xo, yo, ko = k // 4, lax.rem(k // 2, 2), lax.rem(k, 2)
        here = at_home & (xo == x) & (yo == yh) & (ko == core)
        not_when(here, lambda: await_block(r.mix_rows.at[yo, :, head_columns(xo, ko)], r.mx_r.at[k]))

    loop(16, mix_arrived)

    mix = r.mix_rows[...].reshape(128, 1024)
    hidden = r.tok[...].astype(F32) + (dot(mix, r.wo_all[...].reshape(1024, 1024)) + r.small_all[4:5, :])
    r.hidden[...] = hidden
    normed, _ = norm_rows(hidden)
    r.mlp_in[...] = (normed * r.small_all[5:6, :] + r.small_all[6:7, :]).astype(BF16)

    loop(8, across(r.w1_all, r.w1_r, r.w1c_s, r.w1c_r, 64), 1)
    block = r.w2_all.at[1 - yl, half(core, 256)]
    await_block(block, r.w2_r.at[0])
    w2_across = remote(block, block, r.w2c_s.at[0], r.w2c_r.at[0], sib)
    w2_across.start()
    for k in range(1, 4):
        await_block(r.cot_all.at[lax.rem(x - k + 4, 4)], r.ct_r.at[k])
    loop(
        8,
        lambda k: await_block(r.w1_all.at[lax.rem(s - k + 8, 8), half(1 - core, 64)], r.w1c_r.at[k]),
        1,
    )
    await_block(r.w2_all.at[1 - yl, half(1 - core, 256)], r.w2c_r.at[0])
    for copy in own[1:]:
        copy.wait()

    def sent(k):
        small_to(k).wait_send()
        for t in range(3):
            wq_to(k, t).wait_send()
        wo_to(k).wait_send()
        w1_to(k).wait_send()
        for whole, sem in ((r.wo_all, r.woc_s), (r.w1_all, r.w1c_s)):
            block = whole.at[lax.rem(s - k + 8, 8), half(core, 64)]
            remote(block, block, sem.at[k], sem.at[k], sib).wait_send()

    loop(8, sent, 1)
    for k in range(1, 4):
        tok_to(k).wait_send()
        wq_along(k).wait_send()
        cot_to(k).wait_send()
    for k in range(4):
        wq_across(k).wait_send()
    w2_to().wait_send()
    w2_across.wait_send()
    loop(16, lambda k: not_when(k == c, lambda: parts_to(k).wait_send()))
    loop(16, lambda k: mix_to(k).wait_send(), 1)
    not_when(at_home, lambda: mix_to(0).wait_send())


def named_call(kernel, name, cid, ins, outs, scratch, operands):
    results = pl.pallas_call(
        kernel,
        name=name,
        out_shape=[jax.ShapeDtypeStruct(shape, dtype) for _, _, shape, dtype in outs],
        in_specs=[pl.BlockSpec(memory_space=space) for _, space in ins],
        out_specs=[pl.BlockSpec(memory_space=space) for _, space, _, _ in outs],
        scratch_shapes=[kind for _, kind in scratch],
        compiler_params=pltpu.CompilerParams(
            collective_id=cid, has_side_effects=True, vmem_limit_bytes=60 << 20
        ),
    )(*[operands[name] for name, _ in ins])
    return SimpleNamespace(**dict(zip([o[0] for o in outs], results, strict=True)))


def mix_forth(rows_in, parts, a0, a1, local):
    c, s, core, x, yl = place()
    z, yh = c // 4, lax.rem(c // 2, 2)
    barrier = pltpu.get_barrier_semaphore()
    at_home = z == x
    source = 2 * z + yl
    for k in range(1, 16):
        pl.semaphore_signal(
            barrier, inc=1, device_id=(lax.rem(c + k, 16), source), device_id_type=MESH
        )

    @pl.when(jnp.logical_not(at_home))
    def _():
        pl.semaphore_signal(barrier, inc=1, device_id=(c, source), device_id_type=MESH)

    pl.semaphore_wait(barrier, 16 - at_home.astype(jnp.int32))

    def copy_to(k):
        xo, yo, ko = k // 4, (k // 2) % 2, k % 2
        return pltpu.make_async_remote_copy(
            src_ref=rows_in.at[yo, :, pl.ds(xo * 256 + ko * 128, 128)],
            dst_ref=parts.at[c],
            send_sem=a0.at[k],
            recv_sem=a1.at[c],
            device_id=(x * 4 + yo * 2 + ko, 2 * xo + yl),
            device_id_type=MESH,
        )

    for k in range(16):
        xo, yo, ko = k // 4, (k // 2) % 2, k % 2
        mine = at_home & (xo == x) & (yo == yh) & (ko == core)

        @pl.when(jnp.logical_not(mine))
        def _():
            copy_to(k).start()

    @pl.when(at_home)
    def _():
        copy = pltpu.make_async_copy(
            rows_in.at[yh, :, head_columns(x, core)], parts.at[c], local.at[0]
        )
        copy.start()
        copy.wait()

    for k in range(1, 16):
        origin = lax.rem(c + k, 16)
        arrived(parts.at[origin], (a0, a1), origin, c, s)

    @pl.when(jnp.logical_not(at_home))
    def _():
        arrived(parts.at[c], (a0, a1), c, c, s)

    for k in range(16):
        xo, yo, ko = k // 4, (k // 2) % 2, k % 2
        mine = at_home & (xo == x) & (yo == yh) & (ko == core)

        @pl.when(jnp.logical_not(mine))
        def _():
            copy_to(k).wait_send()


def gather_x(mine, whole, a0, a1, local):
    c, s, core, x, yl = place()
    greet([(c, 2 * lax.rem(x + k, 4) + yl) for k in range(1, 4)])
    out = []
    for k in range(1, 4):
        peer = lax.rem(x + k, 4)
        out.append(send(mine, whole.at[x], (a0, a1), k - 1, (c, 2 * peer + yl)))
    own = pltpu.make_async_copy(mine, whole.at[x], local.at[0])
    own.start()
    for k in range(1, 4):
        arrived(whole.at[lax.rem(x - k + 4, 4)], (a0, a1), k - 1, c, s)
    for copy in out:
        copy.wait_send()
    own.wait()


def scatter_x(part_one, part_two, got_one, got_two, a0, a1, b0, b1, local):
    c, s, core, x, yl = place()
    greet([(c, 2 * lax.rem(x + k, 4) + yl) for k in range(1, 4)])
    out = []
    for part, got, sems in ((part_one, got_one, (a0, a1)), (part_two, got_two, (b0, b1))):
        for k in range(1, 4):
            peer = lax.rem(x + k, 4)
            out.append(send(part.at[peer], got.at[k - 1], sems, k - 1, (c, 2 * peer + yl)))
    for got, sems in ((got_one, (a0, a1)), (got_two, (b0, b1))):
        for k in range(1, 4):
            arrived(got.at[k - 1], sems, k - 1, c, s)
    for copy in out:
        copy.wait_send()


def heads_back(parts, whole, a0, a1, local):
    c, s, core, x, yl = place()
    greet([(lax.rem(c + k, 16), s) for k in range(1, 16)])
    cols = pl.ds(pl.multiple_of(core * 384, 128), 384)
    out = []
    for k in range(1, 16):
        peer = lax.rem(c + k, 16)
        out.append(send(parts.at[peer], whole.at[c // 2, :, cols], (a0, a1), k - 1, (peer, s)))
    own = pltpu.make_async_copy(parts.at[c], whole.at[c // 2, :, cols], local.at[0])
    own.start()
    for k in range(1, 16):
        origin = lax.rem(c - k + 16, 16)
        place_of = pl.ds(pl.multiple_of(lax.rem(origin, 2) * 384, 128), 384)
        arrived(whole.at[origin // 2, :, place_of], (a0, a1), k - 1, c, s)
    for copy in out:
        copy.wait_send()
    own.wait()


def sum_ctx(
    part, g_qkv, g_out, g_one, g_two, vec,
    got_part, s_qkv, s_out, s_one, s_two, s_vec,
    n_qkv, n_out, n_one, n_two, t_qkv, t_out, t_one, t_two, t_vec,
    p0, p1, a0, a1, b0, b1, v0, v1, local,
):
    c, s, core, x, yl = place()
    sib = (sibling(c), s)
    chip = c // 2
    greet(
        [(lax.rem(c + k, 16), s) for k in range(1, 16)]
        + [(c, 2 * lax.rem(x + k, 4) + yl) for k in range(1, 4)]
    )
    out = []
    for k in range(1, 4):
        peer = lax.rem(x + k, 4)
        out.append(send(part.at[peer], got_part.at[k - 1], (p0, p1), k - 1, (c, 2 * peer + yl)))
    for k in range(1, 16):
        peer = lax.rem(c + k, 16)
        out.append(send(vec.at[peer], t_vec.at[k - 1], (v0, v1), k - 1, (peer, s)))
    grads = (
        (g_two, n_two, t_two, s_two),
        (g_one, n_one, t_one, s_one),
        (g_out, n_out, t_out, s_out),
        (g_qkv, n_qkv, t_qkv, s_qkv),
    )
    for i, (g, near, far, total) in enumerate(grads):
        out.append(send(g.at[:, 1 - core], near, (a0, a1), i, sib))
    for i, (g, near, far, total) in enumerate(grads):
        arrived(near, (a0, a1), i, c, s)

        def add(j, _):
            near[j] = (near[j].astype(F32) + g[j, core].astype(F32)).astype(BF16)
            return 0

        lax.fori_loop(0, 8, add, 0)
        for k in range(1, 8):
            peer = lax.rem(chip + k, 8)
            out.append(
                send(near.at[peer], far.at[k - 1], (b0, b1), 7 * i + k - 1, (2 * peer + core, s))
            )
    for k in range(1, 16):
        arrived(t_vec.at[k - 1], (v0, v1), k - 1, c, s)
    s_vec[...] = vec[c] + jnp.sum(t_vec[...], axis=0)
    for i, (g, near, far, total) in enumerate(grads):
        for k in range(1, 8):
            arrived(far.at[k - 1], (b0, b1), 7 * i + k - 1, c, s)

        def add_rows(j, _):
            rows = pl.ds(pl.multiple_of(j * 16, 16), 16)
            acc = near[chip, rows].astype(F32)
            for k in range(7):
                acc = acc + far[k, rows].astype(F32)
            total[rows] = acc
            return 0

        lax.fori_loop(0, 4, add_rows, 0)
    for k in range(1, 4):
        arrived(got_part.at[k - 1], (p0, p1), k - 1, c, s)
    for copy in out:
        copy.wait_send()


def to_owners(
    s_qkv, s_out, s_one, s_two, s_vec,
    r_qkv, r_out, r_one, r_two, r_vec,
    a0, a1, b0, b1, d0, d1, e0, e1, f0, f1, local,
):
    c, s, core, x, yl = place()
    barrier = pltpu.get_barrier_semaphore()
    low = lax.rem(c, 4)
    to_c, to_x = 4 * x + c // 4, low
    from_c, from_x = 4 * low + x, c // 4
    stays = (to_c == c) & (to_x == x)
    for k in range(1, 8):
        pl.semaphore_signal(
            barrier, inc=1, device_id=(c, lax.rem(s + k, 8)), device_id_type=MESH
        )
    for y in range(2):

        @pl.when(jnp.logical_not(stays & (yl == y)))
        def _():
            pl.semaphore_signal(
                barrier, inc=1, device_id=(from_c, 2 * from_x + y), device_id_type=MESH
            )

    pl.semaphore_wait(barrier, 9 - stays.astype(jnp.int32))
    out = []

    def two_to(y):
        return pltpu.make_async_remote_copy(
            src_ref=s_two.at[y],
            dst_ref=r_two.at[yl],
            send_sem=e0.at[y],
            recv_sem=e1.at[yl],
            device_id=(to_c, 2 * to_x + y),
            device_id_type=MESH,
        )

    for y in range(2):

        @pl.when(jnp.logical_not(stays & (yl == y)))
        def _():
            two_to(y).start()

    @pl.when(stays)
    def _():
        copy = pltpu.make_async_copy(s_two.at[yl], r_two.at[yl], local.at[0])
        copy.start()
        copy.wait()

    triples = ((s_qkv, r_qkv, (a0, a1)), (s_out, r_out, (b0, b1)), (s_one, r_one, (d0, d1)))
    for k in range(1, 8):
        peer = lax.rem(s + k, 8)
        rows = pl.ds(pl.multiple_of(peer * 8, 8), 8)
        for src, dst, sems in triples:
            out.append(send(src.at[rows], dst.at[s], sems, k - 1, (c, peer)))
        out.append(send(s_vec, r_vec.at[s], (f0, f1), k - 1, (c, peer)))
    own_rows = pl.ds(pl.multiple_of(s * 8, 8), 8)
    own = [
        pltpu.make_async_copy(src.at[own_rows], dst.at[s], local.at[1 + i])
        for i, (src, dst, _) in enumerate(triples)
    ] + [pltpu.make_async_copy(s_vec, r_vec.at[s], local.at[4])]
    for copy in own:
        copy.start()
    for k in range(1, 8):
        origin = lax.rem(s - k + 8, 8)
        for _, dst, sems in triples:
            arrived(dst.at[origin], sems, k - 1, c, s)
        arrived(r_vec.at[origin], (f0, f1), k - 1, c, s)
    for y in range(2):

        @pl.when(jnp.logical_not(stays & (yl == y)))
        def _():
            arrived(r_two.at[y], (e0, e1), y, c, s)

    for copy in out:
        copy.wait_send()
    for y in range(2):

        @pl.when(jnp.logical_not(stays & (yl == y)))
        def _():
            two_to(y).wait_send()

    for copy in own:
        copy.wait()


def exact_gelu(inputs):
    return jax.nn.gelu(inputs, approximate=False)


def norm_parts(inputs):
    centre = inputs - jnp.mean(inputs, axis=-1, keepdims=True)
    spread = jnp.mean(centre * centre, axis=-1, keepdims=True)
    inverse = lax.rsqrt(spread + eps_norm)
    return (centre * inverse, inverse)


def norm_back(grad_normed, normed, inverse, gain):
    scaled = grad_normed * gain
    centred = scaled - jnp.mean(scaled, axis=-1, keepdims=True)
    return inverse * (centred - normed * jnp.mean(scaled * normed, axis=-1, keepdims=True))


def dot(left, right):
    return jnp.dot(left, right, preferred_element_type=F32)


def dot_rows(left, right):
    return jnp.einsum("rd,re->de", left, right, preferred_element_type=F32)


def dot_back(left, right):
    return jnp.einsum("re,de->rd", left, right, preferred_element_type=F32)


def shards(
    tokens,
    lengths,
    block_pairs,
    ln1_gain,
    ln1_bias,
    w_qkv,
    query_bias,
    value_bias,
    w_out,
    out_bias,
    ln2_gain,
    ln2_bias,
    w_fc1,
    fc1_bias,
    w_fc2,
    fc2_bias,
    out_cotangent,
):
    c, s = lax.axis_index("ctx"), lax.axis_index("shard")
    core, x, yl = c % 2, s // 2, s % 2
    scale = HEAD_DIM ** (-0.5)
    tok = tokens.reshape(128, 1024)
    cot = out_cotangent.reshape(128, 1024)

    f = named_call(
        forward_kernel,
        "forward",
        0,
        FORWARD_IN,
        FORWARD_OUT,
        FORWARD_SCRATCH,
        dict(
            lengths=lengths,
            block_pairs=block_pairs,
            tok=tok,
            ln1_gain=ln1_gain.reshape(1, 128),
            ln1_bias=ln1_bias.reshape(1, 128),
            query_bias=query_bias.reshape(1, 128),
            value_bias=value_bias.reshape(1, 128),
            out_bias=out_bias.reshape(1, 128),
            ln2_gain=ln2_gain.reshape(1, 128),
            ln2_bias=ln2_bias.reshape(1, 128),
            fc2_bias=fc2_bias.reshape(1, 128),
            fc1_bias=fc1_bias.reshape(4, 128),
            w_qkv=w_qkv,
            w_out=w_out,
            w_fc1=w_fc1,
            w_fc2=w_fc2,
            cot=cot,
        ),
    )
    gain_one, gain_two, bias_down = f.small_all[0], f.small_all[5], f.small_all[7]
    bias_up = lax.dynamic_slice_in_dim(
        f.small_all[8:12].reshape(4, 8, 128).transpose(1, 0, 2).reshape(4096), x * 1024, 1024
    )
    len_x = f.small_all[12].reshape(4, 2, 128)[:, :, :2]
    len_x = jnp.where(yl == 0, len_x[:, 0], len_x[:, 1]).reshape(8)
    my_places = lax.dynamic_slice_in_dim(f.places[:, 0], c * 64, 64)
    w_q = f.wq_all.reshape(1024, 768)
    w_o = f.wo_all.reshape(1024, 1024)
    w_up = f.w1_all.reshape(1024, 1024)
    w_down = f.w2_all.reshape(1024, 1024)
    attn_in = f.attn_all.reshape(512, 1024)
    mix_rows = f.mix_rows.reshape(128, 1024)
    cot_all = f.cot_all
    parts = f.parts.reshape(1024, 3, 2, 64)
    q, k, v = parts[:, 0], parts[:, 1], parts[:, 2]

    residual = tok.astype(F32)
    hidden = f.hidden
    normed_two, inverse_two = norm_parts(hidden)
    mlp_in = f.mlp_in
    (mlp_all,) = comm_call(gather_x, "gather_x", 3, [((4, 128, 1024), BF16)], [3], (mlp_in,))
    mlp_all = mlp_all.reshape(512, 1024)

    pre_act = dot(mlp_all, w_up) + bias_up
    activated, gelu_pull = jax.vjp(exact_gelu, pre_act)
    act_low = activated.astype(BF16)
    mlp_part = dot(act_low, w_down)
    valid_all = (my_places[None, :] < len_x[:, None]).astype(F32).reshape(512, 1)
    g_all = cot_all.reshape(512, 1024).astype(F32) * valid_all
    g_low = g_all.astype(BF16)
    grad_act = dot_back(g_low, w_down)
    grad_pre = gelu_pull(grad_act)[0]
    grad_up_b = jnp.sum(grad_pre, axis=0)
    grad_pre_low = grad_pre.astype(BF16)
    gm_part = dot_back(grad_pre_low, w_up)
    g_two = dot_rows(act_low, g_low).astype(BF16)
    g_one = dot_rows(mlp_all, grad_pre_low).astype(BF16)
    gm_part = gm_part.reshape(4, 128, 1024)
    mlp_part = mlp_part.reshape(4, 128, 1024)
    got_gm, got_out = comm_call(
        scatter_x,
        "scatter_x",
        4,
        [((3, 128, 1024), BF16)] * 2,
        [3, 3],
        (gm_part.astype(BF16), mlp_part.astype(BF16)),
    )

    def own_block(blocks4):
        return lax.dynamic_index_in_dim(blocks4, x, 0, keepdims=False)

    grad_mlp_in = own_block(gm_part) + jnp.sum(got_gm.astype(F32), axis=0)
    mlp_out = own_block(mlp_part) + jnp.sum(got_out.astype(F32), axis=0) + bias_down
    row_valid = own_block(valid_all.reshape(4, 128, 1))
    layer_out = (row_valid * (hidden + mlp_out)).astype(BF16).reshape(tokens.shape)
    grad_out = cot.astype(F32) * row_valid
    grad_down_b = jnp.sum(grad_out, axis=0)
    grad_gain_two = jnp.sum(grad_mlp_in * normed_two, axis=0)
    grad_bias_two = jnp.sum(grad_mlp_in, axis=0)
    grad_hidden = grad_out + norm_back(grad_mlp_in, normed_two, inverse_two, gain_two)
    hidden_low = grad_hidden.astype(BF16)
    grad_out_b = jnp.sum(grad_hidden, axis=0)
    grad_mixed = dot_back(hidden_low, w_o).astype(BF16).reshape(2, 64, 1024)
    g_out = dot_rows(mix_rows, hidden_low).astype(BF16)
    (gm,) = comm_call(mix_forth, "mix_forth", 5, [((16, 64, 128), BF16)], [16], (grad_mixed,))

    gm = gm.reshape(1024, 2, 64)
    probs_low = jnp.swapaxes(f.probs, 1, 2)
    probs = probs_low.astype(F32)
    grad_probs = jnp.einsum("qhd,khd->hqk", gm, v, preferred_element_type=F32)
    delta = jnp.sum(probs * grad_probs, axis=-1, keepdims=True)
    grad_scores = (probs * (grad_probs - delta)).astype(BF16)
    gq = jnp.einsum("hqk,khd->qhd", grad_scores, k, preferred_element_type=F32) * scale
    gk = jnp.einsum("hqk,qhd->khd", grad_scores, q, preferred_element_type=F32) * scale
    gv = jnp.einsum("hqk,qhd->khd", probs_low, gm, preferred_element_type=F32)
    gq, gk, gv = (g.reshape(1024, 128) for g in (gq, gk, gv))
    grad_bq, grad_bv = jnp.sum(gq, axis=0), jnp.sum(gv, axis=0)
    g_parts = jnp.concatenate([gq, gk, gv], axis=1).astype(BF16).reshape(16, 64, 384)
    (g_qkv,) = comm_call(heads_back, "heads_back", 6, [((8, 64, 768), BF16)], [15], (g_parts,))
    g_qkv = g_qkv.reshape(512, 2, 3, 128).swapaxes(1, 2).reshape(512, 768)
    ga_part = dot_back(g_qkv, w_q).reshape(4, 128, 1024)
    gw_qkv = dot_rows(attn_in, g_qkv).astype(BF16)

    zeros = jnp.zeros((1024,), F32)
    head_at = x * 256 + core * 128
    full = [
        grad_out_b,
        grad_gain_two,
        grad_bias_two,
        grad_down_b,
        lax.dynamic_update_slice(zeros, grad_bq, (head_at,)),
        lax.dynamic_update_slice(zeros, grad_bv, (head_at,)),
    ]
    up_full = lax.dynamic_update_slice(jnp.zeros((4096,), F32), grad_up_b, (x * 1024,))

    def chunks(vectors, tail):
        body = jnp.stack([v.reshape(16, 64) for v in vectors], axis=1).reshape(16, -1, 128)
        if tail is not None:
            body = jnp.concatenate([body, tail.reshape(16, 2, 128)], axis=1)
        return jnp.pad(body, ((0, 0), (0, 8 - body.shape[1]), (0, 0)))

    vec = chunks(full, up_full)
    sums = comm_call(
        sum_ctx,
        "sum_ctx",
        7,
        [
            ((3, 128, 1024), BF16),
            ((64, 768), F32),
            ((64, 1024), F32),
            ((64, 1024), F32),
            ((64, 1024), F32),
            ((8, 128), F32),
        ],
        [3, 4, 28, 15],
        (
            ga_part.astype(BF16),
            gw_qkv.reshape(8, 2, 64, 768),
            g_out.reshape(8, 2, 64, 1024),
            g_one.reshape(8, 2, 64, 1024),
            g_two.reshape(8, 2, 64, 1024),
            vec,
        ),
        spaces=[ANY, VMEM, VMEM, VMEM, VMEM, VMEM],
        out_spaces=[ANY, VMEM, VMEM, VMEM, VMEM, VMEM],
        scratch=[
            pltpu.VMEM((8, 64, 768), BF16),
            pltpu.VMEM((8, 64, 1024), BF16),
            pltpu.VMEM((8, 64, 1024), BF16),
            pltpu.VMEM((8, 64, 1024), BF16),
            pltpu.VMEM((7, 64, 768), BF16),
            pltpu.VMEM((7, 64, 1024), BF16),
            pltpu.VMEM((7, 64, 1024), BF16),
            pltpu.VMEM((7, 64, 1024), BF16),
            pltpu.VMEM((15, 8, 128), F32),
        ],
    )
    got_ga, s_qkv, s_out, s_one, s_two, s_vec = sums
    normed_one, inverse_one = norm_parts(residual)
    grad_attn_in = own_block(ga_part) + jnp.sum(got_ga.astype(F32), axis=0)
    input_grad = (
        (grad_hidden + norm_back(grad_attn_in, normed_one, inverse_one, gain_one))
        .astype(BF16)
        .reshape(tokens.shape)
    )
    vec_one = chunks([jnp.sum(grad_attn_in * normed_one, axis=0), jnp.sum(grad_attn_in, axis=0)], None)
    (s_vec_one,) = comm_call(
        sum_vec,
        "sum_vec",
        8,
        [((8, 128), F32)],
        [15],
        (vec_one,),
        spaces=[VMEM],
        out_spaces=[VMEM],
        scratch=[pltpu.VMEM((15, 8, 128), F32)],
    )
    s_vec = jnp.concatenate([s_vec, s_vec_one], axis=0)
    r_qkv, r_out, r_one, r_two, r_vec = comm_call(
        to_owners,
        "to_owners",
        9,
        [
            ((8, 8, 768), F32),
            ((8, 8, 1024), F32),
            ((8, 8, 1024), F32),
            ((2, 32, 1024), F32),
            ((8, 16, 128), F32),
        ],
        [7, 7, 7, 2, 7],
        (s_qkv, s_out, s_one, s_two.reshape(2, 32, 1024), s_vec),
    )
    by_x = jnp.sum(r_qkv.reshape(4, 2, 8, 3, 256), axis=1)
    grad_w_qkv = by_x.transpose(1, 2, 0, 3).reshape(8, 3072)
    grad_w_out = jnp.sum(r_out, axis=0)
    one_x = jnp.sum(r_one.reshape(4, 2, 8, 1024), axis=1)
    grad_w_fc1 = one_x.transpose(1, 0, 2).reshape(8, 4096)
    grad_w_fc2 = jnp.sum(r_two, axis=0)
    vec_sum = jnp.sum(r_vec, axis=0)
    small_sums = vec_sum[:3].reshape(6, 8, 8)
    small_sums = lax.dynamic_index_in_dim(small_sums, s, 1, keepdims=False)
    up_sum = lax.dynamic_index_in_dim(vec_sum[3:5].reshape(8, 32), s, 0, keepdims=False)
    one_sums = vec_sum[8:9].reshape(2, 8, 8)
    one_sums = lax.dynamic_index_in_dim(one_sums, s, 1, keepdims=False)
    return (
        layer_out,
        input_grad,
        one_sums[0],
        one_sums[1],
        grad_w_qkv,
        small_sums[4],
        small_sums[5],
        grad_w_out,
        small_sums[0],
        small_sums[1],
        small_sums[2],
        grad_w_fc1,
        up_sum,
        grad_w_fc2,
        small_sums[3],
    )


def sum_vec(vec, total, got, a0, a1, local):
    c, s, core, x, yl = place()
    greet([(lax.rem(c + k, 16), s) for k in range(1, 16)])
    out = []
    for k in range(1, 16):
        peer = lax.rem(c + k, 16)
        out.append(send(vec.at[peer], got.at[k - 1], (a0, a1), k - 1, (peer, s)))
    for k in range(1, 16):
        arrived(got.at[k - 1], (a0, a1), k - 1, c, s)
    total[...] = vec[c] + jnp.sum(got[...], axis=0)
    for copy in out:
        copy.wait_send()


def solution(mesh):
    one, both = P("shard"), P(("ctx", "shard"))
    rows, both_rows = P("shard", None), P(("ctx", "shard"), None)
    whole = P("ctx", "shard", None, None)
    return jax.shard_map(
        shards,
        mesh=mesh,
        in_specs=(
            whole, one, P(), one, one, rows, one, one, rows, one, one, one, rows, one, rows, one, whole,
        ),
        out_specs=(
            whole, whole, both, both, both_rows, both, both, both_rows, both, both, both,
            both_rows, both, both_rows, both,
        ),
        check_vma=False,
    )
```

```python
from types import SimpleNamespace

import jax
import jax.numpy as jnp
from jax import lax
from jax.experimental import pallas as pl
from jax.experimental.pallas import tpu as pltpu
from jax.sharding import PartitionSpec as P

HEADS = 16
HEAD_DIM = 64
MESH = pl.DeviceIdType.MESH
ANY = pl.ANY
VMEM = pltpu.VMEM
F32 = jnp.float32
BF16 = jnp.bfloat16

eps_norm = 1e-05
negative = -1e30


def place():
    c, s = lax.axis_index("ctx"), lax.axis_index("shard")
    return c, s, lax.rem(c, 2), s // 2, lax.rem(s, 2)


def sibling(c):
    return c + 1 - 2 * lax.rem(c, 2)


def norm_back(grad_normed, normed, inverse, gain):
    scaled = grad_normed * gain
    centred = scaled - jnp.mean(scaled, axis=-1, keepdims=True)
    return inverse * (centred - normed * jnp.mean(scaled * normed, axis=-1, keepdims=True))


def dot(left, right):
    return jnp.dot(left, right, preferred_element_type=F32)


def dot_tn(left, right):
    return lax.dot_general(left, right, (((0,), (0,)), ((), ())), preferred_element_type=F32)


def head_columns(x, core):
    return pl.ds(pl.multiple_of(x * 256 + core * 128, 128), 128)


def pick(value, unit):
    return pl.multiple_of(value * unit, unit)


def loop(count, body, first=0):
    def step(k, carry):
        body(k)
        return carry

    lax.fori_loop(first, count, step, 0)


def remote(src, dst, send_sem, recv_sem, device):
    return pltpu.make_async_remote_copy(
        src_ref=src,
        dst_ref=dst,
        send_sem=send_sem,
        recv_sem=recv_sem,
        device_id=device,
        device_id_type=MESH,
    )


def not_when(condition, body):
    pl.when(jnp.logical_not(condition))(body)


def norm_rows(rows):
    centre = rows - jnp.mean(rows, axis=-1, keepdims=True)
    inverse = lax.rsqrt(jnp.mean(centre * centre, axis=-1, keepdims=True) + eps_norm)
    return centre * inverse, inverse


def dot_nt(left, right):
    return lax.dot_general(left, right, (((1,), (1,)), ((), ())), preferred_element_type=F32)


VECTORS = (
    "ln1_gain", "ln1_bias", "query_bias", "value_bias", "out_bias", "ln2_gain", "ln2_bias", "fc2_bias",
)

LAYER_IN = (
    ("lengths", pltpu.SMEM),
    ("block_pairs", pltpu.SMEM),
    ("tok", VMEM),
    *[(name, VMEM) for name in VECTORS],
    ("fc1_bias", VMEM),
    ("w_qkv", ANY),
    ("w_out", ANY),
    ("w_fc1", ANY),
    ("w_fc2", ANY),
    ("cot", ANY),
)

LAYER_OUT = (
    ("layer_out", VMEM, (128, 1024), BF16),
    ("input_grad", VMEM, (128, 1024), BF16),
    ("o_qkv", VMEM, (8, 3072), F32),
    ("o_out", VMEM, (8, 1024), F32),
    ("o_one", VMEM, (8, 4096), F32),
    ("o_two", VMEM, (32, 1024), F32),
    ("o_vec", VMEM, (8, 128), F32),
    ("o_up", VMEM, (1, 128), F32),
)

LAYER_SCRATCH = (
    *[
        (name, pltpu.VMEM(shape, BF16))
        for name, shape in (
            ("tok_all", (4, 128, 1024)), ("attn_all", (4, 128, 1024)), ("cot_all", (4, 128, 1024)),
            ("wq_all", (8, 128, 768)), ("wo_all", (8, 128, 1024)), ("w1_all", (8, 128, 1024)),
            ("w2_all", (2, 512, 1024)), ("qkv", (16, 64, 384)), ("parts", (16, 64, 384)),
            ("probs", (2, 1024, 1024)), ("mixed", (16, 64, 128)), ("mix_rows", (2, 64, 1024)),
            ("mlp_all", (4, 128, 1024)), ("act_all", (4, 128, 1024)), ("gp_all", (4, 128, 1024)),
            ("gm_out", (4, 128, 1024)), ("mo_out", (4, 128, 1024)), ("gm_in", (4, 128, 1024)),
            ("mo_in", (4, 128, 1024)), ("hidden_low", (128, 1024)), ("gmix", (2, 64, 1024)),
            ("gmixed", (16, 64, 128)), ("gparts", (16, 64, 384)), ("gback", (16, 64, 384)),
            ("gqkv", (4, 128, 768)), ("ga_out", (4, 128, 1024)), ("ga_in", (4, 128, 1024)),
            ("g_two", (8, 2, 64, 1024)), ("g_one", (8, 2, 64, 1024)), ("g_out", (8, 2, 64, 1024)),
            ("g_qkv", (8, 2, 64, 768)), ("n_two", (8, 64, 1024)), ("n_one", (8, 64, 1024)),
            ("n_out", (8, 64, 1024)), ("n_qkv", (8, 64, 768)), ("f_two", (8, 64, 1024)),
            ("f_one", (8, 64, 1024)), ("f_out", (8, 64, 1024)), ("f_qkv", (8, 64, 768)),
        )
    ],
    *[
        (name, pltpu.VMEM(shape, F32))
        for name, shape in (
            ("small", (16, 128)), ("small_all", (16, 1024)), ("places", (1024, 128)), ("mix_t", (128, 1024)),
            ("hidden", (128, 1024)), ("gm_own", (128, 1024)), ("mo_own", (128, 1024)),
            ("grad_hidden", (128, 1024)), ("ga_own", (128, 1024)), ("gq_t", (128, 1024)), ("delta", (2, 1024)),
            ("s_two", (64, 1024)), ("s_one", (64, 1024)), ("s_out", (64, 1024)), ("s_qkv", (64, 768)),
            ("r_two", (2, 32, 1024)), ("r_one", (8, 8, 1024)), ("r_out", (8, 8, 1024)), ("r_qkv", (8, 8, 768)),
            ("vec", (8, 1024)), ("vec_sib", (8, 1024)), ("vec_in", (8, 8, 128)), ("vec_sum", (8, 128)),
            ("vec_all", (8, 8, 128)), ("up", (1, 1024)), ("up_sib", (1, 1024)), ("up_in", (8, 1, 1024)),
            ("up_sum", (1, 1024)), ("up_sum_own", (1, 1024)), ("up_all", (8, 1, 1024)),
        )
    ],
    *[
        (name, pltpu.SemaphoreType.DMA((count,)))
        for name, count in (
            ("local", 16), ("sm_s", 8), ("sm_r", 8), ("wq_s", 24), ("wq_r", 24), ("tk_s", 4), ("tk_r", 4),
            ("wz_s", 4), ("wz_r", 4), ("wc_s", 4), ("wc_r", 4), ("qa_s", 16), ("qa_r", 16),
            ("mx_s", 16), ("mx_r", 16), ("wo_s", 8), ("wo_r", 8), ("woc_s", 8), ("woc_r", 8),
            ("w1_s", 8), ("w1_r", 8), ("w1c_s", 8), ("w1c_r", 8), ("w2_s", 2), ("w2_r", 2), ("w2c_s", 2),
            ("w2c_r", 2), ("ct_s", 4), ("ct_r", 4), ("ml_s", 4), ("ml_r", 4), ("gm_s", 4), ("gm_r", 4),
            ("mo_s", 4), ("mo_r", 4), ("mf_s", 16), ("mf_r", 16), ("hb_s", 16), ("hb_r", 16), ("ga_s", 4),
            ("ga_r", 4), ("ns_s", 8), ("ns_r", 8), ("two_s", 8), ("two_r", 8), ("one_s", 8), ("one_r", 8),
            ("out_s", 8), ("out_r", 8), ("qk_s", 8), ("qk_r", 8), ("v1_s", 8), ("v1_r", 8), ("u1_s", 8),
            ("u1_r", 8), ("v2_s", 8), ("v2_r", 8), ("u2_s", 8), ("u2_r", 8), ("t_two_s", 2), ("t_two_r", 2),
            ("t_one_s", 8), ("t_one_r", 8), ("t_out_s", 8), ("t_out_r", 8), ("t_qk_s", 8), ("t_qk_r", 8),
        )
    ],
)


def layer_kernel(*refs):
    names = [n[0] for n in LAYER_IN + LAYER_OUT + LAYER_SCRATCH]
    r = SimpleNamespace(**dict(zip(names, refs, strict=True)))
    c, s, core, x, yl = place()
    z, yh = c // 4, lax.rem(c // 2, 2)
    sib = (sibling(c), s)
    at_home = z == x

    barrier = pltpu.get_barrier_semaphore()

    def hail(device):
        pl.semaphore_signal(barrier, inc=1, device_id=device, device_id_type=MESH)

    loop(8, lambda k: hail((c, lax.rem(s + k, 8))), 1)
    loop(16, lambda k: hail((lax.rem(c + k, 16), s)), 1)

    def hail_source(k):
        co, so = x * 4 + lax.rem(k, 4), 2 * (k // 4) + yl
        not_when((co == c) & (so == s), lambda: hail((co, so)))

    loop(16, hail_source)
    loop(16, lambda k: hail((lax.rem(c + k, 16), 2 * z + yl)), 1)
    not_when(at_home, lambda: hail((c, 2 * z + yl)))

    low = lax.rem(c, 4)
    to_c, to_x, from_c, from_x = 4 * x + z, low, 4 * low + x, z
    stays = (to_c == c) & (to_x == x)
    for y in range(2):
        not_when(stays & (yl == y), lambda: hail((from_c, 2 * from_x + y)))

    for i, name in enumerate(VECTORS):
        r.small[i : i + 1, :] = getattr(r, name)[...].astype(F32)
    r.small[8:12, :] = r.fc1_bias[...].astype(F32)
    lane = lax.broadcasted_iota(jnp.int32, (4, 128), 1)
    r.small[12:16, :] = jnp.where(
        lane == 0, r.lengths[0].astype(F32), jnp.where(lane == 1, r.lengths[1].astype(F32), 0.0)
    )
    pl.semaphore_wait(barrier, 56 - 2 * at_home.astype(jnp.int32) - stays.astype(jnp.int32))

    def await_block(dst, recv_sem):
        remote(dst, dst, r.local.at[15], recv_sem, sib).wait_recv()

    slice_rows = pl.ds(pick(z * 2 + core, 16), 16)
    columns_of = lambda peer: pl.ds(pick(peer, 128), 128)

    def small_to(k):
        return remote(
            r.small, r.small_all.at[:, columns_of(s)], r.sm_s.at[k], r.sm_r.at[k], (c, lax.rem(s + k, 8))
        )

    def wq_to(k, t):
        peer = lax.rem(s + k, 8)
        cols = pl.ds(pick(t * 4 + peer // 2, 256), 256)
        return remote(
            r.w_qkv.at[slice_rows, cols],
            r.wq_all.at[s, slice_rows, t * 256 : t * 256 + 256],
            r.wq_s.at[3 * k + t],
            r.wq_r.at[3 * k + t],
            (c, peer),
        )

    def tok_to(k):
        peer = 2 * lax.rem(x + k, 4) + yl
        return remote(r.tok, r.tok_all.at[x], r.tk_s.at[k], r.tk_r.at[k], (c, peer))

    loop(8, lambda k: small_to(k).start(), 1)

    def wq_start(k):
        for t in range(3):
            wq_to(k, t).start()

    loop(8, wq_start, 1)
    tok_to(1).start()
    tok_to(3).start()
    tok_to(2).start()
    own = [
        pltpu.make_async_copy(
            r.w_qkv.at[slice_rows, pl.ds(pick(t * 4 + x, 256), 256)],
            r.wq_all.at[s, slice_rows, t * 256 : t * 256 + 256],
            r.local.at[t],
        )
        for t in range(3)
    ]
    for copy in own:
        copy.start()
    r.small_all[:, columns_of(s)] = r.small[...]
    r.tok_all[x] = r.tok[...]

    sub = lax.broadcasted_iota(jnp.int32, (64, 128), 0)

    def set_places(k):
        pair = r.block_pairs[k]
        block = jnp.where(sub < 32, pair, 31 - pair)
        r.places[pl.ds(pick(k, 64), 64), :] = (block * 32 + lax.rem(sub, 32)).astype(F32)

    loop(16, set_places)

    for copy in own:
        copy.wait()

    def wq_arrived(k):
        origin = lax.rem(s - k + 8, 8)
        for t in range(3):
            await_block(r.wq_all.at[origin, slice_rows, t * 256 : t * 256 + 256], r.wq_r.at[3 * k + t])

    loop(8, wq_arrived, 1)

    def slice_of(zp, core_of):
        return r.wq_all.at[:, pl.ds(pick(zp * 2 + core_of, 16), 16)]

    def wq_along(k):
        block = slice_of(z, core)
        return remote(block, block, r.wz_s.at[k], r.wz_r.at[k], (lax.rem(c + 4 * k, 16), s))

    def wq_across(k):
        block = slice_of(lax.rem(z - k + 4, 4), core)
        return remote(block, block, r.wc_s.at[k], r.wc_r.at[k], sib)

    wq_along(1).start()
    wq_along(3).start()
    wq_along(2).start()
    wq_across(0).start()
    loop(
        8,
        lambda k: await_block(r.small_all.at[:, columns_of(lax.rem(s - k + 8, 8))], r.sm_r.at[k]),
        1,
    )
    for k in (1, 3, 2):
        await_block(slice_of(lax.rem(z - k + 4, 4), core), r.wz_r.at[k])
        wq_across(k).start()

    half = lambda which, rows: pl.ds(pick(which, rows), rows)

    def wo_to(k):
        peer = lax.rem(s + k, 8)
        return remote(
            r.w_out.at[half(core, 64)], r.wo_all.at[s, half(core, 64)], r.wo_s.at[k], r.wo_r.at[k], (c, peer)
        )

    def cot_to(k):
        peer = 2 * lax.rem(x + k, 4) + yl
        return remote(r.cot, r.cot_all.at[x], r.ct_s.at[k], r.ct_r.at[k], (c, peer))

    def w1_to(k):
        peer = lax.rem(s + k, 8)
        return remote(
            r.w_fc1.at[half(core, 64), pl.ds(pick(peer // 2, 1024), 1024)],
            r.w1_all.at[s, half(core, 64)],
            r.w1_s.at[k],
            r.w1_r.at[k],
            (c, peer),
        )

    def w2_to():
        mate = (c, s + 1 - 2 * yl)
        rows = half(core, 256)
        return remote(r.w_fc2.at[rows], r.w2_all.at[yl, rows], r.w2_s.at[0], r.w2_r.at[0], mate)

    own = [
        pltpu.make_async_copy(r.w_out, r.wo_all.at[s], r.local.at[4]),
        pltpu.make_async_copy(r.w_fc1.at[:, pl.ds(pick(x, 1024), 1024)], r.w1_all.at[s], r.local.at[5]),
        pltpu.make_async_copy(r.w_fc2, r.w2_all.at[yl], r.local.at[6]),
        pltpu.make_async_copy(r.cot, r.cot_all.at[x], r.local.at[7]),
    ]

    gain_one, bias_one = r.small_all[0:1, :], r.small_all[1:2, :]
    head_cols = pl.ds(pick(x, 256), 256)
    bias_qkv = (r.small_all[2:3, head_cols], None, r.small_all[3:4, head_cols])

    def parts_to(target):
        return remote(
            r.qkv.at[target], r.parts.at[c], r.qa_s.at[target], r.qa_r.at[c], (target, s)
        )

    def qkv_block(k):
        hop = k + (k // 2) * (1 - 2 * lax.rem(k, 2))
        origin = lax.rem(x - hop + 4, 4)

        @pl.when(k > 0)
        def _():
            await_block(r.tok_all.at[origin], r.tk_r.at[hop])

        normed, _ = norm_rows(r.tok_all[origin].astype(F32))
        r.attn_all[origin] = (normed * gain_one + bias_one).astype(BF16)

        @pl.when(k == 0)
        def _():
            for j in range(4):
                await_block(slice_of(lax.rem(z - j + 4, 4), 1 - core), r.wc_r.at[j])

        for t in range(3):
            cols = slice(t * 256, t * 256 + 256)
            acc = dot(r.attn_all[origin], r.wq_all[:, :, cols].reshape(1024, 256))
            if bias_qkv[t] is not None:
                acc = acc + bias_qkv[t]
            acc = acc.astype(BF16)
            for j in range(2):
                for p in range(2):
                    r.qkv[origin * 4 + j * 2 + p, :, t * 128 : t * 128 + 128] = acc[
                        j * 64 : j * 64 + 64, p * 128 : p * 128 + 128
                    ]

        for j in range(4):
            target = origin * 4 + j
            not_when(target == c, lambda: parts_to(target).start())

    loop(4, qkv_block)
    loop(8, lambda k: wo_to(k).start(), 1)
    for k in (1, 3, 2):
        cot_to(k).start()
    for copy in own:
        copy.start()
    r.parts[c] = r.qkv[c]
    loop(16, lambda k: await_block(r.parts.at[lax.rem(c + k, 16)], r.qa_r.at[lax.rem(c + k, 16)]), 1)
    w2_to().start()
    loop(8, lambda k: w1_to(k).start(), 1)

    slot_lane = lax.rem(c // 2, 2)
    row = r.small_all[12:13, columns_of(2 * (c // 4) + yl)]
    lane = lax.broadcasted_iota(jnp.int32, (1, 128), 1)
    length = jnp.sum(jnp.where(lane == slot_lane, row, 0.0), axis=1, keepdims=True)
    head_lane = lax.broadcasted_iota(jnp.int32, (1, 128), 1) // 64
    value_t = r.parts[:, :, 256:384].reshape(1024, 128).T

    def attend(i):
        keys = r.parts[:, :, 128:256].reshape(1024, 128)
        key_place = r.places[:, 0:1]
        query_place = r.places[pl.ds(pick(i, 256), 256), :].T[0:1, :]
        allowed = (key_place < length) & (key_place <= query_place)
        queries = r.parts[pl.ds(i * 4, 4), :, 0:128].reshape(256, 128) * jnp.asarray(0.125, BF16)
        cols = pl.ds(pick(i, 256), 256)
        for h in range(2):
            mine = jnp.where(head_lane == h, queries, jnp.zeros_like(queries))
            scores = jnp.where(allowed, dot_nt(keys, mine), negative)
            powers = jnp.exp(scores - jnp.max(scores, axis=0, keepdims=True))
            low = (powers * (1.0 / jnp.sum(powers, axis=0, keepdims=True))).astype(BF16)
            r.probs[h, :, cols] = low
            r.mix_t[h * 64 : h * 64 + 64, cols] = dot(value_t[h * 64 : h * 64 + 64], low)

    loop(4, attend)
    r.mixed[...] = r.mix_t[...].T.astype(BF16).reshape(16, 64, 128)

    def mix_to(k):
        peer = lax.rem(c + k, 16)
        return remote(
            r.mixed.at[peer],
            r.mix_rows.at[yh, :, head_columns(x, core)],
            r.mx_s.at[k],
            r.mx_r.at[x * 4 + yh * 2 + core],
            (peer, 2 * z + yl),
        )

    loop(16, lambda k: mix_to(k).start(), 1)
    not_when(at_home, lambda: mix_to(0).start())

    @pl.when(at_home)
    def _():
        r.mix_rows[yh, :, head_columns(x, core)] = r.mixed[c]

    def across(whole, recv, send_next, recv_next, rows):
        def body(k):
            block = whole.at[lax.rem(s - k + 8, 8), half(core, rows)]
            await_block(block, recv.at[k])
            remote(block, block, send_next.at[k], recv_next.at[k], sib).start()

        return body

    loop(8, across(r.wo_all, r.wo_r, r.woc_s, r.woc_r, 64), 1)
    loop(
        8,
        lambda k: await_block(r.wo_all.at[lax.rem(s - k + 8, 8), half(1 - core, 64)], r.woc_r.at[k]),
        1,
    )
    own[0].wait()

    def mix_arrived(k):
        xo, yo, ko = k // 4, lax.rem(k // 2, 2), lax.rem(k, 2)
        here = at_home & (xo == x) & (yo == yh) & (ko == core)
        not_when(here, lambda: await_block(r.mix_rows.at[yo, :, head_columns(xo, ko)], r.mx_r.at[k]))

    loop(16, mix_arrived)

    mix = r.mix_rows[...].reshape(128, 1024)
    hidden = r.tok[...].astype(F32) + (dot(mix, r.wo_all[...].reshape(1024, 1024)) + r.small_all[4:5, :])
    r.hidden[...] = hidden
    normed, _ = norm_rows(hidden)
    r.mlp_all[x] = (normed * r.small_all[5:6, :] + r.small_all[6:7, :]).astype(BF16)

    def mlp_to(k):
        peer = 2 * lax.rem(x + k, 4) + yl
        return remote(r.mlp_all.at[x], r.mlp_all.at[x], r.ml_s.at[k], r.ml_r.at[k], (c, peer))

    for k in (1, 3, 2):
        mlp_to(k).start()
    loop(8, across(r.w1_all, r.w1_r, r.w1c_s, r.w1c_r, 64), 1)
    block = r.w2_all.at[1 - yl, half(core, 256)]
    await_block(block, r.w2_r.at[0])
    w2_across = remote(block, block, r.w2c_s.at[0], r.w2c_r.at[0], sib)
    w2_across.start()
    for copy in own[1:]:
        copy.wait()
    loop(
        8,
        lambda k: await_block(r.w1_all.at[lax.rem(s - k + 8, 8), half(1 - core, 64)], r.w1c_r.at[k]),
        1,
    )
    await_block(r.w2_all.at[1 - yl, half(1 - core, 256)], r.w2c_r.at[0])

    r.up[...] = jnp.zeros_like(r.up)
    row_lane = lax.broadcasted_iota(jnp.int32, (1, 128), 1)
    upper = lax.broadcasted_iota(jnp.int32, (128, 1), 0) < 64

    def valid_of(origin):
        row = r.small_all[12:13, columns_of(2 * origin + yl)]
        lens = [jnp.sum(jnp.where(row_lane == j, row, 0.0), axis=1, keepdims=True) for j in range(2)]
        mine = r.places[pl.ds(pick(c, 64), 64), 0:1]
        return (jnp.concatenate([mine, mine], axis=0) < jnp.where(upper, lens[0], lens[1])).astype(F32)

    def part_to(out, into, sems, k):
        peer = lax.rem(x + k, 4)
        return remote(out.at[peer], into.at[k], sems[0].at[k], sems[1].at[k], (c, 2 * peer + yl))

    gm_sems, mo_sems, ga_sems = (r.gm_s, r.gm_r), (r.mo_s, r.mo_r), (r.ga_s, r.ga_r)

    def mlp_block(k):
        hop = k + (k // 2) * (1 - 2 * lax.rem(k, 2))
        origin = lax.rem(x - hop + 4, 4)

        @pl.when(k > 0)
        def _():
            await_block(r.mlp_all.at[origin], r.ml_r.at[hop])
            await_block(r.cot_all.at[origin], r.ct_r.at[hop])

        r.cot_all[origin] = (r.cot_all[origin].astype(F32) * valid_of(origin)).astype(BF16)
        for i in range(4):
            cols = slice(i * 256, i * 256 + 256)
            bias = jnp.concatenate(
                [
                    r.small_all[8 + (2 * i + a) % 4 : 9 + (2 * i + a) % 4, columns_of(2 * x + i // 2)]
                    for a in range(2)
                ],
                axis=1,
            )
            pre = dot(r.mlp_all[origin], r.w1_all[:, :, cols].reshape(1024, 256)) + bias
            spread = 0.5 * (1.0 + lax.erf(pre * 0.7071067811865476))
            r.act_all[origin, :, cols] = (pre * spread).astype(BF16)
            slope = spread + pre * (0.3989422804014327 * jnp.exp(-0.5 * pre * pre))
            grad = dot_nt(r.cot_all[origin], r.w2_all[i // 2, (i % 2) * 256 : (i % 2) * 256 + 256]) * slope
            r.up[:, cols] += jnp.sum(grad, axis=0, keepdims=True)
            r.gp_all[origin, :, cols] = grad.astype(BF16)
        for i in range(4):
            cols = slice(i * 256, i * 256 + 256)
            part = dot_nt(r.gp_all[origin], r.w1_all[2 * i : 2 * i + 2].reshape(256, 1024))
            r.gm_out[origin, :, cols] = part.astype(BF16)

            @pl.when(k == 0)
            def _():
                r.gm_own[:, cols] = part

        @pl.when(k > 0)
        def _():
            part_to(r.gm_out, r.gm_in, gm_sems, 4 - hop).start()

        for i in range(4):
            cols = slice(i * 256, i * 256 + 256)
            part = dot(r.act_all[origin], r.w2_all[:, :, cols].reshape(1024, 256))
            r.mo_out[origin, :, cols] = part.astype(BF16)

            @pl.when(k == 0)
            def _():
                r.mo_own[:, cols] = part

    loop(4, mlp_block)
    for k in (1, 3, 2):
        part_to(r.mo_out, r.mo_in, mo_sems, k).start()

    def outer(left, right, into, width):
        def body(i):
            rows = pl.ds(pick(i, 256), 256)
            part = dot_tn(left[:, :, rows].reshape(512, 256), right[...].reshape(512, width))
            into[pl.ds(2 * i, 2)] = part.astype(BF16).reshape(2, 2, 64, width)

        loop(4, body)

    def near_to(which, grad, near):
        return remote(grad.at[:, 1 - core], near, r.ns_s.at[which], r.ns_r.at[which], sib)

    def far_to(k, near, far, sems):
        peer = lax.rem(c // 2 + k, 8)
        return remote(near.at[peer], far.at[k], sems[0].at[k], sems[1].at[k], (2 * peer + core, s))

    def pair_sum(which, grad, near, far, sems):
        await_block(near, r.ns_r.at[which])

        def add(j):
            near[j] = (near[j].astype(F32) + grad[j, core].astype(F32)).astype(BF16)

        loop(8, add)
        loop(8, lambda k: far_to(k, near, far, sems).start(), 1)

    def far_sum(near, far, sems, total):
        loop(8, lambda k: await_block(far.at[k], sems[1].at[k]), 1)

        def add(j):
            rows = pl.ds(pick(j, 16), 16)
            acc = near[c // 2, rows].astype(F32)
            for k in range(1, 8):
                acc = acc + far[k, rows].astype(F32)
            total[rows] = acc

        loop(4, add)

    two = (r.n_two, r.f_two, (r.two_s, r.two_r))
    one = (r.n_one, r.f_one, (r.one_s, r.one_r))
    out = (r.n_out, r.f_out, (r.out_s, r.out_r))
    qk = (r.n_qkv, r.f_qkv, (r.qk_s, r.qk_r))

    outer(r.act_all, r.cot_all, r.g_two, 1024)
    near_to(0, r.g_two, r.n_two).start()
    outer(r.mlp_all, r.gp_all, r.g_one, 1024)
    near_to(1, r.g_one, r.n_one).start()

    total = r.gm_own[...]
    for k in (1, 3, 2):
        await_block(r.gm_in.at[k], r.gm_r.at[k])
        total = total + r.gm_in[k].astype(F32)
    normed, inverse = norm_rows(r.hidden[...])
    grad_out = r.cot_all[x].astype(F32)
    grad_hidden = grad_out + norm_back(total, normed, inverse, r.small_all[5:6, :])
    r.grad_hidden[...] = grad_hidden
    r.hidden_low[...] = grad_hidden.astype(BF16)
    for i, rows in enumerate((grad_hidden, total * normed, total, grad_out)):
        r.vec[i : i + 1, :] = jnp.sum(rows, axis=0, keepdims=True)
    for i in range(4):
        part = dot_nt(r.hidden_low[...], r.wo_all[2 * i : 2 * i + 2].reshape(256, 1024))
        r.gmix[:, :, i * 256 : i * 256 + 256] = part.astype(BF16).reshape(2, 64, 256)

    def gmix_to(k):
        xo, yo, ko = k // 4, lax.rem(k // 2, 2), lax.rem(k, 2)
        return remote(
            r.gmix.at[yo, :, head_columns(xo, ko)],
            r.gmixed.at[c],
            r.mf_s.at[k],
            r.mf_r.at[c],
            (x * 4 + yo * 2 + ko, 2 * xo + yl),
        )

    def gmix_away(k):
        return at_home & (k // 4 == x) & (lax.rem(k // 2, 2) == yh) & (lax.rem(k, 2) == core)

    loop(16, lambda k: not_when(gmix_away(k), lambda: gmix_to(k).start()))

    @pl.when(at_home)
    def _():
        r.gmixed[c] = r.gmix[yh, :, head_columns(x, core)]

    def out_rows(i):
        rows = pl.ds(pick(i, 256), 256)
        part = dot_tn(r.mix_rows[:, :, rows].reshape(128, 256), r.hidden_low[...])
        r.g_out[pl.ds(2 * i, 2)] = part.astype(BF16).reshape(2, 2, 64, 1024)

    loop(4, out_rows)
    near_to(2, r.g_out, r.n_out).start()
    pair_sum(0, r.g_two, *two)
    pair_sum(1, r.g_one, *one)
    pair_sum(2, r.g_out, *out)

    loop(16, lambda k: await_block(r.gmixed.at[lax.rem(c + k, 16)], r.mf_r.at[lax.rem(c + k, 16)]), 1)
    not_when(at_home, lambda: await_block(r.gmixed.at[c], r.mf_r.at[c]))

    def masked(rows, h):
        return jnp.where(head_lane == h, rows, jnp.zeros_like(rows))

    def values_back(i):
        gm = r.gmixed[...].reshape(1024, 128)
        rows = pl.ds(pick(i, 256), 256)
        acc = dot(r.probs[0, rows], masked(gm, 0)) + dot(r.probs[1, rows], masked(gm, 1))
        r.gparts[pl.ds(i * 4, 4), :, 256:384] = acc.astype(BF16).reshape(4, 64, 128)
        return jnp.sum(acc, axis=0, keepdims=True)

    bias_v = lax.fori_loop(0, 4, lambda i, acc: acc + values_back(i), jnp.zeros((1, 128), F32))
    products = r.gmixed[...].reshape(1024, 128).astype(F32).T * r.mix_t[...]
    for h in range(2):
        r.delta[h : h + 1, :] = jnp.sum(products[h * 64 : h * 64 + 64], axis=0, keepdims=True)
    keys_t = r.parts[:, :, 128:256].reshape(1024, 128).T

    def scores_back(i):
        cols = pl.ds(pick(i, 256), 256)
        values = r.parts[:, :, 256:384].reshape(1024, 128)
        gm = r.gmixed[pl.ds(i * 4, 4)].reshape(256, 128)
        for h in range(2):
            grad = dot_nt(values, masked(gm, h)) - r.delta[h : h + 1, cols]
            low = (r.probs[h, :, cols].astype(F32) * grad).astype(BF16)
            r.probs[h, :, cols] = low
            r.gq_t[h * 64 : h * 64 + 64, cols] = dot(keys_t[h * 64 : h * 64 + 64], low)

    loop(4, scores_back)

    def keys_back(i):
        queries = r.parts[:, :, 0:128].reshape(1024, 128) * jnp.asarray(0.125, BF16)
        rows = pl.ds(pick(i, 256), 256)
        acc = dot(r.probs[0, rows], masked(queries, 0)) + dot(r.probs[1, rows], masked(queries, 1))
        r.gparts[pl.ds(i * 4, 4), :, 128:256] = acc.astype(BF16).reshape(4, 64, 128)

    loop(4, keys_back)
    gq = r.gq_t[...].T * 0.125
    r.gparts[:, :, 0:128] = gq.astype(BF16).reshape(16, 64, 128)

    def back_to(k):
        peer = lax.rem(c + k, 16)
        return remote(r.gparts.at[peer], r.gback.at[c], r.hb_s.at[k], r.hb_r.at[c], (peer, s))

    loop(16, lambda k: back_to(k).start(), 1)
    r.gback[c] = r.gparts[c]
    wide = lax.broadcasted_iota(jnp.int32, (1, 1024), 1) // 128 == 2 * x + core
    for i, sums in ((4, jnp.sum(gq, axis=0, keepdims=True)), (5, bias_v)):
        r.vec[i : i + 1, :] = jnp.where(wide, jnp.concatenate([sums] * 8, axis=1), 0.0)

    total = r.mo_own[...] + r.small_all[7:8, :]
    for k in (1, 3, 2):
        await_block(r.mo_in.at[k], r.mo_r.at[k])
        total = total + r.mo_in[k].astype(F32)
    r.layer_out[...] = (valid_of(x) * (r.hidden[...] + total)).astype(BF16)
    loop(16, lambda k: await_block(r.gback.at[lax.rem(c + k, 16)], r.hb_r.at[lax.rem(c + k, 16)]), 1)

    r.vec[6:8, :] = jnp.zeros((2, 1024), F32)

    def attn_back(k):
        hop = jnp.where(k == 0, 2, jnp.where(k == 1, 3, jnp.where(k == 2, 1, 0)))
        origin = lax.rem(x + hop, 4)
        for t in range(3):
            for j in range(2):
                for p in range(2):
                    r.gqkv[origin, j * 64 : j * 64 + 64, t * 256 + p * 128 : t * 256 + p * 128 + 128] = r.gback[
                        origin * 4 + j * 2 + p, :, t * 128 : t * 128 + 128
                    ]
        normed, _ = norm_rows(r.tok_all[origin].astype(F32))
        for i in range(4):
            cols = slice(i * 256, i * 256 + 256)
            part = dot_nt(r.gqkv[origin], r.wq_all[2 * i : 2 * i + 2].reshape(256, 768))
            r.ga_out[origin, :, cols] = part.astype(BF16)
            r.vec[6:7, cols] += jnp.sum(part * normed[:, cols], axis=0, keepdims=True)
            r.vec[7:8, cols] += jnp.sum(part, axis=0, keepdims=True)

            @pl.when(k == 3)
            def _():
                r.ga_own[:, cols] = part

        @pl.when(k < 3)
        def _():
            part_to(r.ga_out, r.ga_in, ga_sems, hop).start()

    loop(4, attn_back)
    vec_across = remote(r.vec, r.vec_sib, r.ns_s.at[4], r.ns_r.at[4], sib)
    up_across = remote(r.up, r.up_sib, r.ns_s.at[5], r.ns_r.at[5], sib)
    vec_across.start()
    up_across.start()
    outer(r.attn_all, r.gqkv, r.g_qkv, 768)
    near_to(3, r.g_qkv, r.n_qkv).start()
    await_block(r.vec_sib, r.ns_r.at[4])
    await_block(r.up_sib, r.ns_r.at[5])
    vec_across.wait_send()
    up_across.wait_send()
    r.vec[...] += r.vec_sib[...]
    r.up[...] += r.up_sib[...]
    chip = c // 2

    def vec_to(k):
        peer = lax.rem(chip + k, 8)
        return remote(r.vec.at[:, columns_of(peer)], r.vec_in.at[k], r.v1_s.at[k], r.v1_r.at[k], (2 * peer + core, s))

    def up_to(k):
        peer = lax.rem(chip + k, 8)
        return remote(r.up, r.up_in.at[k], r.u1_s.at[k], r.u1_r.at[k], (2 * peer + core, s))

    loop(8, lambda k: vec_to(k).start(), 1)
    loop(8, lambda k: up_to(k).start(), 1)
    pair_sum(3, r.g_qkv, *qk)

    def rows_to(k, total, into, sems):
        peer = lax.rem(s + k, 8)
        rows = pl.ds(pick(peer, 8), 8)
        return remote(total.at[rows], into.at[s], sems[0].at[k], sems[1].at[k], (c, peer))

    def two_to(y):
        return remote(
            r.s_two.at[32 * y : 32 * y + 32],
            r.r_two.at[yl],
            r.t_two_s.at[y],
            r.t_two_r.at[yl],
            (to_c, 2 * to_x + y),
        )

    my_rows = pl.ds(pick(s, 8), 8)
    one_set = (r.s_one, r.r_one, (r.t_one_s, r.t_one_r))
    out_set = (r.s_out, r.r_out, (r.t_out_s, r.t_out_r))
    qk_set = (r.s_qkv, r.r_qkv, (r.t_qk_s, r.t_qk_r))

    def spread_rows(total, into, sems):
        loop(8, lambda k: rows_to(k, total, into, sems).start(), 1)
        into[s] = total[my_rows]

    far_sum(*two, r.s_two)
    for y in range(2):
        not_when(stays & (yl == y), lambda: two_to(y).start())

    @pl.when(stays)
    def _():
        r.r_two[yl] = r.s_two[pl.ds(pick(yl, 32), 32)]

    far_sum(*one, r.s_one)
    spread_rows(*one_set)
    far_sum(*out, r.s_out)
    spread_rows(*out_set)

    loop(8, lambda k: await_block(r.vec_in.at[k], r.v1_r.at[k]), 1)
    loop(8, lambda k: await_block(r.up_in.at[k], r.u1_r.at[k]), 1)
    sums = r.vec[:, columns_of(chip)]
    up_sums = r.up[...]
    for k in range(1, 8):
        sums = sums + r.vec_in[k]
        up_sums = up_sums + r.up_in[k]
    r.vec_sum[...] = sums
    r.up_sum[...] = up_sums

    def vec_rows_to(k):
        return remote(r.vec_sum, r.vec_all.at[s], r.v2_s.at[k], r.v2_r.at[k], (c, lax.rem(s + k, 8)))

    def up_rows_to(k):
        return remote(r.up_sum, r.up_all.at[s], r.u2_s.at[k], r.u2_r.at[k], (c, lax.rem(s + k, 8)))

    loop(8, lambda k: vec_rows_to(k).start(), 1)
    loop(8, lambda k: up_rows_to(k).start(), 1)
    r.vec_all[s] = sums
    r.up_all[s] = up_sums

    total = r.ga_own[...]
    for k in (1, 3, 2):
        await_block(r.ga_in.at[k], r.ga_r.at[k])
        total = total + r.ga_in[k].astype(F32)
    normed, inverse = norm_rows(r.tok[...].astype(F32))
    r.input_grad[...] = (
        r.grad_hidden[...] + norm_back(total, normed, inverse, r.small_all[0:1, :])
    ).astype(BF16)

    far_sum(*qk, r.s_qkv)
    spread_rows(*qk_set)

    def rows_arrived(into, sems):
        loop(8, lambda k: await_block(into.at[lax.rem(s - k + 8, 8)], sems[1].at[k]), 1)

    for y in range(2):
        not_when(stays & (yl == y), lambda: await_block(r.r_two.at[y], r.t_two_r.at[y]))
    r.o_two[...] = r.r_two[0] + r.r_two[1]
    rows_arrived(r.r_one, one_set[2])
    for i in range(4):
        r.o_one[:, i * 1024 : i * 1024 + 1024] = r.r_one[2 * i] + r.r_one[2 * i + 1]
    rows_arrived(r.r_out, out_set[2])
    total = r.r_out[0]
    for i in range(1, 8):
        total = total + r.r_out[i]
    r.o_out[...] = total
    rows_arrived(r.vec_all, (r.v2_s, r.v2_r))
    rows_arrived(r.up_all, (r.u2_s, r.u2_r))
    total = r.vec_all[0]
    for i in range(1, 8):
        total = total + r.vec_all[i]
    r.o_vec[...] = total
    up_sums = r.up_all[2 * z] + r.up_all[2 * z + 1]
    r.up_sum_own[...] = up_sums
    r.o_up[...] = r.up_sum_own[:, columns_of(2 * low + s // 4)]
    rows_arrived(r.r_qkv, qk_set[2])
    for i in range(4):
        total = r.r_qkv[2 * i] + r.r_qkv[2 * i + 1]
        for t in range(3):
            r.o_qkv[:, t * 1024 + i * 256 : t * 1024 + i * 256 + 256] = total[:, t * 256 : t * 256 + 256]

    def sent(k):
        small_to(k).wait_send()
        for t in range(3):
            wq_to(k, t).wait_send()
        wo_to(k).wait_send()
        w1_to(k).wait_send()
        for whole, sem in ((r.wo_all, r.woc_s), (r.w1_all, r.w1c_s)):
            block = whole.at[lax.rem(s - k + 8, 8), half(core, 64)]
            remote(block, block, sem.at[k], sem.at[k], sib).wait_send()
        for group in (two, one, out, qk):
            far_to(k, *group).wait_send()
        for group in (one_set, out_set, qk_set):
            rows_to(k, *group).wait_send()
        vec_to(k).wait_send()
        up_to(k).wait_send()
        vec_rows_to(k).wait_send()
        up_rows_to(k).wait_send()

    loop(8, sent, 1)
    for k in range(1, 4):
        tok_to(k).wait_send()
        wq_along(k).wait_send()
        cot_to(k).wait_send()
        mlp_to(k).wait_send()
        part_to(r.gm_out, r.gm_in, gm_sems, k).wait_send()
        part_to(r.mo_out, r.mo_in, mo_sems, k).wait_send()
        part_to(r.ga_out, r.ga_in, ga_sems, k).wait_send()
    for k in range(4):
        wq_across(k).wait_send()
    near_to(0, r.g_two, r.n_two).wait_send()
    near_to(1, r.g_one, r.n_one).wait_send()
    near_to(2, r.g_out, r.n_out).wait_send()
    near_to(3, r.g_qkv, r.n_qkv).wait_send()
    w2_to().wait_send()
    w2_across.wait_send()
    loop(16, lambda k: not_when(k == c, lambda: parts_to(k).wait_send()))
    loop(16, lambda k: mix_to(k).wait_send(), 1)
    loop(16, lambda k: back_to(k).wait_send(), 1)
    loop(16, lambda k: not_when(gmix_away(k), lambda: gmix_to(k).wait_send()))
    not_when(at_home, lambda: mix_to(0).wait_send())
    for y in range(2):
        not_when(stays & (yl == y), lambda: two_to(y).wait_send())


def named_call(kernel, name, cid, ins, outs, scratch, operands):
    results = pl.pallas_call(
        kernel,
        name=name,
        out_shape=[jax.ShapeDtypeStruct(shape, dtype) for _, _, shape, dtype in outs],
        in_specs=[pl.BlockSpec(memory_space=space) for _, space in ins],
        out_specs=[pl.BlockSpec(memory_space=space) for _, space, _, _ in outs],
        scratch_shapes=[kind for _, kind in scratch],
        compiler_params=pltpu.CompilerParams(
            collective_id=cid, has_side_effects=True, vmem_limit_bytes=60 << 20
        ),
    )(*[operands[name] for name, _ in ins])
    return SimpleNamespace(**dict(zip([o[0] for o in outs], results, strict=True)))


def shards(
    tokens,
    lengths,
    block_pairs,
    ln1_gain,
    ln1_bias,
    w_qkv,
    query_bias,
    value_bias,
    w_out,
    out_bias,
    ln2_gain,
    ln2_bias,
    w_fc1,
    fc1_bias,
    w_fc2,
    fc2_bias,
    out_cotangent,
):
    c, s = lax.axis_index("ctx"), lax.axis_index("shard")
    f = named_call(
        layer_kernel,
        "layer",
        0,
        LAYER_IN,
        LAYER_OUT,
        LAYER_SCRATCH,
        dict(
            lengths=lengths,
            block_pairs=block_pairs,
            tok=tokens.reshape(128, 1024),
            ln1_gain=ln1_gain.reshape(1, 128),
            ln1_bias=ln1_bias.reshape(1, 128),
            query_bias=query_bias.reshape(1, 128),
            value_bias=value_bias.reshape(1, 128),
            out_bias=out_bias.reshape(1, 128),
            ln2_gain=ln2_gain.reshape(1, 128),
            ln2_bias=ln2_bias.reshape(1, 128),
            fc2_bias=fc2_bias.reshape(1, 128),
            fc1_bias=fc1_bias.reshape(4, 128),
            w_qkv=w_qkv,
            w_out=w_out,
            w_fc1=w_fc1,
            w_fc2=w_fc2,
            cot=out_cotangent.reshape(128, 1024),
        ),
    )
    mine = lax.dynamic_slice(f.o_vec, (0, (c % 2) * 64 + s * 8), (8, 8))
    up = lax.dynamic_slice_in_dim(f.o_up[0], (s % 4) * 32, 32)
    return (
        f.layer_out.reshape(tokens.shape),
        f.input_grad.reshape(tokens.shape),
        mine[6],
        mine[7],
        f.o_qkv,
        mine[4],
        mine[5],
        f.o_out,
        mine[0],
        mine[1],
        mine[2],
        f.o_one,
        up,
        f.o_two,
        mine[3],
    )


def solution(mesh):
    one, both = P("shard"), P(("ctx", "shard"))
    rows, both_rows = P("shard", None), P(("ctx", "shard"), None)
    whole = P("ctx", "shard", None, None)
    return jax.shard_map(
        shards,
        mesh=mesh,
        in_specs=(
            whole, one, P(), one, one, rows, one, one, rows, one, one, one, rows, one, rows, one, whole,
        ),
        out_specs=(
            whole, whole, both, both, both_rows, both, both, both_rows, both, both, both,
            both_rows, both, both_rows, both,
        ),
        check_vma=False,
    )
```

```python
from types import SimpleNamespace

import jax
import jax.numpy as jnp
from jax import lax
from jax.experimental import pallas as pl
from jax.experimental.pallas import tpu as pltpu
from jax.sharding import PartitionSpec as P

HEADS = 16
HEAD_DIM = 64
MESH = pl.DeviceIdType.MESH
ANY = pl.ANY
VMEM = pltpu.VMEM
F32 = jnp.float32
BF16 = jnp.bfloat16

eps_norm = 1e-05
negative = -1e30


def place():
    c, s = lax.axis_index("ctx"), lax.axis_index("shard")
    return c, s, lax.rem(c, 2), s // 2, lax.rem(s, 2)


def sibling(c):
    return c + 1 - 2 * lax.rem(c, 2)


def norm_back(grad_normed, normed, inverse, gain):
    scaled = grad_normed * gain
    centred = scaled - jnp.mean(scaled, axis=-1, keepdims=True)
    return inverse * (centred - normed * jnp.mean(scaled * normed, axis=-1, keepdims=True))


def dot(left, right):
    return jnp.dot(left, right, preferred_element_type=F32)


def dot_tn(left, right):
    return lax.dot_general(left, right, (((0,), (0,)), ((), ())), preferred_element_type=F32)


def pick(value, unit):
    return pl.multiple_of(value * unit, unit)


def loop(count, body, first=0):
    def step(k, carry):
        body(k)
        return carry

    lax.fori_loop(first, count, step, 0)


def remote(src, dst, send_sem, recv_sem, device):
    return pltpu.make_async_remote_copy(
        src_ref=src,
        dst_ref=dst,
        send_sem=send_sem,
        recv_sem=recv_sem,
        device_id=device,
        device_id_type=MESH,
    )


def not_when(condition, body):
    pl.when(jnp.logical_not(condition))(body)


def norm_rows(rows):
    centre = rows - jnp.mean(rows, axis=-1, keepdims=True)
    inverse = lax.rsqrt(jnp.mean(centre * centre, axis=-1, keepdims=True) + eps_norm)
    return centre * inverse, inverse


def dot_nt(left, right):
    return lax.dot_general(left, right, (((1,), (1,)), ((), ())), preferred_element_type=F32)


VECTORS = (
    "ln1_gain", "ln1_bias", "query_bias", "value_bias", "out_bias", "ln2_gain", "ln2_bias", "fc2_bias",
)

LAYER_IN = (
    ("lengths", pltpu.SMEM),
    ("block_pairs", pltpu.SMEM),
    ("tok", VMEM),
    *[(name, VMEM) for name in VECTORS],
    ("fc1_bias", VMEM),
    ("w_qkv", ANY),
    ("w_out", ANY),
    ("w_fc1", ANY),
    ("w_fc2", ANY),
    ("cot", ANY),
)

LAYER_OUT = (
    ("layer_out", VMEM, (128, 1024), BF16),
    ("input_grad", VMEM, (128, 1024), BF16),
    ("o_qkv", VMEM, (8, 3072), F32),
    ("o_out", VMEM, (8, 1024), F32),
    ("o_one", VMEM, (8, 4096), F32),
    ("o_two", VMEM, (32, 1024), F32),
    ("o_vec", VMEM, (16, 128), F32),
)

WEIGHTS = (("wq", 768), ("wo", 1024), ("w1", 1024), ("w2", 1024))
GRADS = (("two", 1024), ("one", 1024), ("out", 1024), ("qkv", 768))

LAYER_SCRATCH = (
    *[(name + "_all", pltpu.VMEM((8, 128, width), BF16)) for name, width in WEIGHTS],
    *[
        (prefix + name, pltpu.VMEM((*shape, width), BF16))
        for name, width in GRADS
        for prefix, shape in (
            ("g_", (8, 2, 64)), ("n_", (8, 64)), ("a_", (4, 4, 32)), ("b_", (4, 4, 32)), ("m_", (4, 32)), ("h_", (4, 32)),
        )
    ],
    *[("s_" + name, pltpu.VMEM((32, width), F32)) for name, width in GRADS],
    *[
        (name, pltpu.VMEM(shape, BF16))
        for name, shape in (
            ("tok_all", (4, 128, 1024)), ("attn_all", (4, 128, 1024)), ("cot_all", (4, 128, 1024)),
            ("qkv", (4, 4, 64, 384)), ("parts", (4, 4, 64, 384)),
            ("probs", (2, 1024, 1024)), ("mixed", (16, 64, 128)), ("mix_rows", (2, 64, 1024)),
            ("mlp_all", (4, 128, 1024)), ("act_all", (4, 128, 1024)), ("gp_all", (4, 128, 1024)),
            ("gm_out", (4, 128, 1024)), ("mo_out", (4, 128, 1024)), ("gm_in", (4, 128, 1024)),
            ("mo_in", (4, 128, 1024)), ("hidden_low", (128, 1024)), ("gmix", (2, 64, 1024)),
            ("gmixed", (16, 64, 128)), ("gparts", (4, 4, 64, 384)), ("gback", (4, 4, 64, 384)),
            ("gqkv", (4, 128, 768)), ("ga_out", (4, 128, 1024)), ("ga_in", (4, 128, 1024)),
        )
    ],
    *[
        (name, pltpu.VMEM(shape, F32))
        for name, shape in (
            ("small", (16, 128)), ("small_all", (16, 1024)), ("places", (1024, 128)), ("mix_t", (128, 1024)),
            ("hidden", (128, 1024)), ("gm_own", (128, 1024)), ("mo_own", (128, 1024)),
            ("grad_hidden", (128, 1024)), ("ga_own", (128, 1024)), ("gq_t", (128, 1024)), ("delta", (2, 1024)),
            ("r_two", (32, 1024)), ("r_one", (4, 8, 1024)), ("r_out", (4, 8, 1024)), ("r_qkv", (4, 8, 768)),
            ("vec", (16, 1024)), ("vec_sib", (16, 1024)), ("vec_in", (8, 16, 128)), ("vec_sum", (16, 128)),
            ("vec_all", (8, 16, 128)),
        )
    ],
    *[
        (prefix + name + end, pltpu.SemaphoreType.DMA((4,)))
        for name, _ in WEIGHTS
        for prefix in ("own_", "far_", "mate_")
        for end in ("_s", "_r")
    ],
    *[
        (prefix + name + end, pltpu.SemaphoreType.DMA((4,)))
        for name, _ in GRADS
        for prefix in ("first_", "second_", "last_")
        for end in ("_s", "_r")
    ],
    *[
        (name + end, pltpu.SemaphoreType.DMA((count,)))
        for name, count in (
            ("local", 16), ("sm", 8), ("tk", 4), ("qa", 16), ("mx", 16), ("ct", 4), ("ml", 4), ("gm", 4), ("mo", 4),
            ("mf", 16), ("hb", 16), ("ga", 4), ("ns", 8), ("v1", 8), ("v2", 8),
        )
        for end in ("_s", "_r")
    ],
)


def layer_kernel(*refs):
    names = [n[0] for n in LAYER_IN + LAYER_OUT + LAYER_SCRATCH]
    r = SimpleNamespace(**dict(zip(names, refs, strict=True)))
    ref = lambda *name: getattr(r, "".join(name))
    c, s, core, x, yl = place()
    z, yh, q4 = c // 4, lax.rem(c // 2, 2), lax.rem(c, 4)
    sib = (sibling(c), s)
    mate_s = s + 1 - 2 * yl
    half = lambda which: pl.ds(pick(which, 64), 64)

    pieces = [(r.w_qkv, r.wq_all, t * 1024 + z * 256, t * 256, 256) for t in range(3)]
    pieces += [(r.w_fc1, r.w1_all, t * 512 + z * 128, t * 128, 128) for t in range(8)]
    own = [
        pltpu.make_async_copy(
            weight.at[half(core), pl.ds(pl.multiple_of(source, 128), width)],
            whole.at[s, half(core), target : target + width],
            r.local_s.at[i],
        )
        for i, (weight, whole, source, target, width) in enumerate(pieces)
    ]
    own.append(pltpu.make_async_copy(r.w_out.at[half(core)], r.wo_all.at[s, half(core)], r.local_s.at[11]))
    own.append(
        pltpu.make_async_copy(r.w_fc2.at[half(2 * z + core)], r.w2_all.at[s, half(core)], r.local_s.at[12])
    )
    own.append(pltpu.make_async_copy(r.cot, r.cot_all.at[z], r.local_s.at[13]))
    for copy in own:
        copy.start()

    barrier = pltpu.get_barrier_semaphore()

    def hail(device):
        pl.semaphore_signal(barrier, inc=1, device_id=device, device_id_type=MESH)

    to_z, from_x, from_yl = 2 * yl + lax.rem(x, 2), x // 2 * 2 + lax.rem(z, 2), z // 2
    at_home = to_z == z
    two_to = (to_z * 4 + yh * 2 + z // 2, (lax.rem(z, 2) * 2 + core) * 2 + x // 2)
    two_from = (
        (core * 2 + x // 2) * 4 + yh * 2 + lax.rem(x, 2),
        (yl * 2 + lax.rem(z, 2)) * 2 + z // 2,
    )
    two_stays = (two_to[0] == c) & (two_to[1] == s)
    loop(8, lambda k: hail((c, lax.rem(s + k, 8))), 1)
    loop(16, lambda k: hail((lax.rem(c + k, 16), s)), 1)
    hail((c + 2 - 4 * yh, mate_s))
    loop(4, lambda k: not_when(at_home & (k == z), lambda: hail((k * 4 + q4, 2 * from_x + from_yl))))
    not_when(two_stays, lambda: hail(two_from))

    for i, name in enumerate(VECTORS):
        r.small[i : i + 1, :] = ref(name)[...].astype(F32)
    r.small[8:12, :] = r.fc1_bias[...].astype(F32)
    r.small[12:16, :] = jnp.zeros((4, 128), F32)
    for copy in own[:3]:
        copy.wait()
    pl.semaphore_wait(barrier, 28 - at_home.astype(jnp.int32) - two_stays.astype(jnp.int32))

    def await_block(dst, recv_sem):
        remote(dst, dst, r.local_s.at[15], recv_sem, sib).wait_recv()

    columns_of = lambda which: pl.ds(pick(which, 128), 128)
    z_peer = lambda k: (lax.rem(c + 4 * k, 16), s)
    x_peer = lambda k: (c, 2 * lax.rem(x + k, 4) + yl)

    def small_to(k):
        return remote(
            r.small, r.small_all.at[:, columns_of(s)], r.sm_s.at[k], r.sm_r.at[k], (c, lax.rem(s + k, 8))
        )

    def tok_to(k):
        return remote(r.tok, r.tok_all.at[z], r.tk_s.at[k], r.tk_r.at[k], z_peer(k))

    def cot_to(k):
        return remote(r.cot, r.cot_all.at[z], r.ct_s.at[k], r.ct_r.at[k], z_peer(k))

    def weight_copy(name, kind, k):
        whole = ref(name, "_all")
        device = (c, mate_s) if kind == "mate_" else x_peer(k)
        block = whole.at[mate_s if kind == "far_" else s, half(core)]
        if kind == "mate_" and k == 0:
            device, block = sib, whole.at[:, half(core)]
        return remote(block, block, ref(kind, name, "_s").at[k], ref(kind, name, "_r").at[k], device)

    def weight_own(name):
        weight_copy(name, "mate_", 1).start()
        for k in (1, 3, 2):
            weight_copy(name, "own_", k).start()

    def weight_far(name):
        await_block(ref(name, "_all").at[mate_s, half(core)], ref("mate_", name, "_r").at[1])
        for k in (1, 3, 2):
            weight_copy(name, "far_", k).start()

    def weight_across(name):
        for k in (1, 3, 2):
            origin = 2 * lax.rem(x - k + 4, 4)
            await_block(ref(name, "_all").at[origin + yl, half(core)], ref("own_", name, "_r").at[k])
            await_block(ref(name, "_all").at[origin + 1 - yl, half(core)], ref("far_", name, "_r").at[k])
        weight_copy(name, "mate_", 0).start()

    def weight_ready(name):
        await_block(ref(name, "_all").at[:, half(1 - core)], ref("mate_", name, "_r").at[0])

    weight_own("wq")
    loop(8, lambda k: small_to(k).start(), 1)
    for k in (1, 3, 2):
        tok_to(k).start()
    r.small_all[:, columns_of(s)] = r.small[...]
    r.tok_all[z] = r.tok[...]
    weight_far("wq")

    sub = lax.broadcasted_iota(jnp.int32, (64, 128), 0)

    def set_places(k):
        pair = r.block_pairs[k]
        block = jnp.where(sub < 32, pair, 31 - pair)
        r.places[pl.ds(pick(k, 64), 64), :] = (block * 32 + lax.rem(sub, 32)).astype(F32)

    loop(16, set_places)
    loop(
        8,
        lambda k: await_block(r.small_all.at[:, columns_of(lax.rem(s - k + 8, 8))], r.sm_r.at[k]),
        1,
    )
    weight_across("wq")
    for copy in own[3:]:
        copy.wait()
    weight_own("wo")

    gain_one, bias_one = r.small_all[0:1, :], r.small_all[1:2, :]
    head_cols = pl.ds(pick(z, 256), 256)
    bias_qkv = (r.small_all[2:3, head_cols], None, r.small_all[3:4, head_cols])

    def parts_to(m, origin):
        peer = lax.rem(q4 + m, 4)
        return remote(
            r.qkv.at[peer, origin],
            r.parts.at[origin, q4],
            r.qa_s.at[4 * m + origin],
            r.qa_r.at[4 * m + origin],
            (4 * z + peer, s),
        )

    def norm_block(origin):
        normed, _ = norm_rows(r.tok_all[origin].astype(F32))
        r.attn_all[origin] = (normed * gain_one + bias_one).astype(BF16)

    norm_block(z)
    weight_ready("wq")

    def hop_of(k):
        return k + (k // 2) * (1 - 2 * lax.rem(k, 2))

    def qkv_block(k):
        hop = hop_of(k)
        origin = lax.rem(z - hop + 4, 4)

        @pl.when(k > 0)
        def _():
            await_block(r.tok_all.at[origin], r.tk_r.at[hop])
            norm_block(origin)

        for t in range(3):
            cols = slice(t * 256, t * 256 + 256)
            acc = dot(r.attn_all[origin], r.wq_all[:, :, cols].reshape(1024, 256))
            if bias_qkv[t] is not None:
                acc = acc + bias_qkv[t]
            acc = acc.astype(BF16)
            for j in range(2):
                for p in range(2):
                    r.qkv[j * 2 + p, origin, :, t * 128 : t * 128 + 128] = acc[
                        j * 64 : j * 64 + 64, p * 128 : p * 128 + 128
                    ]
        for m in (1, 2, 3):
            parts_to(m, origin).start()
        r.parts[origin, q4] = r.qkv[q4, origin]

    loop(4, qkv_block)
    weight_far("wo")
    for k in (1, 3, 2):
        cot_to(k).start()
    weight_own("w1")

    def parts_arrived(k):
        m = 1 + k // 4
        origin = lax.rem(k, 4)
        await_block(r.parts.at[origin, lax.rem(q4 - m + 4, 4)], r.qa_r.at[4 * m + origin])

    loop(12, parts_arrived)
    weight_far("w1")
    weight_own("w2")

    length = jnp.where(yh == 0, r.lengths[0], r.lengths[1]).astype(F32)
    head_lane = lax.broadcasted_iota(jnp.int32, (1, 128), 1) // 64
    value_t = r.parts[:, :, :, 256:384].reshape(1024, 128).T

    def masked(rows, h):
        return jnp.where(head_lane == h, rows, jnp.zeros_like(rows))

    def attend(i):
        keys = r.parts[:, :, :, 128:256].reshape(1024, 128)
        key_place = r.places[:, 0:1]
        query_place = r.places[pl.ds(pick(i, 256), 256), :].T[0:1, :]
        allowed = (key_place < length) & (key_place <= query_place)
        queries = r.parts[i, :, :, 0:128].reshape(256, 128) * jnp.asarray(0.125, BF16)
        cols = pl.ds(pick(i, 256), 256)
        for h in range(2):
            scores = jnp.where(allowed, dot_nt(keys, masked(queries, h)), negative)
            powers = jnp.exp(scores - jnp.max(scores, axis=0, keepdims=True))
            low = (powers * (1.0 / jnp.sum(powers, axis=0, keepdims=True))).astype(BF16)
            r.probs[h, :, cols] = low
            r.mix_t[h * 64 : h * 64 + 64, cols] = dot(value_t[h * 64 : h * 64 + 64], low)

    loop(4, attend)
    r.mixed[...] = r.mix_t[...].T.astype(BF16).reshape(16, 64, 128)

    def pair_columns(which):
        return columns_of(which // 4 * 2 + lax.rem(which, 2))

    def slot_of(which):
        return lax.rem(which // 2, 2)

    def mix_to(k):
        peer = lax.rem(c + k, 16)
        return remote(
            r.mixed.at[peer], r.mix_rows.at[yh, :, pair_columns(c)], r.mx_s.at[k], r.mx_r.at[k], (peer, s)
        )

    loop(16, lambda k: mix_to(k).start(), 1)
    r.mix_rows[yh, :, pair_columns(c)] = r.mixed[c]
    weight_far("w2")
    weight_across("wo")
    weight_across("w1")
    weight_ready("wo")

    def mix_arrived(k):
        origin = lax.rem(c - k + 16, 16)
        await_block(r.mix_rows.at[slot_of(origin), :, pair_columns(origin)], r.mx_r.at[k])

    loop(16, mix_arrived, 1)

    mix = r.mix_rows[...].reshape(128, 1024)
    hidden = r.tok[...].astype(F32) + (dot(mix, r.wo_all[...].reshape(1024, 1024)) + r.small_all[4:5, :])
    r.hidden[...] = hidden
    normed, _ = norm_rows(hidden)
    r.mlp_all[z] = (normed * r.small_all[5:6, :] + r.small_all[6:7, :]).astype(BF16)

    def mlp_to(k):
        return remote(r.mlp_all.at[z], r.mlp_all.at[z], r.ml_s.at[k], r.ml_r.at[k], z_peer(k))

    for k in (1, 3, 2):
        mlp_to(k).start()
    weight_across("w2")
    weight_ready("w1")
    weight_ready("w2")

    r.vec[...] = jnp.zeros_like(r.vec)
    up_row = pl.ds(8 + z, 1)
    upper = lax.broadcasted_iota(jnp.int32, (128, 1), 0) < 64
    row_length = jnp.where(upper, r.lengths[0], r.lengths[1]).astype(F32)

    def valid_of(origin):
        mine = r.places[half(origin * 4 + q4), 0:1]
        return (jnp.concatenate([mine, mine], axis=0) < row_length).astype(F32)

    def part_to(out, into, sems, k):
        return remote(out.at[lax.rem(z + k, 4)], into.at[k], sems[0].at[k], sems[1].at[k], z_peer(k))

    gm_sems, mo_sems, ga_sems = (r.gm_s, r.gm_r), (r.mo_s, r.mo_r), (r.ga_s, r.ga_r)

    def mlp_block(k):
        hop = hop_of(k)
        origin = lax.rem(z - hop + 4, 4)

        @pl.when(k > 0)
        def _():
            await_block(r.mlp_all.at[origin], r.ml_r.at[hop])
            await_block(r.cot_all.at[origin], r.ct_r.at[hop])

        r.cot_all[origin] = (r.cot_all[origin].astype(F32) * valid_of(origin)).astype(BF16)
        for i in range(4):
            cols = slice(i * 256, i * 256 + 256)
            pre = dot(r.mlp_all[origin], r.w1_all[:, :, cols].reshape(1024, 256)) + r.small_all[up_row, cols]
            spread = 0.5 * (1.0 + lax.erf(pre * 0.7071067811865476))
            r.act_all[origin, :, cols] = (pre * spread).astype(BF16)
            slope = spread + pre * (0.3989422804014327 * jnp.exp(-0.5 * pre * pre))
            grad = dot_nt(r.cot_all[origin], r.w2_all[2 * i : 2 * i + 2].reshape(256, 1024)) * slope
            r.vec[up_row, cols] += jnp.sum(grad, axis=0, keepdims=True)
            r.gp_all[origin, :, cols] = grad.astype(BF16)
        for i in range(4):
            cols = slice(i * 256, i * 256 + 256)
            part = dot_nt(r.gp_all[origin], r.w1_all[2 * i : 2 * i + 2].reshape(256, 1024))
            r.gm_out[origin, :, cols] = part.astype(BF16)

            @pl.when(k == 0)
            def _():
                r.gm_own[:, cols] = part

        @pl.when(k > 0)
        def _():
            part_to(r.gm_out, r.gm_in, gm_sems, 4 - hop).start()

        for i in range(4):
            cols = slice(i * 256, i * 256 + 256)
            part = dot(r.act_all[origin], r.w2_all[:, :, cols].reshape(1024, 256))
            r.mo_out[origin, :, cols] = part.astype(BF16)

            @pl.when(k == 0)
            def _():
                r.mo_own[:, cols] = part

    loop(4, mlp_block)
    for k in (1, 3, 2):
        part_to(r.mo_out, r.mo_in, mo_sems, k).start()

    def outer(name, left, right, width):
        into = ref("g_", name)

        def body(i):
            rows = pl.ds(pick(i, 256), 256)
            part = dot_tn(left[:, :, rows].reshape(512, 256), right[...].reshape(512, width))
            into[pl.ds(2 * i, 2)] = part.astype(BF16).reshape(2, 2, 64, width)

        loop(4, body)

    def near_to(which):
        name = GRADS[which][0]
        return remote(
            ref("g_", name).at[:, 1 - core], ref("n_", name), r.ns_s.at[which], r.ns_r.at[which], sib
        )

    def y_peer(k):
        yh_to, yl_to = (1 - yh if k // 2 else yh), (1 - yl if k % 2 else yl)
        return (c + 2 * (yh_to - yh), s + yl_to - yl), 2 * yh_to + yl_to

    here = {"x": x, "y": 2 * yh + yl}
    order = {"two": "xy", "one": "yx", "out": "xy", "qkv": "xy"}

    def peer_of(axis, k):
        return (x_peer(k), lax.rem(x + k, 4)) if axis == "x" else y_peer(k)

    def first_to(name, k):
        device, index = peer_of(order[name][0], k)
        sems = ref("first_", name, "_s"), ref("first_", name, "_r")
        return remote(ref("a_", name).at[index], ref("b_", name).at[k], sems[0].at[k], sems[1].at[k], device)

    def second_to(name, k):
        device, index = peer_of(order[name][1], k)
        sems = ref("second_", name, "_s"), ref("second_", name, "_r")
        return remote(ref("m_", name).at[index], ref("h_", name).at[k], sems[0].at[k], sems[1].at[k], device)

    def pair_sum(which):
        name = GRADS[which][0]
        grad, near, into = ref("g_", name), ref("n_", name), ref("a_", name)
        await_block(near, r.ns_r.at[which])

        def add(j):
            y_to = lax.rem(j, 2) * 2 + j // 4
            for xh in range(2):
                x_to = 2 * xh + lax.rem(j // 2, 2)
                rows = slice(32 * xh, 32 * xh + 32)
                total = near[j, rows].astype(F32) + grad[j, core, rows].astype(F32)
                target = (x_to, y_to) if order[name] == "xy" else (y_to, x_to)
                into[target[0], target[1]] = total.astype(BF16)

        loop(8, add)
        for k in (1, 3, 2):
            first_to(name, k).start()

    def first_sum(name):
        mine, others, into = ref("a_", name), ref("b_", name), ref("m_", name)
        for k in (1, 3, 2):
            await_block(others.at[k], ref("first_", name, "_r").at[k])

        def add(j):
            total = mine[here[order[name][0]], j].astype(F32)
            for k in (1, 2, 3):
                total = total + others[k, j].astype(F32)
            into[j] = total.astype(BF16)

        loop(4, add)
        for k in (1, 3, 2):
            second_to(name, k).start()

    def second_sum(name):
        mine, others = ref("m_", name), ref("h_", name)
        for k in (1, 3, 2):
            await_block(others.at[k], ref("second_", name, "_r").at[k])
        total = mine[here[order[name][1]]].astype(F32)
        for k in (1, 2, 3):
            total = total + others[k].astype(F32)
        ref("s_", name)[...] = total

    outer("two", r.act_all, r.cot_all, 1024)
    near_to(0).start()
    outer("one", r.mlp_all, r.gp_all, 1024)
    near_to(1).start()

    total = r.gm_own[...]
    for k in (1, 3, 2):
        await_block(r.gm_in.at[k], r.gm_r.at[k])
        total = total + r.gm_in[k].astype(F32)
    normed, inverse = norm_rows(r.hidden[...])
    grad_out = r.cot_all[z].astype(F32)
    grad_hidden = grad_out + norm_back(total, normed, inverse, r.small_all[5:6, :])
    r.grad_hidden[...] = grad_hidden
    r.hidden_low[...] = grad_hidden.astype(BF16)
    for i, rows in enumerate((grad_hidden, total * normed, total, grad_out)):
        r.vec[i : i + 1, :] = jnp.sum(rows, axis=0, keepdims=True)
    for i in range(4):
        part = dot_nt(r.hidden_low[...], r.wo_all[2 * i : 2 * i + 2].reshape(256, 1024))
        r.gmix[:, :, i * 256 : i * 256 + 256] = part.astype(BF16).reshape(2, 64, 256)

    def gmix_to(k):
        peer = lax.rem(c + k, 16)
        return remote(
            r.gmix.at[slot_of(peer), :, pair_columns(peer)], r.gmixed.at[c], r.mf_s.at[k], r.mf_r.at[k], (peer, s)
        )

    loop(16, lambda k: gmix_to(k).start(), 1)
    r.gmixed[c] = r.gmix[yh, :, pair_columns(c)]

    def out_rows(i):
        rows = pl.ds(pick(i, 256), 256)
        part = dot_tn(r.mix_rows[:, :, rows].reshape(128, 256), r.hidden_low[...])
        r.g_out[pl.ds(2 * i, 2)] = part.astype(BF16).reshape(2, 2, 64, 1024)

    pair_sum(0)
    pair_sum(1)
    loop(4, out_rows)
    near_to(2).start()
    loop(16, lambda k: await_block(r.gmixed.at[lax.rem(c - k + 16, 16)], r.mf_r.at[k]), 1)

    def back_to(m, piece):
        peer = lax.rem(q4 + m, 4)
        cols = slice(256, 384) if piece else slice(0, 256)
        return remote(
            r.gparts.at[:, peer, :, cols],
            r.gback.at[q4, :, :, cols],
            r.hb_s.at[4 * piece + m],
            r.hb_r.at[4 * piece + m],
            (4 * z + peer, s),
        )

    def values_back(i):
        gm = r.gmixed[...].reshape(1024, 128)
        rows = pl.ds(pick(i, 256), 256)
        acc = dot(r.probs[0, rows], masked(gm, 0)) + dot(r.probs[1, rows], masked(gm, 1))
        r.gparts[i, :, :, 256:384] = acc.astype(BF16).reshape(4, 64, 128)
        return jnp.sum(acc, axis=0, keepdims=True)

    bias_v = lax.fori_loop(0, 4, lambda i, acc: acc + values_back(i), jnp.zeros((1, 128), F32))
    for m in (1, 2, 3):
        back_to(m, 1).start()
    products = r.gmixed[...].reshape(1024, 128).astype(F32).T * r.mix_t[...]
    for h in range(2):
        r.delta[h : h + 1, :] = jnp.sum(products[h * 64 : h * 64 + 64], axis=0, keepdims=True)
    keys_t = r.parts[:, :, :, 128:256].reshape(1024, 128).T

    def scores_back(i):
        cols = pl.ds(pick(i, 256), 256)
        values = r.parts[:, :, :, 256:384].reshape(1024, 128)
        gm = r.gmixed[pl.ds(i * 4, 4)].reshape(256, 128)
        for h in range(2):
            grad = dot_nt(values, masked(gm, h)) - r.delta[h : h + 1, cols]
            low = (r.probs[h, :, cols].astype(F32) * grad).astype(BF16)
            r.probs[h, :, cols] = low
            r.gq_t[h * 64 : h * 64 + 64, cols] = dot(keys_t[h * 64 : h * 64 + 64], low)

    loop(4, scores_back)

    def keys_back(i):
        queries = r.parts[:, :, :, 0:128].reshape(1024, 128) * jnp.asarray(0.125, BF16)
        rows = pl.ds(pick(i, 256), 256)
        acc = dot(r.probs[0, rows], masked(queries, 0)) + dot(r.probs[1, rows], masked(queries, 1))
        r.gparts[i, :, :, 128:256] = acc.astype(BF16).reshape(4, 64, 128)

    loop(4, keys_back)
    gq = r.gq_t[...].T * 0.125
    r.gparts[:, :, :, 0:128] = gq.astype(BF16).reshape(4, 4, 64, 128)
    for m in (1, 2, 3):
        back_to(m, 0).start()
    r.gback[q4] = r.gparts[:, q4]
    wide = lax.broadcasted_iota(jnp.int32, (1, 1024), 1) // 128 == 2 * z + core
    for i, sums in ((4, jnp.sum(gq, axis=0, keepdims=True)), (5, bias_v)):
        r.vec[i : i + 1, :] = jnp.where(wide, jnp.concatenate([sums] * 8, axis=1), 0.0)

    pair_sum(2)
    first_sum("two")
    first_sum("one")
    total = r.mo_own[...] + r.small_all[7:8, :]
    for k in (1, 3, 2):
        await_block(r.mo_in.at[k], r.mo_r.at[k])
        total = total + r.mo_in[k].astype(F32)
    r.layer_out[...] = (valid_of(z) * (r.hidden[...] + total)).astype(BF16)
    for m in (1, 2, 3):
        for piece, cols in ((1, slice(256, 384)), (0, slice(0, 256))):
            await_block(r.gback.at[lax.rem(q4 - m + 4, 4), :, :, cols], r.hb_r.at[4 * piece + m])

    def attn_back(k):
        hop = jnp.where(k == 0, 2, jnp.where(k == 1, 3, jnp.where(k == 2, 1, 0)))
        origin = lax.rem(z + hop, 4)
        for t in range(3):
            for j in range(2):
                for p in range(2):
                    r.gqkv[origin, j * 64 : j * 64 + 64, t * 256 + p * 128 : t * 256 + p * 128 + 128] = r.gback[
                        j * 2 + p, origin, :, t * 128 : t * 128 + 128
                    ]
        normed, _ = norm_rows(r.tok_all[origin].astype(F32))
        for i in range(4):
            cols = slice(i * 256, i * 256 + 256)
            part = dot_nt(r.gqkv[origin], r.wq_all[2 * i : 2 * i + 2].reshape(256, 768))
            r.ga_out[origin, :, cols] = part.astype(BF16)
            r.vec[6:7, cols] += jnp.sum(part * normed[:, cols], axis=0, keepdims=True)
            r.vec[7:8, cols] += jnp.sum(part, axis=0, keepdims=True)

            @pl.when(k == 3)
            def _():
                r.ga_own[:, cols] = part

        @pl.when(k < 3)
        def _():
            part_to(r.ga_out, r.ga_in, ga_sems, hop).start()

    loop(4, attn_back)
    vec_across = remote(r.vec, r.vec_sib, r.ns_s.at[4], r.ns_r.at[4], sib)
    vec_across.start()
    outer("qkv", r.attn_all, r.gqkv, 768)
    near_to(3).start()
    await_block(r.vec_sib, r.ns_r.at[4])
    vec_across.wait_send()
    r.vec[...] += r.vec_sib[...]
    chip = c // 2

    def vec_to(k):
        peer = lax.rem(chip + k, 8)
        return remote(r.vec.at[:, columns_of(peer)], r.vec_in.at[k], r.v1_s.at[k], r.v1_r.at[k], (2 * peer + core, s))

    loop(8, lambda k: vec_to(k).start(), 1)
    pair_sum(3)

    my_part = pl.ds(pick(lax.rem(x, 2) * 2 + yl, 8), 8)

    def last_to(name, k):
        rows = slice(8 * k, 8 * k + 8)
        sems = ref("last_", name, "_s"), ref("last_", name, "_r")
        device = (to_z * 4 + q4, 2 * (x // 2 * 2 + k // 2) + k % 2)
        return remote(ref("s_", name).at[rows], ref("r_", name).at[z], sems[0].at[k], sems[1].at[z], device)

    def at_owner(k):
        return at_home & (lax.rem(x, 2) == k // 2) & (yl == k % 2)

    def spread(name):
        for k in range(4):
            not_when(at_owner(k), lambda: last_to(name, k).start())

        @pl.when(at_home)
        def _():
            ref("r_", name)[z] = ref("s_", name)[my_part]

    def two_copy():
        return remote(r.s_two, r.r_two, r.last_two_s.at[0], r.last_two_r.at[0], two_to)

    second_sum("two")
    not_when(two_stays, lambda: two_copy().start())

    @pl.when(two_stays)
    def _():
        r.r_two[...] = r.s_two[...]

    second_sum("one")
    spread("one")
    first_sum("out")

    loop(8, lambda k: await_block(r.vec_in.at[k], r.v1_r.at[k]), 1)
    sums = r.vec[:, columns_of(chip)]
    for k in range(1, 8):
        sums = sums + r.vec_in[k]
    r.vec_sum[...] = sums

    def vec_rows_to(k):
        return remote(r.vec_sum, r.vec_all.at[s], r.v2_s.at[k], r.v2_r.at[k], (c, lax.rem(s + k, 8)))

    loop(8, lambda k: vec_rows_to(k).start(), 1)
    r.vec_all[s] = sums
    first_sum("qkv")
    second_sum("out")
    spread("out")

    total = r.ga_own[...]
    for k in (1, 3, 2):
        await_block(r.ga_in.at[k], r.ga_r.at[k])
        total = total + r.ga_in[k].astype(F32)
    normed, inverse = norm_rows(r.tok[...].astype(F32))
    r.input_grad[...] = (
        r.grad_hidden[...] + norm_back(total, normed, inverse, r.small_all[0:1, :])
    ).astype(BF16)

    second_sum("qkv")
    spread("qkv")

    def rows_arrived(name):
        into = ref("r_", name)
        for k in range(4):
            not_when(at_home & (z == k), lambda: await_block(into.at[k], ref("last_", name, "_r").at[k]))

    not_when(two_stays, lambda: await_block(r.r_two, r.last_two_r.at[0]))
    r.o_two[...] = r.r_two[...]
    rows_arrived("one")
    for i in range(4):
        for t in range(8):
            r.o_one[:, t * 512 + i * 128 : t * 512 + i * 128 + 128] = r.r_one[i, :, t * 128 : t * 128 + 128]
    rows_arrived("out")
    r.o_out[...] = (r.r_out[0] + r.r_out[1]) + (r.r_out[2] + r.r_out[3])
    loop(8, lambda k: await_block(r.vec_all.at[lax.rem(s - k + 8, 8)], r.v2_r.at[k]), 1)
    total = r.vec_all[0]
    for i in range(1, 8):
        total = total + r.vec_all[i]
    r.o_vec[...] = total
    rows_arrived("qkv")
    for i in range(4):
        for t in range(3):
            r.o_qkv[:, t * 1024 + i * 256 : t * 1024 + i * 256 + 256] = r.r_qkv[i, :, t * 256 : t * 256 + 256]

    def sent(k):
        small_to(k).wait_send()
        vec_to(k).wait_send()
        vec_rows_to(k).wait_send()

    loop(8, sent, 1)
    for k in range(1, 4):
        for copy in (tok_to(k), cot_to(k), mlp_to(k)):
            copy.wait_send()
        part_to(r.gm_out, r.gm_in, gm_sems, k).wait_send()
        part_to(r.mo_out, r.mo_in, mo_sems, k).wait_send()
        part_to(r.ga_out, r.ga_in, ga_sems, k).wait_send()
        for name, _ in WEIGHTS:
            weight_copy(name, "own_", k).wait_send()
            weight_copy(name, "far_", k).wait_send()
        for name, _ in GRADS:
            first_to(name, k).wait_send()
            second_to(name, k).wait_send()
        for piece in range(2):
            back_to(k, piece).wait_send()
        for origin in range(4):
            parts_to(k, origin).wait_send()
    for name, _ in WEIGHTS:
        weight_copy(name, "mate_", 0).wait_send()
        weight_copy(name, "mate_", 1).wait_send()
    for which in range(4):
        near_to(which).wait_send()
    for name in ("one", "out", "qkv"):
        for k in range(4):
            not_when(at_owner(k), lambda: last_to(name, k).wait_send())
    not_when(two_stays, lambda: two_copy().wait_send())
    loop(16, lambda k: mix_to(k).wait_send(), 1)
    loop(16, lambda k: gmix_to(k).wait_send(), 1)


def named_call(kernel, name, cid, ins, outs, scratch, operands):
    results = pl.pallas_call(
        kernel,
        name=name,
        out_shape=[jax.ShapeDtypeStruct(shape, dtype) for _, _, shape, dtype in outs],
        in_specs=[pl.BlockSpec(memory_space=space) for _, space in ins],
        out_specs=[pl.BlockSpec(memory_space=space) for _, space, _, _ in outs],
        scratch_shapes=[kind for _, kind in scratch],
        compiler_params=pltpu.CompilerParams(
            collective_id=cid, has_side_effects=True, vmem_limit_bytes=60 << 20
        ),
    )(*[operands[name] for name, _ in ins])
    return SimpleNamespace(**dict(zip([o[0] for o in outs], results, strict=True)))


def shards(
    tokens,
    lengths,
    block_pairs,
    ln1_gain,
    ln1_bias,
    w_qkv,
    query_bias,
    value_bias,
    w_out,
    out_bias,
    ln2_gain,
    ln2_bias,
    w_fc1,
    fc1_bias,
    w_fc2,
    fc2_bias,
    out_cotangent,
):
    c, s = lax.axis_index("ctx"), lax.axis_index("shard")
    f = named_call(
        layer_kernel,
        "layer",
        0,
        LAYER_IN,
        LAYER_OUT,
        LAYER_SCRATCH,
        dict(
            lengths=lengths,
            block_pairs=block_pairs,
            tok=tokens.reshape(128, 1024),
            ln1_gain=ln1_gain.reshape(1, 128),
            ln1_bias=ln1_bias.reshape(1, 128),
            query_bias=query_bias.reshape(1, 128),
            value_bias=value_bias.reshape(1, 128),
            out_bias=out_bias.reshape(1, 128),
            ln2_gain=ln2_gain.reshape(1, 128),
            ln2_bias=ln2_bias.reshape(1, 128),
            fc2_bias=fc2_bias.reshape(1, 128),
            fc1_bias=fc1_bias.reshape(4, 128),
            w_qkv=w_qkv,
            w_out=w_out,
            w_fc1=w_fc1,
            w_fc2=w_fc2,
            cot=out_cotangent.reshape(128, 1024),
        ),
    )
    mine = lax.dynamic_slice(f.o_vec, (0, (c % 2) * 64 + s * 8), (8, 8))
    up = lax.dynamic_slice(f.o_vec, (8 + c % 2 * 2 + s // 4, (s % 4) * 32), (1, 32))[0]
    return (
        f.layer_out.reshape(tokens.shape),
        f.input_grad.reshape(tokens.shape),
        mine[6],
        mine[7],
        f.o_qkv,
        mine[4],
        mine[5],
        f.o_out,
        mine[0],
        mine[1],
        mine[2],
        f.o_one,
        up,
        f.o_two,
        mine[3],
    )


def solution(mesh):
    one, both = P("shard"), P(("ctx", "shard"))
    rows, both_rows = P("shard", None), P(("ctx", "shard"), None)
    whole = P("ctx", "shard", None, None)
    return jax.shard_map(
        shards,
        mesh=mesh,
        in_specs=(
            whole, one, P(), one, one, rows, one, one, rows, one, one, one, rows, one, rows, one, whole,
        ),
        out_specs=(
            whole, whole, both, both, both_rows, both, both, both_rows, both, both, both,
            both_rows, both, both_rows, both,
        ),
        check_vma=False,
    )
```

```python
from types import SimpleNamespace

import jax
import jax.numpy as jnp
from jax import lax
from jax.experimental import pallas as pl
from jax.experimental.pallas import tpu as pltpu
from jax.sharding import PartitionSpec as P

HEADS = 16
HEAD_DIM = 64
MESH = pl.DeviceIdType.MESH
ANY = pl.ANY
VMEM = pltpu.VMEM
F32 = jnp.float32
BF16 = jnp.bfloat16

eps_norm = 1e-05
negative = -1e30


def place():
    c, s = lax.axis_index("ctx"), lax.axis_index("shard")
    return c, s, lax.rem(c, 2), s // 2, lax.rem(s, 2)


def sibling(c):
    return c + 1 - 2 * lax.rem(c, 2)


def norm_back(grad_normed, normed, inverse, gain):
    scaled = grad_normed * gain
    centred = scaled - jnp.mean(scaled, axis=-1, keepdims=True)
    return inverse * (centred - normed * jnp.mean(scaled * normed, axis=-1, keepdims=True))


def dot(left, right):
    return jnp.dot(left, right, preferred_element_type=F32)


def dot_tn(left, right):
    return lax.dot_general(left, right, (((0,), (0,)), ((), ())), preferred_element_type=F32)


def pick(value, unit):
    return pl.multiple_of(value * unit, unit)


def loop(count, body, first=0):
    def step(k, carry):
        body(k)
        return carry

    lax.fori_loop(first, count, step, 0)


def remote(src, dst, send_sem, recv_sem, device):
    return pltpu.make_async_remote_copy(
        src_ref=src,
        dst_ref=dst,
        send_sem=send_sem,
        recv_sem=recv_sem,
        device_id=device,
        device_id_type=MESH,
    )


def not_when(condition, body):
    pl.when(jnp.logical_not(condition))(body)


def norm_rows(rows):
    centre = rows - jnp.mean(rows, axis=-1, keepdims=True)
    inverse = lax.rsqrt(jnp.mean(centre * centre, axis=-1, keepdims=True) + eps_norm)
    return centre * inverse, inverse


def dot_nt(left, right):
    return lax.dot_general(left, right, (((1,), (1,)), ((), ())), preferred_element_type=F32)


VECTORS = (
    "ln1_gain", "ln1_bias", "query_bias", "value_bias", "out_bias", "ln2_gain", "ln2_bias", "fc2_bias",
)

LAYER_IN = (
    ("lengths", pltpu.SMEM),
    ("block_pairs", pltpu.SMEM),
    ("tok", ANY),
    *[(name, VMEM) for name in VECTORS],
    ("fc1_bias", VMEM),
    ("w_qkv", ANY),
    ("w_out", ANY),
    ("w_fc1", ANY),
    ("w_fc2", ANY),
    ("cot", ANY),
)

LAYER_OUT = (
    ("layer_out", ANY, (128, 1024), BF16),
    ("input_grad", ANY, (128, 1024), BF16),
    ("o_qkv", ANY, (8, 3072), F32),
    ("o_out", ANY, (8, 1024), F32),
    ("o_one", ANY, (8, 4096), F32),
    ("o_two", ANY, (32, 1024), F32),
    ("o_vec", ANY, (16, 128), F32),
)

WEIGHTS = (("wq", 768), ("wo", 1024), ("w1", 1024), ("w2", 1024))
GRADS = (("two", 1024), ("one", 1024), ("out", 1024), ("qka", 384), ("qkb", 384))

LAYER_SCRATCH = (
    *[(name + "_all", pltpu.VMEM((8, 128, width), BF16)) for name, width in WEIGHTS],
    *[
        (prefix + name, pltpu.VMEM((*shape, width), BF16))
        for name, width in GRADS
        for prefix, shape in (
            ("g_", (8, 2, 64)), ("n_", (8, 64)), ("a_", (4, 4, 32)), ("b_", (4, 4, 32)), ("m_", (4, 32)), ("h_", (4, 32)),
        )
    ],
    *[("s_" + name, pltpu.VMEM((32, width), F32)) for name, width in GRADS],
    *[
        (name, pltpu.VMEM(shape, BF16))
        for name, shape in (
            ("tok_all", (4, 128, 1024)), ("attn_all", (4, 128, 1024)), ("cot_all", (4, 128, 1024)),
            ("qkv", (4, 4, 64, 384)), ("parts", (4, 4, 64, 384)),
            ("probs", (2, 1024, 1024)), ("mixed", (16, 64, 128)), ("mix_rows", (2, 64, 1024)),
            ("mlp_all", (4, 128, 1024)), ("act_all", (4, 128, 1024)), ("gp_all", (4, 128, 1024)),
            ("gm_out", (4, 128, 1024)), ("mo_out", (4, 128, 1024)), ("gm_in", (4, 128, 1024)),
            ("mo_in", (4, 128, 1024)), ("hidden_low", (128, 1024)), ("gmix", (2, 64, 1024)),
            ("gmixed", (16, 64, 128)), ("gparts", (4, 4, 64, 384)), ("gback", (4, 4, 64, 384)),
            ("gqkv", (4, 128, 768)), ("ga_out", (4, 128, 1024)), ("ga_in", (4, 128, 1024)), ("ga_via", (4, 64, 1024)),
            ("w_layer", (128, 1024)), ("w_input", (128, 1024)),
        )
    ],
    *[
        (name, pltpu.VMEM(shape, F32))
        for name, shape in (
            ("small", (16, 128)), ("small_all", (16, 1024)), ("places", (1024, 128)), ("mix_t", (128, 1024)),
            ("hidden", (128, 1024)), ("gm_own", (128, 1024)), ("mo_own", (128, 1024)),
            ("grad_hidden", (128, 1024)), ("ga_own", (128, 1024)), ("gq_t", (128, 1024)), ("delta", (2, 1024)),
            ("r_two", (32, 1024)), ("r_one", (4, 8, 1024)), ("r_out", (4, 8, 1024)), ("r_qka", (4, 8, 384)),
            ("r_qkb", (4, 8, 384)), ("w_qkv_out", (8, 3072)), ("w_out_out", (8, 1024)), ("w_one_out", (8, 4096)),
            ("w_vec_out", (16, 128)),
            ("vec", (16, 1024)), ("vec_sib", (16, 1024)), ("vec_in", (8, 16, 128)), ("vec_sum", (16, 128)),
            ("vec_all", (8, 16, 128)),
        )
    ],
    *[
        (prefix + name + end, pltpu.SemaphoreType.DMA((4,)))
        for name, _ in WEIGHTS
        for prefix in ("own_", "far_", "mate_")
        for end in ("_s", "_r")
    ],
    *[
        (prefix + name + end, pltpu.SemaphoreType.DMA((4,)))
        for name, _ in GRADS
        for prefix in ("first_", "second_", "last_")
        for end in ("_s", "_r")
    ],
    *[
        (name + end, pltpu.SemaphoreType.DMA((count,)))
        for name, count in (
            ("local", 16), ("done", 8), ("sm", 8), ("tk", 4), ("tf", 4), ("qa", 16), ("mx", 16), ("ct", 4), ("ml", 4),
            ("mg", 4), ("gm", 4), ("mo", 4), ("mf", 16), ("hb", 48), ("ga", 4), ("gv", 4), ("ns", 8), ("v1", 8), ("v2", 8),
        )
        for end in ("_s", "_r")
    ],
)


def layer_kernel(*refs):
    names = [n[0] for n in LAYER_IN + LAYER_OUT + LAYER_SCRATCH]
    r = SimpleNamespace(**dict(zip(names, refs, strict=True)))
    ref = lambda *name: getattr(r, "".join(name))
    c, s, core, x, yl = place()
    z, yh, q4 = c // 4, lax.rem(c // 2, 2), lax.rem(c, 4)
    sib = (sibling(c), s)
    mate_s = s + 1 - 2 * yl
    half = lambda which: pl.ds(pick(which, 64), 64)

    pieces = [(r.w_qkv, r.wq_all, t * 1024 + z * 256, t * 256, 256) for t in range(3)]
    pieces += [(r.w_fc1, r.w1_all, t * 512 + z * 128, t * 128, 128) for t in range(8)]
    own = [
        pltpu.make_async_copy(
            weight.at[half(core), pl.ds(pl.multiple_of(source, 128), width)],
            whole.at[s, half(core), target : target + width],
            r.local_s.at[i],
        )
        for i, (weight, whole, source, target, width) in enumerate(pieces)
    ]
    own.append(pltpu.make_async_copy(r.w_out.at[half(core)], r.wo_all.at[s, half(core)], r.local_s.at[11]))
    own.append(
        pltpu.make_async_copy(r.w_fc2.at[half(2 * z + core)], r.w2_all.at[s, half(core)], r.local_s.at[12])
    )
    own.append(pltpu.make_async_copy(r.cot, r.cot_all.at[z], r.local_s.at[13]))
    own.append(pltpu.make_async_copy(r.tok, r.tok_all.at[z], r.local_s.at[14]))

    barrier = pltpu.get_barrier_semaphore()

    def hail(device):
        pl.semaphore_signal(barrier, inc=1, device_id=device, device_id_type=MESH)

    to_z, from_x, from_yl = 2 * yl + lax.rem(x, 2), x // 2 * 2 + lax.rem(z, 2), z // 2
    at_home = to_z == z
    two_to = (to_z * 4 + yh * 2 + z // 2, (lax.rem(z, 2) * 2 + core) * 2 + x // 2)
    two_from = (
        (core * 2 + x // 2) * 4 + yh * 2 + lax.rem(x, 2),
        (yl * 2 + lax.rem(z, 2)) * 2 + z // 2,
    )
    two_stays = (two_to[0] == c) & (two_to[1] == s)
    loop(8, lambda k: hail((c, lax.rem(s + k, 8))), 1)
    loop(16, lambda k: hail((lax.rem(c + k, 16), s)), 1)
    hail((c + 2 - 4 * yh, mate_s))
    loop(4, lambda k: not_when(at_home & (k == z), lambda: hail((k * 4 + q4, 2 * from_x + from_yl))))
    not_when(two_stays, lambda: hail(two_from))
    for copy in own:
        copy.start()

    for i, name in enumerate(VECTORS):
        r.small[i : i + 1, :] = ref(name)[...].astype(F32)
    r.small[8:12, :] = r.fc1_bias[...].astype(F32)
    r.small[12:16, :] = jnp.zeros((4, 128), F32)
    for copy in own[:3]:
        copy.wait()
    pl.semaphore_wait(barrier, 28 - at_home.astype(jnp.int32) - two_stays.astype(jnp.int32))

    def await_block(dst, recv_sem):
        remote(dst, dst, r.local_s.at[15], recv_sem, sib).wait_recv()

    columns_of = lambda which: pl.ds(pick(which, 128), 128)
    z_peer = lambda k: (lax.rem(c + 4 * k, 16), s)
    x_peer = lambda k: (c, 2 * lax.rem(x + k, 4) + yl)

    def small_to(k):
        return remote(
            r.small, r.small_all.at[:, columns_of(s)], r.sm_s.at[k], r.sm_r.at[k], (c, lax.rem(s + k, 8))
        )

    def tok_to(k):
        return remote(r.tok, r.tok_all.at[z], r.tk_s.at[k], r.tk_r.at[k], z_peer(k))

    def cot_to(k):
        return remote(r.cot, r.cot_all.at[z], r.ct_s.at[k], r.ct_r.at[k], z_peer(k))

    z_of = lambda hop: lax.rem(z - hop + 4, 4)

    def pass_on(whole, send_sems, recv_sems, k):
        rows = slice(0, 64) if k == 1 else slice(64, 128)
        block = whole.at[z_of(k), rows]
        return remote(block, block, send_sems.at[k], recv_sems.at[k], z_peer(k))

    def ring_arrived(whole, recv_sems, send_next, recv_next, k):
        @pl.when(k == 1)
        def _():
            for j in (1, 3):
                await_block(whole.at[z_of(j)], recv_sems.at[j])
                pass_on(whole, send_next, recv_next, j).start()

        @pl.when(k == 3)
        def _():
            for j, rows in ((1, slice(0, 64)), (3, slice(64, 128))):
                await_block(whole.at[z_of(2), rows], recv_next.at[j])

    def weight_copy(name, kind, k):
        whole = ref(name, "_all")
        device = (c, mate_s) if kind == "mate_" else x_peer(k)
        block = whole.at[mate_s if kind == "far_" else s, half(core)]
        if kind == "mate_" and k == 0:
            device, block = sib, whole.at[:, half(core)]
        return remote(block, block, ref(kind, name, "_s").at[k], ref(kind, name, "_r").at[k], device)

    def weight_own(name):
        weight_copy(name, "mate_", 1).start()
        for k in (1, 3, 2):
            weight_copy(name, "own_", k).start()

    def weight_far(name):
        await_block(ref(name, "_all").at[mate_s, half(core)], ref("mate_", name, "_r").at[1])
        for k in (1, 3, 2):
            weight_copy(name, "far_", k).start()

    def weight_across(name):
        for k in (1, 3, 2):
            origin = 2 * lax.rem(x - k + 4, 4)
            await_block(ref(name, "_all").at[origin + yl, half(core)], ref("own_", name, "_r").at[k])
            await_block(ref(name, "_all").at[origin + 1 - yl, half(core)], ref("far_", name, "_r").at[k])
        weight_copy(name, "mate_", 0).start()

    def weight_ready(name):
        await_block(ref(name, "_all").at[:, half(1 - core)], ref("mate_", name, "_r").at[0])

    for k in (1, 3):
        tok_to(k).start()
    weight_own("wq")
    loop(8, lambda k: small_to(k).start(), 1)
    r.small_all[:, columns_of(s)] = r.small[...]
    weight_far("wq")

    sub = lax.broadcasted_iota(jnp.int32, (64, 128), 0)

    def set_places(k):
        pair = r.block_pairs[k]
        block = jnp.where(sub < 32, pair, 31 - pair)
        r.places[pl.ds(pick(k, 64), 64), :] = (block * 32 + lax.rem(sub, 32)).astype(F32)

    loop(16, set_places)
    loop(
        8,
        lambda k: await_block(r.small_all.at[:, columns_of(lax.rem(s - k + 8, 8))], r.sm_r.at[k]),
        1,
    )
    weight_across("wq")
    for copy in own[3:14]:
        copy.wait()
    weight_own("wo")

    gain_one, bias_one = r.small_all[0:1, :], r.small_all[1:2, :]
    head_cols = pl.ds(pick(z, 256), 256)
    bias_qkv = (r.small_all[2:3, head_cols], None, r.small_all[3:4, head_cols])

    def parts_to(m, origin):
        peer = lax.rem(q4 + m, 4)
        return remote(
            r.qkv.at[peer, origin],
            r.parts.at[origin, q4],
            r.qa_s.at[4 * m + origin],
            r.qa_r.at[4 * m + origin],
            (4 * z + peer, s),
        )

    def norm_block(origin):
        normed, _ = norm_rows(r.tok_all[origin].astype(F32))
        r.attn_all[origin] = (normed * gain_one + bias_one).astype(BF16)

    own[14].wait()
    norm_block(z)
    weight_ready("wq")

    def hop_of(k):
        return k + (k // 2) * (1 - 2 * lax.rem(k, 2))

    def qkv_block(k):
        hop = hop_of(k)
        origin = z_of(hop)
        ring_arrived(r.tok_all, r.tk_r, r.tf_s, r.tf_r, k)

        @pl.when(k > 0)
        def _():
            norm_block(origin)

        for t in range(3):
            cols = slice(t * 256, t * 256 + 256)
            acc = dot(r.attn_all[origin], r.wq_all[:, :, cols].reshape(1024, 256))
            if bias_qkv[t] is not None:
                acc = acc + bias_qkv[t]
            acc = acc.astype(BF16)
            for j in range(2):
                for p in range(2):
                    r.qkv[j * 2 + p, origin, :, t * 128 : t * 128 + 128] = acc[
                        j * 64 : j * 64 + 64, p * 128 : p * 128 + 128
                    ]
        for m in (1, 2, 3):
            parts_to(m, origin).start()
        r.parts[origin, q4] = r.qkv[q4, origin]

    loop(4, qkv_block)
    weight_far("wo")
    for k in (1, 3, 2):
        cot_to(k).start()
    weight_own("w1")

    def parts_arrived(k):
        m = 1 + k // 4
        origin = lax.rem(k, 4)
        await_block(r.parts.at[origin, lax.rem(q4 - m + 4, 4)], r.qa_r.at[4 * m + origin])

    loop(12, parts_arrived)
    weight_far("w1")
    weight_own("w2")

    length = jnp.where(yh == 0, r.lengths[0], r.lengths[1]).astype(F32)
    head_lane = lax.broadcasted_iota(jnp.int32, (1, 128), 1) // 64
    value_t = r.parts[:, :, :, 256:384].reshape(1024, 128).T

    def masked(rows, h):
        return jnp.where(head_lane == h, rows, jnp.zeros_like(rows))

    def pair_columns(which):
        return columns_of(which // 4 * 2 + lax.rem(which, 2))

    def slot_of(which):
        return lax.rem(which // 2, 2)

    def mix_to(peer):
        return remote(
            r.mixed.at[peer], r.mix_rows.at[yh, :, pair_columns(c)], r.mx_s.at[peer], r.mx_r.at[c], (peer, s)
        )

    def attend(k):
        i = lax.rem(z + k + 1, 4)
        keys = r.parts[:, :, :, 128:256].reshape(1024, 128)
        key_place = r.places[:, 0:1]
        query_place = r.places[pl.ds(pick(i, 256), 256), :].T[0:1, :]
        allowed = (key_place < length) & (key_place <= query_place)
        queries = r.parts[i, :, :, 0:128].reshape(256, 128) * jnp.asarray(0.125, BF16)
        cols = pl.ds(pick(i, 256), 256)
        for h in range(2):
            scores = jnp.where(allowed, dot_nt(keys, masked(queries, h)), negative)
            powers = jnp.exp(scores - jnp.max(scores, axis=0, keepdims=True))
            low = (powers * (1.0 / jnp.sum(powers, axis=0, keepdims=True))).astype(BF16)
            r.probs[h, :, cols] = low
            r.mix_t[h * 64 : h * 64 + 64, cols] = dot(value_t[h * 64 : h * 64 + 64], low)
        r.mixed[pl.ds(4 * i, 4)] = r.mix_t[:, cols].T.astype(BF16).reshape(4, 64, 128)
        for q in range(4):
            not_when(4 * i + q == c, lambda: mix_to(4 * i + q).start())

    loop(4, attend)

    r.mix_rows[yh, :, pair_columns(c)] = r.mixed[c]
    weight_far("w2")
    weight_across("wo")
    weight_across("w1")
    weight_ready("wo")

    def mix_arrived(k):
        origin = lax.rem(c - k + 16, 16)
        await_block(r.mix_rows.at[slot_of(origin), :, pair_columns(origin)], r.mx_r.at[origin])

    loop(16, mix_arrived, 1)

    mix = r.mix_rows[...].reshape(128, 1024)
    hidden = r.tok_all[z].astype(F32) + (dot(mix, r.wo_all[...].reshape(1024, 1024)) + r.small_all[4:5, :])
    r.hidden[...] = hidden
    normed, _ = norm_rows(hidden)
    r.mlp_all[z] = (normed * r.small_all[5:6, :] + r.small_all[6:7, :]).astype(BF16)

    def mlp_to(k):
        return remote(r.mlp_all.at[z], r.mlp_all.at[z], r.ml_s.at[k], r.ml_r.at[k], z_peer(k))

    for k in (1, 3):
        mlp_to(k).start()
    weight_across("w2")
    weight_ready("w1")
    weight_ready("w2")

    r.vec[...] = jnp.zeros_like(r.vec)
    up_row = pl.ds(8 + z, 1)
    upper = lax.broadcasted_iota(jnp.int32, (128, 1), 0) < 64
    row_length = jnp.where(upper, r.lengths[0], r.lengths[1]).astype(F32)

    def valid_of(origin):
        mine = r.places[half(origin * 4 + q4), 0:1]
        return (jnp.concatenate([mine, mine], axis=0) < row_length).astype(F32)

    def part_to(out, into, sems, k):
        return remote(out.at[lax.rem(z + k, 4)], into.at[k], sems[0].at[k], sems[1].at[k], z_peer(k))

    gm_sems, mo_sems, ga_sems = (r.gm_s, r.gm_r), (r.mo_s, r.mo_r), (r.ga_s, r.ga_r)

    def mlp_block(k):
        hop = hop_of(k)
        origin = z_of(hop)
        ring_arrived(r.mlp_all, r.ml_r, r.mg_s, r.mg_r, k)

        @pl.when(k > 0)
        def _():
            await_block(r.cot_all.at[origin], r.ct_r.at[hop])

        r.cot_all[origin] = (r.cot_all[origin].astype(F32) * valid_of(origin)).astype(BF16)
        for i in range(4):
            cols = slice(i * 256, i * 256 + 256)
            pre = dot(r.mlp_all[origin], r.w1_all[:, :, cols].reshape(1024, 256)) + r.small_all[up_row, cols]
            spread = 0.5 * (1.0 + lax.erf(pre * 0.7071067811865476))
            r.act_all[origin, :, cols] = (pre * spread).astype(BF16)
            slope = spread + pre * (0.3989422804014327 * jnp.exp(-0.5 * pre * pre))
            grad = dot_nt(r.cot_all[origin], r.w2_all[2 * i : 2 * i + 2].reshape(256, 1024)) * slope
            r.vec[up_row, cols] += jnp.sum(grad, axis=0, keepdims=True)
            r.gp_all[origin, :, cols] = grad.astype(BF16)
        for i in range(4):
            cols = slice(i * 256, i * 256 + 256)
            part = dot_nt(r.gp_all[origin], r.w1_all[2 * i : 2 * i + 2].reshape(256, 1024))
            r.gm_out[origin, :, cols] = part.astype(BF16)

            @pl.when(k == 0)
            def _():
                r.gm_own[:, cols] = part

        @pl.when(k > 0)
        def _():
            part_to(r.gm_out, r.gm_in, gm_sems, 4 - hop).start()

    loop(4, mlp_block)

    def mlp_out(origin):
        for i in range(4):
            cols = slice(i * 256, i * 256 + 256)
            part = dot(r.act_all[origin], r.w2_all[:, :, cols].reshape(1024, 256))
            r.mo_out[origin, :, cols] = part.astype(BF16)

            @pl.when(origin == z)
            def _():
                r.mo_own[:, cols] = part

    def outer(name, left, right, width, first=0):
        into = ref("g_", name)

        def body(i):
            rows = pl.ds(pick(i, 256), 256)
            part = dot_tn(
                left[:, :, rows].reshape(512, 256), right[:, :, first : first + width].reshape(512, width)
            )
            into[pl.ds(2 * i, 2)] = part.astype(BF16).reshape(2, 2, 64, width)

        loop(4, body)

    def near_to(which):
        name = GRADS[which][0]
        return remote(
            ref("g_", name).at[:, 1 - core], ref("n_", name), r.ns_s.at[which], r.ns_r.at[which], sib
        )

    def y_peer(k):
        yh_to, yl_to = (1 - yh if k // 2 else yh), (1 - yl if k % 2 else yl)
        return (c + 2 * (yh_to - yh), s + yl_to - yl), 2 * yh_to + yl_to

    here = {"x": x, "y": 2 * yh + yl}
    order = {"two": "xy", "one": "yx", "out": "xy", "qka": "xy", "qkb": "yx"}

    def peer_of(axis, k):
        return (x_peer(k), lax.rem(x + k, 4)) if axis == "x" else y_peer(k)

    def first_to(name, k):
        device, index = peer_of(order[name][0], k)
        sems = ref("first_", name, "_s"), ref("first_", name, "_r")
        return remote(ref("a_", name).at[index], ref("b_", name).at[k], sems[0].at[k], sems[1].at[k], device)

    def second_to(name, k):
        device, index = peer_of(order[name][1], k)
        sems = ref("second_", name, "_s"), ref("second_", name, "_r")
        return remote(ref("m_", name).at[index], ref("h_", name).at[k], sems[0].at[k], sems[1].at[k], device)

    def pair_sum(which):
        name = GRADS[which][0]
        grad, near, into = ref("g_", name), ref("n_", name), ref("a_", name)
        await_block(near, r.ns_r.at[which])

        def add(j):
            y_to = lax.rem(j, 2) * 2 + j // 4
            for xh in range(2):
                x_to = 2 * xh + lax.rem(j // 2, 2)
                rows = slice(32 * xh, 32 * xh + 32)
                total = near[j, rows].astype(F32) + grad[j, core, rows].astype(F32)
                target = (x_to, y_to) if order[name] == "xy" else (y_to, x_to)
                into[target[0], target[1]] = total.astype(BF16)

        loop(8, add)
        for k in (1, 3, 2):
            first_to(name, k).start()

    def first_sum(name):
        mine, others, into = ref("a_", name), ref("b_", name), ref("m_", name)
        for k in (1, 3, 2):
            await_block(others.at[k], ref("first_", name, "_r").at[k])

        def add(j):
            total = mine[here[order[name][0]], j].astype(F32)
            for k in (1, 2, 3):
                total = total + others[k, j].astype(F32)
            into[j] = total.astype(BF16)

        loop(4, add)
        for k in (1, 3, 2):
            second_to(name, k).start()

    def second_sum(name):
        mine, others = ref("m_", name), ref("h_", name)
        for k in (1, 3, 2):
            await_block(others.at[k], ref("second_", name, "_r").at[k])
        total = mine[here[order[name][1]]].astype(F32)
        for k in (1, 2, 3):
            total = total + others[k].astype(F32)
        ref("s_", name)[...] = total

    outer("two", r.act_all, r.cot_all, 1024)
    near_to(0).start()
    outer("one", r.mlp_all, r.gp_all, 1024)
    near_to(1).start()
    loop(4, mlp_out)

    total = r.gm_own[...]
    for k in (1, 3, 2):
        await_block(r.gm_in.at[k], r.gm_r.at[k])
        total = total + r.gm_in[k].astype(F32)
    normed, inverse = norm_rows(r.hidden[...])
    grad_out = r.cot_all[z].astype(F32)
    grad_hidden = grad_out + norm_back(total, normed, inverse, r.small_all[5:6, :])
    r.grad_hidden[...] = grad_hidden
    r.hidden_low[...] = grad_hidden.astype(BF16)
    for i, rows in enumerate((grad_hidden, total * normed, total, grad_out)):
        r.vec[i : i + 1, :] = jnp.sum(rows, axis=0, keepdims=True)
    for i in range(4):
        part = dot_nt(r.hidden_low[...], r.wo_all[2 * i : 2 * i + 2].reshape(256, 1024))
        r.gmix[:, :, i * 256 : i * 256 + 256] = part.astype(BF16).reshape(2, 64, 256)

    def gmix_to(k):
        peer = lax.rem(c + k, 16)
        return remote(
            r.gmix.at[slot_of(peer), :, pair_columns(peer)], r.gmixed.at[c], r.mf_s.at[k], r.mf_r.at[k], (peer, s)
        )

    loop(16, lambda k: gmix_to(k).start(), 1)
    r.gmixed[c] = r.gmix[yh, :, pair_columns(c)]

    def out_rows(i):
        rows = pl.ds(pick(i, 256), 256)
        part = dot_tn(r.mix_rows[:, :, rows].reshape(128, 256), r.hidden_low[...])
        r.g_out[pl.ds(2 * i, 2)] = part.astype(BF16).reshape(2, 2, 64, 1024)

    pair_sum(0)
    pair_sum(1)
    loop(4, out_rows)
    near_to(2).start()
    loop(16, lambda k: await_block(r.gmixed.at[lax.rem(c - k + 16, 16)], r.mf_r.at[k]), 1)
    for k in (1, 3, 2):
        part_to(r.mo_out, r.mo_in, mo_sems, k).start()

    def back_to(m, piece, i):
        peer = lax.rem(q4 + m, 4)
        cols = slice(piece * 128, piece * 128 + 128)
        sem = 16 * piece + 4 * i + m
        return remote(
            r.gparts.at[i, peer, :, cols],
            r.gback.at[q4, i, :, cols],
            r.hb_s.at[sem],
            r.hb_r.at[sem],
            (4 * z + peer, s),
        )

    def back_start(piece, i):
        for m in (1, 2, 3):
            back_to(m, piece, i).start()

    def values_back(i):
        gm = r.gmixed[...].reshape(1024, 128)
        rows = pl.ds(pick(i, 256), 256)
        acc = dot(r.probs[0, rows], masked(gm, 0)) + dot(r.probs[1, rows], masked(gm, 1))
        r.gparts[i, :, :, 256:384] = acc.astype(BF16).reshape(4, 64, 128)
        back_start(2, i)
        return jnp.sum(acc, axis=0, keepdims=True)

    bias_v = lax.fori_loop(0, 4, lambda i, acc: acc + values_back(i), jnp.zeros((1, 128), F32))
    products = r.gmixed[...].reshape(1024, 128).astype(F32).T * r.mix_t[...]
    for h in range(2):
        r.delta[h : h + 1, :] = jnp.sum(products[h * 64 : h * 64 + 64], axis=0, keepdims=True)
    keys_t = r.parts[:, :, :, 128:256].reshape(1024, 128).T

    def scores_back(i):
        cols = pl.ds(pick(i, 256), 256)
        values = r.parts[:, :, :, 256:384].reshape(1024, 128)
        gm = r.gmixed[pl.ds(i * 4, 4)].reshape(256, 128)
        for h in range(2):
            grad = dot_nt(values, masked(gm, h)) - r.delta[h : h + 1, cols]
            low = (r.probs[h, :, cols].astype(F32) * grad).astype(BF16)
            r.probs[h, :, cols] = low
            r.gq_t[h * 64 : h * 64 + 64, cols] = dot(keys_t[h * 64 : h * 64 + 64], low)
        gq = r.gq_t[:, cols].T * 0.125
        r.gparts[i, :, :, 0:128] = gq.astype(BF16).reshape(4, 64, 128)
        back_start(0, i)
        return jnp.sum(gq, axis=0, keepdims=True)

    bias_q = lax.fori_loop(0, 4, lambda i, acc: acc + scores_back(i), jnp.zeros((1, 128), F32))

    def keys_back(i):
        queries = r.parts[:, :, :, 0:128].reshape(1024, 128) * jnp.asarray(0.125, BF16)
        rows = pl.ds(pick(i, 256), 256)
        acc = dot(r.probs[0, rows], masked(queries, 0)) + dot(r.probs[1, rows], masked(queries, 1))
        r.gparts[i, :, :, 128:256] = acc.astype(BF16).reshape(4, 64, 128)
        back_start(1, i)

    loop(4, keys_back)
    r.gback[q4] = r.gparts[:, q4]
    wide = lax.broadcasted_iota(jnp.int32, (1, 1024), 1) // 128 == 2 * z + core
    for i, sums in ((4, bias_q), (5, bias_v)):
        r.vec[i : i + 1, :] = jnp.where(wide, jnp.concatenate([sums] * 8, axis=1), 0.0)

    pair_sum(2)
    first_sum("two")
    first_sum("one")
    total = r.mo_own[...] + r.small_all[7:8, :]
    for k in (1, 3, 2):
        await_block(r.mo_in.at[k], r.mo_r.at[k])
        total = total + r.mo_in[k].astype(F32)
    r.w_layer[...] = (valid_of(z) * (r.hidden[...] + total)).astype(BF16)
    results = [pltpu.make_async_copy(r.w_layer, r.layer_out, r.done_s.at[0])]
    results[0].start()

    def back_arrived(i):
        for m in (1, 2, 3):
            for piece in (2, 0, 1):
                await_block(
                    r.gback.at[lax.rem(q4 - m + 4, 4), i, :, piece * 128 : piece * 128 + 128],
                    r.hb_r.at[16 * piece + 4 * i + m],
                )

    loop(4, back_arrived)

    def assemble(origin):
        for t in range(3):
            for j in range(2):
                for p in range(2):
                    r.gqkv[origin, j * 64 : j * 64 + 64, t * 256 + p * 128 : t * 256 + p * 128 + 128] = r.gback[
                        j * 2 + p, origin, :, t * 128 : t * 128 + 128
                    ]

    loop(4, assemble)

    def attn_back(hop):
        origin = lax.rem(z + hop, 4)
        normed, _ = norm_rows(r.tok_all[origin].astype(F32))
        for i in range(4):
            cols = slice(i * 256, i * 256 + 256)
            part = dot_nt(r.gqkv[origin], r.wq_all[2 * i : 2 * i + 2].reshape(256, 768))
            r.ga_out[origin, :, cols] = part.astype(BF16)
            r.vec[6:7, cols] += jnp.sum(part * normed[:, cols], axis=0, keepdims=True)
            r.vec[7:8, cols] += jnp.sum(part, axis=0, keepdims=True)

            @pl.when(hop == 0)
            def _():
                r.ga_own[:, cols] = part

    halves = {1: slice(0, 64), 3: slice(64, 128)}

    def via_to(k):
        return remote(
            r.ga_out.at[lax.rem(z + 2, 4), halves[k]], r.ga_via.at[k], r.gv_s.at[k], r.gv_r.at[k], z_peer(k)
        )

    def via_add(k):
        await_block(r.ga_via.at[k], r.gv_r.at[k])
        target = lax.rem(z + k, 4)
        total = r.ga_out[target, halves[k]].astype(F32) + r.ga_via[k].astype(F32)
        r.ga_out[target, halves[k]] = total.astype(BF16)
        part_to(r.ga_out, r.ga_in, ga_sems, k).start()

    attn_back(2)
    via_to(1).start()
    via_to(3).start()
    outer("qka", r.attn_all, r.gqkv, 384)
    near_to(3).start()
    outer("qkb", r.attn_all, r.gqkv, 384, 384)
    near_to(4).start()
    loop(2, lambda k: attn_back(1 + 2 * k))
    via_add(1)
    via_add(3)
    pair_sum(3)
    pair_sum(4)
    attn_back(0)
    vec_across = remote(r.vec, r.vec_sib, r.ns_s.at[5], r.ns_r.at[5], sib)
    vec_across.start()
    await_block(r.vec_sib, r.ns_r.at[5])
    vec_across.wait_send()
    r.vec[...] += r.vec_sib[...]
    chip = c // 2

    def vec_to(k):
        peer = lax.rem(chip + k, 8)
        return remote(r.vec.at[:, columns_of(peer)], r.vec_in.at[k], r.v1_s.at[k], r.v1_r.at[k], (2 * peer + core, s))

    loop(8, lambda k: vec_to(k).start(), 1)

    my_part = pl.ds(pick(lax.rem(x, 2) * 2 + yl, 8), 8)

    def last_to(name, k):
        rows = slice(8 * k, 8 * k + 8)
        sems = ref("last_", name, "_s"), ref("last_", name, "_r")
        device = (to_z * 4 + q4, 2 * (x // 2 * 2 + k // 2) + k % 2)
        return remote(ref("s_", name).at[rows], ref("r_", name).at[z], sems[0].at[k], sems[1].at[z], device)

    def at_owner(k):
        return at_home & (lax.rem(x, 2) == k // 2) & (yl == k % 2)

    def spread(name):
        for k in range(4):
            not_when(at_owner(k), lambda: last_to(name, k).start())

        @pl.when(at_home)
        def _():
            ref("r_", name)[z] = ref("s_", name)[my_part]

    def two_copy():
        return remote(r.s_two, r.r_two, r.last_two_s.at[0], r.last_two_r.at[0], two_to)

    def finish(which, source, target):
        results.append(pltpu.make_async_copy(source, target, r.done_s.at[which]))
        results[-1].start()

    second_sum("two")
    not_when(two_stays, lambda: two_copy().start())

    @pl.when(two_stays)
    def _():
        r.r_two[...] = r.s_two[...]

    second_sum("one")
    spread("one")
    first_sum("out")

    loop(8, lambda k: await_block(r.vec_in.at[k], r.v1_r.at[k]), 1)
    sums = r.vec[:, columns_of(chip)]
    for k in range(1, 8):
        sums = sums + r.vec_in[k]
    r.vec_sum[...] = sums

    def vec_rows_to(k):
        return remote(r.vec_sum, r.vec_all.at[s], r.v2_s.at[k], r.v2_r.at[k], (c, lax.rem(s + k, 8)))

    loop(8, lambda k: vec_rows_to(k).start(), 1)
    r.vec_all[s] = sums
    first_sum("qka")
    first_sum("qkb")
    second_sum("out")
    spread("out")

    total = r.ga_own[...]
    for k in (1, 3):
        await_block(r.ga_in.at[k], r.ga_r.at[k])
        total = total + r.ga_in[k].astype(F32)
    normed, inverse = norm_rows(r.tok_all[z].astype(F32))
    r.w_input[...] = (
        r.grad_hidden[...] + norm_back(total, normed, inverse, r.small_all[0:1, :])
    ).astype(BF16)
    finish(1, r.w_input, r.input_grad)

    second_sum("qka")
    spread("qka")
    second_sum("qkb")
    spread("qkb")

    def rows_arrived(name):
        into = ref("r_", name)
        for k in range(4):
            not_when(at_home & (z == k), lambda: await_block(into.at[k], ref("last_", name, "_r").at[k]))

    not_when(two_stays, lambda: await_block(r.r_two, r.last_two_r.at[0]))
    finish(2, r.r_two, r.o_two)
    rows_arrived("one")
    for i in range(4):
        for t in range(8):
            r.w_one_out[:, t * 512 + i * 128 : t * 512 + i * 128 + 128] = r.r_one[i, :, t * 128 : t * 128 + 128]
    finish(3, r.w_one_out, r.o_one)
    rows_arrived("out")
    r.w_out_out[...] = (r.r_out[0] + r.r_out[1]) + (r.r_out[2] + r.r_out[3])
    finish(4, r.w_out_out, r.o_out)
    loop(8, lambda k: await_block(r.vec_all.at[lax.rem(s - k + 8, 8)], r.v2_r.at[k]), 1)
    total = r.vec_all[0]
    for i in range(1, 8):
        total = total + r.vec_all[i]
    r.w_vec_out[...] = total
    finish(5, r.w_vec_out, r.o_vec)
    rows_arrived("qka")
    rows_arrived("qkb")
    for i in range(4):
        for t in range(6):
            source = r.r_qka if t < 3 else r.r_qkb
            column = t // 2 * 1024 + i * 256 + t % 2 * 128
            r.w_qkv_out[:, column : column + 128] = source[i, :, t % 3 * 128 : t % 3 * 128 + 128]
    finish(6, r.w_qkv_out, r.o_qkv)

    def sent(k):
        small_to(k).wait_send()
        vec_to(k).wait_send()
        vec_rows_to(k).wait_send()

    loop(8, sent, 1)
    for k in range(1, 4):
        cot_to(k).wait_send()
        if k != 2:
            tok_to(k).wait_send()
            mlp_to(k).wait_send()
            pass_on(r.tok_all, r.tf_s, r.tf_r, k).wait_send()
            pass_on(r.mlp_all, r.mg_s, r.mg_r, k).wait_send()
            part_to(r.ga_out, r.ga_in, ga_sems, k).wait_send()
            via_to(k).wait_send()
        part_to(r.gm_out, r.gm_in, gm_sems, k).wait_send()
        part_to(r.mo_out, r.mo_in, mo_sems, k).wait_send()
        for name, _ in WEIGHTS:
            weight_copy(name, "own_", k).wait_send()
            weight_copy(name, "far_", k).wait_send()
        for name, _ in GRADS:
            first_to(name, k).wait_send()
            second_to(name, k).wait_send()
        for piece in range(3):
            loop(4, lambda i: back_to(k, piece, i).wait_send())
        for origin in range(4):
            parts_to(k, origin).wait_send()
    for name, _ in WEIGHTS:
        weight_copy(name, "mate_", 0).wait_send()
        weight_copy(name, "mate_", 1).wait_send()
    for which in range(5):
        near_to(which).wait_send()
    for name in ("one", "out", "qka", "qkb"):
        for k in range(4):
            not_when(at_owner(k), lambda: last_to(name, k).wait_send())
    not_when(two_stays, lambda: two_copy().wait_send())
    loop(16, lambda k: mix_to(lax.rem(c + k, 16)).wait_send(), 1)
    loop(16, lambda k: gmix_to(k).wait_send(), 1)
    for copy in results:
        copy.wait()


PLAIN = ("layer_out", "input_grad", "o_qkv", "o_out", "o_one", "o_two")


def owner_kernel(*refs):
    c, s, core, x, yl = place()
    vec, outs = refs[6], refs[7:]
    for i in range(6):
        outs[i][...] = refs[i][...]
    mine = pltpu.roll(vec[...], 128 - core * 64 - s * 8, 1)
    for i in range(8):
        outs[6 + i][...] = mine[i : i + 1, 0:8]
    up = pltpu.roll(vec[pl.ds(8 + 2 * core + x // 2, 1), :], 128 - lax.rem(s, 4) * 32, 1)
    outs[14][...] = up[:, 0:32]


def owner_call(f):
    arrays = [getattr(f, name) for name in PLAIN]
    shapes = [jax.ShapeDtypeStruct(a.shape, a.dtype) for a in arrays]
    shapes += [jax.ShapeDtypeStruct((1, 8), F32)] * 8 + [jax.ShapeDtypeStruct((1, 32), F32)]
    return pl.pallas_call(
        owner_kernel,
        name="owner",
        out_shape=shapes,
        in_specs=[pl.BlockSpec(memory_space=VMEM)] * 7,
        out_specs=[pl.BlockSpec(memory_space=VMEM)] * 15,
    )(*arrays, f.o_vec)


def named_call(kernel, name, cid, ins, outs, scratch, operands):
    results = pl.pallas_call(
        kernel,
        name=name,
        out_shape=[jax.ShapeDtypeStruct(shape, dtype) for _, _, shape, dtype in outs],
        in_specs=[pl.BlockSpec(memory_space=space) for _, space in ins],
        out_specs=[pl.BlockSpec(memory_space=space) for _, space, _, _ in outs],
        scratch_shapes=[kind for _, kind in scratch],
        compiler_params=pltpu.CompilerParams(
            collective_id=cid, has_side_effects=True, vmem_limit_bytes=60 << 20
        ),
    )(*[operands[name] for name, _ in ins])
    return SimpleNamespace(**dict(zip([o[0] for o in outs], results, strict=True)))


def shards(
    tokens,
    lengths,
    block_pairs,
    ln1_gain,
    ln1_bias,
    w_qkv,
    query_bias,
    value_bias,
    w_out,
    out_bias,
    ln2_gain,
    ln2_bias,
    w_fc1,
    fc1_bias,
    w_fc2,
    fc2_bias,
    out_cotangent,
):
    f = named_call(
        layer_kernel,
        "layer",
        0,
        LAYER_IN,
        LAYER_OUT,
        LAYER_SCRATCH,
        dict(
            lengths=lengths,
            block_pairs=block_pairs,
            tok=tokens.reshape(128, 1024),
            ln1_gain=ln1_gain.reshape(1, 128),
            ln1_bias=ln1_bias.reshape(1, 128),
            query_bias=query_bias.reshape(1, 128),
            value_bias=value_bias.reshape(1, 128),
            out_bias=out_bias.reshape(1, 128),
            ln2_gain=ln2_gain.reshape(1, 128),
            ln2_bias=ln2_bias.reshape(1, 128),
            fc2_bias=fc2_bias.reshape(1, 128),
            fc1_bias=fc1_bias.reshape(4, 128),
            w_qkv=w_qkv,
            w_out=w_out,
            w_fc1=w_fc1,
            w_fc2=w_fc2,
            cot=out_cotangent.reshape(128, 1024),
        ),
    )
    layer_out, input_grad, g_qkv, g_out, g_one, g_two, *vecs = owner_call(f)
    out_b, gain_two, bias_two, fc2_b, query_b, value_b, gain_one, bias_one, up = [v.reshape(-1) for v in vecs]
    return (
        layer_out.reshape(tokens.shape),
        input_grad.reshape(tokens.shape),
        gain_one,
        bias_one,
        g_qkv,
        query_b,
        value_b,
        g_out,
        out_b,
        gain_two,
        bias_two,
        g_one,
        up,
        g_two,
        fc2_b,
    )


def solution(mesh):
    one, both = P("shard"), P(("ctx", "shard"))
    rows, both_rows = P("shard", None), P(("ctx", "shard"), None)
    whole = P("ctx", "shard", None, None)
    return jax.shard_map(
        shards,
        mesh=mesh,
        in_specs=(
            whole, one, P(), one, one, rows, one, one, rows, one, one, one, rows, one, rows, one, whole,
        ),
        out_specs=(
            whole, whole, both, both, both_rows, both, both, both_rows, both, both, both,
            both_rows, both, both_rows, both,
        ),
        check_vma=False,
    )
```

```python
from types import SimpleNamespace

import jax
import jax.numpy as jnp
from jax import lax
from jax.experimental import pallas as pl
from jax.experimental.pallas import tpu as pltpu
from jax.sharding import PartitionSpec as P

HEADS = 16
HEAD_DIM = 64
MESH = pl.DeviceIdType.MESH
ANY = pl.ANY
VMEM = pltpu.VMEM
F32 = jnp.float32
BF16 = jnp.bfloat16

eps_norm = 1e-05
negative = -1e30


def place():
    c, s = lax.axis_index("ctx"), lax.axis_index("shard")
    return c, s, lax.rem(c, 2), s // 2, lax.rem(s, 2)


def sibling(c):
    return c + 1 - 2 * lax.rem(c, 2)


def norm_back(grad_normed, normed, inverse, gain):
    scaled = grad_normed * gain
    centred = scaled - jnp.mean(scaled, axis=-1, keepdims=True)
    return inverse * (centred - normed * jnp.mean(scaled * normed, axis=-1, keepdims=True))


def dot(left, right):
    return jnp.dot(left, right, preferred_element_type=F32)


def dot_tn(left, right):
    return lax.dot_general(left, right, (((0,), (0,)), ((), ())), preferred_element_type=F32)


def pick(value, unit):
    return pl.multiple_of(value * unit, unit)


def loop(count, body, first=0):
    def step(k, carry):
        body(k)
        return carry

    lax.fori_loop(first, count, step, 0)


def remote(src, dst, send_sem, recv_sem, device):
    return pltpu.make_async_remote_copy(
        src_ref=src,
        dst_ref=dst,
        send_sem=send_sem,
        recv_sem=recv_sem,
        device_id=device,
        device_id_type=MESH,
    )


def not_when(condition, body):
    pl.when(jnp.logical_not(condition))(body)


def norm_rows(rows):
    centre = rows - jnp.mean(rows, axis=-1, keepdims=True)
    inverse = lax.rsqrt(jnp.mean(centre * centre, axis=-1, keepdims=True) + eps_norm)
    return centre * inverse, inverse


def dot_nt(left, right):
    return lax.dot_general(left, right, (((1,), (1,)), ((), ())), preferred_element_type=F32)


VECTORS = (
    "ln1_gain", "ln1_bias", "query_bias", "value_bias", "out_bias", "ln2_gain", "ln2_bias", "fc2_bias",
)

LAYER_IN = (
    ("lengths", pltpu.SMEM),
    ("block_pairs", pltpu.SMEM),
    ("tok", ANY),
    *[(name, VMEM) for name in VECTORS],
    ("fc1_bias", VMEM),
    ("w_qkv", ANY),
    ("w_out", ANY),
    ("w_fc1", ANY),
    ("w_fc2", ANY),
    ("cot", ANY),
)

LAYER_OUT = (
    ("layer_out", ANY, (128, 1024), BF16),
    ("input_grad", ANY, (128, 1024), BF16),
    ("o_qkv", ANY, (8, 3072), F32),
    ("o_out", ANY, (8, 1024), F32),
    ("o_one", ANY, (8, 4096), F32),
    ("o_two", ANY, (32, 1024), F32),
    ("o_vec", ANY, (16, 128), F32),
)

WEIGHTS = (("wq", 768), ("wo", 1024), ("w1", 1024), ("w2", 1024))
GRADS = (("two", 1024), ("one", 1024), ("out", 1024), ("qka", 384), ("qkb", 384))

LAYER_SCRATCH = (
    *[(name + "_all", pltpu.VMEM((8, 128, width), BF16)) for name, width in WEIGHTS],
    *[
        (prefix + name, pltpu.VMEM((*shape, width), BF16))
        for name, width in GRADS
        for prefix, shape in (
            ("g_", (8, 2, 64)), ("n_", (8, 64)), ("a_", (4, 4, 32)), ("b_", (4, 4, 32)), ("m_", (4, 32)), ("h_", (4, 32)),
        )
    ],
    *[("s_" + name, pltpu.VMEM((32, width), F32)) for name, width in GRADS],
    *[
        (name, pltpu.VMEM(shape, BF16))
        for name, shape in (
            ("tok_all", (4, 128, 1024)), ("attn_all", (4, 128, 1024)), ("cot_all", (4, 128, 1024)),
            ("qkv", (4, 4, 64, 384)), ("parts", (4, 4, 64, 384)),
            ("probs", (2, 1024, 1024)), ("mixed", (16, 64, 128)), ("mix_rows", (2, 64, 1024)),
            ("mlp_all", (4, 128, 1024)), ("act_all", (4, 128, 1024)), ("gp_all", (4, 128, 1024)),
            ("gm_out", (4, 128, 1024)), ("mo_out", (4, 128, 1024)), ("gm_in", (4, 128, 1024)),
            ("mo_in", (4, 128, 1024)), ("hidden_low", (128, 1024)), ("gmix", (2, 64, 1024)),
            ("gmixed", (16, 64, 128)), ("gparts", (4, 4, 64, 384)), ("gback", (4, 4, 64, 384)),
            ("gqkv", (4, 128, 768)), ("ga_out", (4, 128, 1024)), ("ga_in", (4, 128, 1024)), ("ga_via", (4, 64, 1024)),
            ("w_layer", (128, 1024)), ("w_input", (128, 1024)),
        )
    ],
    *[
        (name, pltpu.VMEM(shape, F32))
        for name, shape in (
            ("small", (16, 128)), ("small_all", (16, 1024)), ("places", (1024, 128)), ("mix_t", (128, 1024)),
            ("hidden", (128, 1024)), ("gm_own", (128, 1024)), ("mo_own", (128, 1024)),
            ("grad_hidden", (128, 1024)), ("ga_own", (128, 1024)), ("gq_t", (128, 1024)), ("delta", (2, 1024)),
            ("r_two", (32, 1024)), ("r_one", (4, 8, 1024)), ("r_out", (4, 8, 1024)), ("r_qka", (4, 8, 384)),
            ("r_qkb", (4, 8, 384)), ("w_qkv_out", (8, 3072)), ("w_out_out", (8, 1024)), ("w_one_out", (8, 4096)),
            ("w_vec_out", (16, 128)),
            ("vec", (16, 1024)), ("vec_sib", (16, 1024)), ("vec_in", (8, 16, 128)), ("vec_sum", (16, 128)),
            ("vec_all", (8, 16, 128)),
        )
    ],
    *[
        (prefix + name, pltpu.SemaphoreType.DMA((count,)))
        for name, _ in WEIGHTS
        for prefix, count in (("sent_", 2), ("along_", 4), ("up_", 1), ("cross_", 1))
    ],
    *[
        (prefix + name, pltpu.SemaphoreType.DMA((1,)))
        for name, _ in GRADS
        for prefix in ("near_s_", "near_r_", "first_s_", "first_r_", "second_s_", "second_r_", "last_s_", "last_r_")
    ],
    *[
        (name + end, pltpu.SemaphoreType.DMA((1,)))
        for name in ("sm", "tf", "qa", "mx", "mg", "gm", "mo", "mf", "hb", "ga", "vs", "v1", "v2")
        for end in ("_s", "_r")
    ],
    *[
        (name, pltpu.SemaphoreType.DMA((count,)))
        for name, count in (
            ("local", 7), ("done", 7), ("tk_s", 1), ("tk_r", 4), ("ct_s", 1), ("ct_r", 4), ("ml_s", 1), ("ml_r", 4),
            ("gv_r", 4),
        )
    ],
)


def layer_kernel(*refs):
    names = [n[0] for n in LAYER_IN + LAYER_OUT + LAYER_SCRATCH]
    r = SimpleNamespace(**dict(zip(names, refs, strict=True)))
    ref = lambda *name: getattr(r, "".join(name))
    c, s, core, x, yl = place()
    z, yh, q4 = c // 4, lax.rem(c // 2, 2), lax.rem(c, 4)
    sib = (sibling(c), s)
    mate_s = s + 1 - 2 * yl
    half = lambda which: pl.ds(pick(which, 64), 64)

    pieces = [(r.w_qkv, r.wq_all, t * 1024 + z * 256, t * 256, 256) for t in range(3)]
    pieces += [(r.w_fc1, r.w1_all, t * 512 + z * 128, t * 128, 128) for t in range(8)]
    own = [
        pltpu.make_async_copy(
            weight.at[half(core), pl.ds(pl.multiple_of(source, 128), width)],
            whole.at[s, half(core), target : target + width],
            r.local.at[0 if i < 3 else 1],
        )
        for i, (weight, whole, source, target, width) in enumerate(pieces)
    ]
    own.append(pltpu.make_async_copy(r.w_out.at[half(core)], r.wo_all.at[s, half(core)], r.local.at[2]))
    own.append(
        pltpu.make_async_copy(r.w_fc2.at[half(2 * z + core)], r.w2_all.at[s, half(core)], r.local.at[3])
    )
    own.append(pltpu.make_async_copy(r.cot, r.cot_all.at[z], r.local.at[4]))
    own.append(pltpu.make_async_copy(r.tok, r.tok_all.at[z], r.local.at[5]))

    barrier = pltpu.get_barrier_semaphore()

    def hail(device):
        pl.semaphore_signal(barrier, inc=1, device_id=device, device_id_type=MESH)

    to_z, from_x, from_yl = 2 * yl + lax.rem(x, 2), x // 2 * 2 + lax.rem(z, 2), z // 2
    at_home = to_z == z
    two_to = (to_z * 4 + yh * 2 + z // 2, (lax.rem(z, 2) * 2 + core) * 2 + x // 2)
    two_from = (
        (core * 2 + x // 2) * 4 + yh * 2 + lax.rem(x, 2),
        (yl * 2 + lax.rem(z, 2)) * 2 + z // 2,
    )
    two_stays = (two_to[0] == c) & (two_to[1] == s)
    loop(8, lambda k: hail((c, lax.rem(s + k, 8))), 1)
    loop(16, lambda k: hail((lax.rem(c + k, 16), s)), 1)
    hail((c + 2 - 4 * yh, mate_s))
    loop(4, lambda k: not_when(at_home & (k == z), lambda: hail((k * 4 + q4, 2 * from_x + from_yl))))
    not_when(two_stays, lambda: hail(two_from))
    for copy in own:
        copy.start()

    for i, name in enumerate(VECTORS):
        r.small[i : i + 1, :] = ref(name)[...].astype(F32)
    r.small[8:12, :] = r.fc1_bias[...].astype(F32)
    r.small[12:16, :] = jnp.zeros((4, 128), F32)


    def own_here(whole, sem):
        block = whole.at[s, half(core)]
        pltpu.make_async_copy(block, block, r.local.at[sem]).wait()

    own_here(r.wq_all, 0)
    pl.semaphore_wait(barrier, 28 - at_home.astype(jnp.int32) - two_stays.astype(jnp.int32))

    def await_block(dst, recv_sem):
        remote(dst, dst, r.local.at[6], recv_sem, sib).wait_recv()

    def await_sent(block, send_sem):
        remote(block, block, send_sem, r.local.at[6], sib).wait_send()

    columns_of = lambda which: pl.ds(pick(which, 128), 128)
    z_peer = lambda k: (lax.rem(c + 4 * k, 16), s)
    x_peer = lambda k: (c, 2 * lax.rem(x + k, 4) + yl)

    def small_to(k):
        return remote(
            r.small, r.small_all.at[:, columns_of(s)], r.sm_s.at[0], r.sm_r.at[0], (c, lax.rem(s + k, 8))
        )

    def tok_to(k):
        return remote(r.tok, r.tok_all.at[z], r.tk_s.at[0], r.tk_r.at[k], z_peer(k))

    def cot_to(k):
        return remote(r.cot, r.cot_all.at[z], r.ct_s.at[0], r.ct_r.at[k], z_peer(k))

    z_of = lambda hop: lax.rem(z - hop + 4, 4)

    def pass_on(whole, send_sems, recv_sems, k):
        rows = slice(0, 64) if k == 1 else slice(64, 128)
        block = whole.at[z_of(k), rows]
        return remote(block, block, send_sems.at[0], recv_sems.at[0], z_peer(k))

    def ring_arrived(whole, recv_sems, send_next, recv_next, k):
        @pl.when(k == 1)
        def _():
            for j in (1, 3):
                await_block(whole.at[z_of(j)], recv_sems.at[j])
                pass_on(whole, send_next, recv_next, j).start()

        @pl.when(k == 3)
        def _():
            await_block(whole.at[z_of(2)], recv_next.at[0])

    y_next = lambda p: (c + (2 - 4 * yh) * p, mate_s)
    some_rows = lambda p: pl.ds(pick(2 * core + p, 32), 32)

    def weight_along(name, kind, k):
        whole = ref(name, "_all")
        block = whole.at[s if kind == "own_" else mate_s, half(core)]
        return remote(
            block, block, ref("sent_", name).at[0], ref("along_", name).at[0 if name == "wo" else k], x_peer(k)
        )

    def weight_up(name, k, p):
        block = ref(name, "_all").at[2 * lax.rem(x - k + 4, 4) + yl, some_rows(p)]
        return remote(block, block, ref("sent_", name).at[0], ref("up_", name).at[0], y_next(p))

    def weight_cross(name):
        block = ref(name, "_all").at[:, half(core)]
        return remote(block, block, ref("sent_", name).at[1], ref("cross_", name).at[0], sib)

    def weight_own(name):
        for p in range(2):
            weight_up(name, 0, p).start()
        for k in (1, 3, 2):
            weight_along(name, "own_", k).start()

    def await_along(name, k):
        block = ref(name, "_all").at[2 * lax.rem(x - k + 4, 4) + yl, half(core)]
        await_block(block, ref("along_", name).at[k])

    def weight_far(name):
        if name == "wo":
            await_block(ref(name, "_all").at[mate_s, half(core)], ref("up_", name).at[0])
            for k in (1, 3, 2):
                weight_along(name, "far_", k).start()
        else:
            for k in (1, 3, 2):
                await_along(name, k)
                for p in range(2):
                    weight_up(name, k, p).start()

    def weight_across(name):
        if name == "wo":
            await_block(ref(name, "_all").at[0:6, 0:64], ref("along_", name).at[0])
        else:
            await_block(ref(name, "_all").at[0:4, 0:64], ref("up_", name).at[0])
        weight_cross(name).start()

    def weight_ready(name):
        await_block(ref(name, "_all").at[:, half(1 - core)], ref("cross_", name).at[0])

    for k in (1, 3):
        tok_to(k).start()
    weight_own("wq")
    loop(8, lambda k: small_to(k).start(), 1)
    r.small_all[:, columns_of(s)] = r.small[...]
    weight_far("wq")

    sub = lax.broadcasted_iota(jnp.int32, (64, 128), 0)

    def set_places(k):
        pair = r.block_pairs[k]
        block = jnp.where(sub < 32, pair, 31 - pair)
        r.places[pl.ds(pick(k, 64), 64), :] = (block * 32 + lax.rem(sub, 32)).astype(F32)

    loop(16, set_places)
    await_block(r.small_all.at[:, 0:896], r.sm_r.at[0])
    weight_across("wq")
    own_here(r.w1_all, 1)
    for copy in own[11:14]:
        copy.wait()
    weight_own("wo")
    weight_own("w1")

    gain_one, bias_one = r.small_all[0:1, :], r.small_all[1:2, :]
    head_cols = pl.ds(pick(z, 256), 256)
    bias_qkv = (r.small_all[2:3, head_cols], None, r.small_all[3:4, head_cols])

    def parts_to(m, origin):
        peer = lax.rem(q4 + m, 4)
        return remote(
            r.qkv.at[peer, origin],
            r.parts.at[origin, q4],
            r.qa_s.at[0],
            r.qa_r.at[0],
            (4 * z + peer, s),
        )

    def norm_block(origin):
        normed, _ = norm_rows(r.tok_all[origin].astype(F32))
        r.attn_all[origin] = (normed * gain_one + bias_one).astype(BF16)

    own[14].wait()
    norm_block(z)
    weight_ready("wq")

    def hop_of(k):
        return k + (k // 2) * (1 - 2 * lax.rem(k, 2))

    def qkv_block(k):
        hop = hop_of(k)
        origin = z_of(hop)
        ring_arrived(r.tok_all, r.tk_r, r.tf_s, r.tf_r, k)

        @pl.when(k > 0)
        def _():
            norm_block(origin)

        for t in range(3):
            cols = slice(t * 256, t * 256 + 256)
            acc = dot(r.attn_all[origin], r.wq_all[:, :, cols].reshape(1024, 256))
            if bias_qkv[t] is not None:
                acc = acc + bias_qkv[t]
            acc = acc.astype(BF16)
            for j in range(2):
                for p in range(2):
                    r.qkv[j * 2 + p, origin, :, t * 128 : t * 128 + 128] = acc[
                        j * 64 : j * 64 + 64, p * 128 : p * 128 + 128
                    ]
        for m in (1, 2, 3):
            parts_to(m, origin).start()
        r.parts[origin, q4] = r.qkv[q4, origin]

    loop(4, qkv_block)
    weight_far("wo")
    for k in (1, 3, 2):
        cot_to(k).start()
    weight_own("w2")

    await_block(r.parts.at[0:3], r.qa_r.at[0])
    weight_far("w1")

    length = jnp.where(yh == 0, r.lengths[0], r.lengths[1]).astype(F32)
    head_lane = lax.broadcasted_iota(jnp.int32, (1, 128), 1) // 64
    value_t = r.parts[:, :, :, 256:384].reshape(1024, 128).T

    def masked(rows, h):
        return jnp.where(head_lane == h, rows, jnp.zeros_like(rows))

    def pair_columns(which):
        return columns_of(which // 4 * 2 + lax.rem(which, 2))

    def slot_of(which):
        return lax.rem(which // 2, 2)

    def mix_to(peer):
        return remote(
            r.mixed.at[peer], r.mix_rows.at[yh, :, pair_columns(c)], r.mx_s.at[0], r.mx_r.at[0], (peer, s)
        )

    def attend(k):
        i = lax.rem(z + k + 1, 4)
        keys = r.parts[:, :, :, 128:256].reshape(1024, 128)
        key_place = r.places[:, 0:1]
        query_place = r.places[pl.ds(pick(i, 256), 256), :].T[0:1, :]
        allowed = (key_place < length) & (key_place <= query_place)
        queries = r.parts[i, :, :, 0:128].reshape(256, 128) * jnp.asarray(0.125, BF16)
        cols = pl.ds(pick(i, 256), 256)
        for h in range(2):
            scores = jnp.where(allowed, dot_nt(keys, masked(queries, h)), negative)
            powers = jnp.exp(scores - jnp.max(scores, axis=0, keepdims=True))
            low = (powers * (1.0 / jnp.sum(powers, axis=0, keepdims=True))).astype(BF16)
            r.probs[h, :, cols] = low
            r.mix_t[h * 64 : h * 64 + 64, cols] = dot(value_t[h * 64 : h * 64 + 64], low)
        r.mixed[pl.ds(4 * i, 4)] = r.mix_t[:, cols].T.astype(BF16).reshape(4, 64, 128)
        for q in range(4):
            not_when(4 * i + q == c, lambda: mix_to(4 * i + q).start())

    loop(4, attend)

    r.mix_rows[yh, :, pair_columns(c)] = r.mixed[c]
    weight_across("wo")
    weight_far("w2")
    weight_across("w1")
    weight_ready("wo")

    await_block(r.mixed.at[0:15], r.mx_r.at[0])

    mix = r.mix_rows[...].reshape(128, 1024)
    hidden = r.tok_all[z].astype(F32) + (dot(mix, r.wo_all[...].reshape(1024, 1024)) + r.small_all[4:5, :])
    r.hidden[...] = hidden
    normed, _ = norm_rows(hidden)
    r.mlp_all[z] = (normed * r.small_all[5:6, :] + r.small_all[6:7, :]).astype(BF16)

    def mlp_to(k):
        return remote(r.mlp_all.at[z], r.mlp_all.at[z], r.ml_s.at[0], r.ml_r.at[k], z_peer(k))

    for k in (1, 3):
        mlp_to(k).start()
    weight_across("w2")
    weight_ready("w1")
    weight_ready("w2")

    r.vec[...] = jnp.zeros_like(r.vec)
    up_row = pl.ds(8 + z, 1)
    upper = lax.broadcasted_iota(jnp.int32, (128, 1), 0) < 64
    row_length = jnp.where(upper, r.lengths[0], r.lengths[1]).astype(F32)

    def valid_of(origin):
        mine = r.places[half(origin * 4 + q4), 0:1]
        return (jnp.concatenate([mine, mine], axis=0) < row_length).astype(F32)

    def part_to(out, into, sems, k):
        return remote(out.at[lax.rem(z + k, 4)], into.at[k], sems[0].at[0], sems[1].at[0], z_peer(k))

    gm_sems, mo_sems, ga_sems = (r.gm_s, r.gm_r), (r.mo_s, r.mo_r), (r.ga_s, r.ga_r)

    def mlp_block(k):
        hop = hop_of(k)
        origin = z_of(hop)
        ring_arrived(r.mlp_all, r.ml_r, r.mg_s, r.mg_r, k)

        @pl.when(k > 0)
        def _():
            await_block(r.cot_all.at[origin], r.ct_r.at[hop])

        r.cot_all[origin] = (r.cot_all[origin].astype(F32) * valid_of(origin)).astype(BF16)
        for i in range(4):
            cols = slice(i * 256, i * 256 + 256)
            pre = dot(r.mlp_all[origin], r.w1_all[:, :, cols].reshape(1024, 256)) + r.small_all[up_row, cols]
            spread = 0.5 * (1.0 + lax.erf(pre * 0.7071067811865476))
            r.act_all[origin, :, cols] = (pre * spread).astype(BF16)
            slope = spread + pre * (0.3989422804014327 * jnp.exp(-0.5 * pre * pre))
            grad = dot_nt(r.cot_all[origin], r.w2_all[2 * i : 2 * i + 2].reshape(256, 1024)) * slope
            r.vec[up_row, cols] += jnp.sum(grad, axis=0, keepdims=True)
            r.gp_all[origin, :, cols] = grad.astype(BF16)
        for i in range(4):
            cols = slice(i * 256, i * 256 + 256)
            part = dot_nt(r.gp_all[origin], r.w1_all[2 * i : 2 * i + 2].reshape(256, 1024))
            r.gm_out[origin, :, cols] = part.astype(BF16)

            @pl.when(k == 0)
            def _():
                r.gm_own[:, cols] = part

        @pl.when(k > 0)
        def _():
            part_to(r.gm_out, r.gm_in, gm_sems, 4 - hop).start()

    loop(4, mlp_block)

    def mlp_out(origin):
        for i in range(4):
            cols = slice(i * 256, i * 256 + 256)
            part = dot(r.act_all[origin], r.w2_all[:, :, cols].reshape(1024, 256))
            r.mo_out[origin, :, cols] = part.astype(BF16)

            @pl.when(origin == z)
            def _():
                r.mo_own[:, cols] = part

    def outer(name, left, right, width, first=0):
        into = ref("g_", name)

        def body(i):
            rows = pl.ds(pick(i, 256), 256)
            part = dot_tn(
                left[:, :, rows].reshape(512, 256), right[:, :, first : first + width].reshape(512, width)
            )
            into[pl.ds(2 * i, 2)] = part.astype(BF16).reshape(2, 2, 64, width)

        loop(4, body)

    def near_to(which):
        name = GRADS[which][0]
        return remote(
            ref("g_", name).at[:, 1 - core], ref("n_", name), ref("near_s_", name).at[0], ref("near_r_", name).at[0], sib
        )

    def y_peer(k):
        yh_to, yl_to = (1 - yh if k // 2 else yh), (1 - yl if k % 2 else yl)
        return (c + 2 * (yh_to - yh), s + yl_to - yl), 2 * yh_to + yl_to

    here = {"x": x, "y": 2 * yh + yl}
    order = {"two": "xy", "one": "yx", "out": "xy", "qka": "xy", "qkb": "yx"}

    def peer_of(axis, k):
        return (x_peer(k), lax.rem(x + k, 4)) if axis == "x" else y_peer(k)

    def first_to(name, k):
        device, index = peer_of(order[name][0], k)
        sems = ref("first_s_", name), ref("first_r_", name)
        return remote(ref("a_", name).at[index], ref("b_", name).at[k], sems[0].at[0], sems[1].at[0], device)

    def second_to(name, k):
        device, index = peer_of(order[name][1], k)
        sems = ref("second_s_", name), ref("second_r_", name)
        return remote(ref("m_", name).at[index], ref("h_", name).at[k], sems[0].at[0], sems[1].at[0], device)

    def pair_sum(which):
        name = GRADS[which][0]
        grad, near, into = ref("g_", name), ref("n_", name), ref("a_", name)
        await_block(near, ref("near_r_", name).at[0])

        def add(j):
            y_to = lax.rem(j, 2) * 2 + j // 4
            for xh in range(2):
                x_to = 2 * xh + lax.rem(j // 2, 2)
                rows = slice(32 * xh, 32 * xh + 32)
                total = near[j, rows].astype(F32) + grad[j, core, rows].astype(F32)
                target = (x_to, y_to) if order[name] == "xy" else (y_to, x_to)
                into[target[0], target[1]] = total.astype(BF16)

        loop(8, add)
        for k in (1, 3, 2):
            first_to(name, k).start()

    def first_sum(name):
        mine, others, into = ref("a_", name), ref("b_", name), ref("m_", name)
        await_block(others.at[1:4], ref("first_r_", name).at[0])

        def add(j):
            total = mine[here[order[name][0]], j].astype(F32)
            for k in (1, 2, 3):
                total = total + others[k, j].astype(F32)
            into[j] = total.astype(BF16)

        loop(4, add)
        for k in (1, 3, 2):
            second_to(name, k).start()

    def second_sum(name):
        mine, others = ref("m_", name), ref("h_", name)
        await_block(others.at[1:4], ref("second_r_", name).at[0])
        total = mine[here[order[name][1]]].astype(F32)
        for k in (1, 2, 3):
            total = total + others[k].astype(F32)
        ref("s_", name)[...] = total

    outer("two", r.act_all, r.cot_all, 1024)
    near_to(0).start()
    outer("one", r.mlp_all, r.gp_all, 1024)
    near_to(1).start()
    loop(4, mlp_out)

    total = r.gm_own[...]
    await_block(r.gm_in.at[1:4], r.gm_r.at[0])
    for k in (1, 3, 2):
        total = total + r.gm_in[k].astype(F32)
    normed, inverse = norm_rows(r.hidden[...])
    grad_out = r.cot_all[z].astype(F32)
    grad_hidden = grad_out + norm_back(total, normed, inverse, r.small_all[5:6, :])
    r.grad_hidden[...] = grad_hidden
    r.hidden_low[...] = grad_hidden.astype(BF16)
    for i, rows in enumerate((grad_hidden, total * normed, total, grad_out)):
        r.vec[i : i + 1, :] = jnp.sum(rows, axis=0, keepdims=True)
    for i in range(4):
        part = dot_nt(r.hidden_low[...], r.wo_all[2 * i : 2 * i + 2].reshape(256, 1024))
        r.gmix[:, :, i * 256 : i * 256 + 256] = part.astype(BF16).reshape(2, 64, 256)

    def gmix_to(k):
        peer = lax.rem(c + k, 16)
        return remote(
            r.gmix.at[slot_of(peer), :, pair_columns(peer)], r.gmixed.at[c], r.mf_s.at[0], r.mf_r.at[0], (peer, s)
        )

    loop(16, lambda k: gmix_to(k).start(), 1)
    r.gmixed[c] = r.gmix[yh, :, pair_columns(c)]

    def out_rows(i):
        rows = pl.ds(pick(i, 256), 256)
        part = dot_tn(r.mix_rows[:, :, rows].reshape(128, 256), r.hidden_low[...])
        r.g_out[pl.ds(2 * i, 2)] = part.astype(BF16).reshape(2, 2, 64, 1024)

    pair_sum(0)
    loop(4, out_rows)
    near_to(2).start()
    await_block(r.gmixed.at[0:15], r.mf_r.at[0])
    for k in (1, 3, 2):
        part_to(r.mo_out, r.mo_in, mo_sems, k).start()

    def back_to(m, piece, i):
        peer = lax.rem(q4 + m, 4)
        cols = slice(piece * 128, piece * 128 + 128)
        return remote(
            r.gparts.at[i, peer, :, cols],
            r.gback.at[q4, i, :, cols],
            r.hb_s.at[0],
            r.hb_r.at[0],
            (4 * z + peer, s),
        )

    def back_start(piece, i):
        for m in (1, 2, 3):
            back_to(m, piece, i).start()

    def values_back(i):
        gm = r.gmixed[...].reshape(1024, 128)
        rows = pl.ds(pick(i, 256), 256)
        acc = dot(r.probs[0, rows], masked(gm, 0)) + dot(r.probs[1, rows], masked(gm, 1))
        r.gparts[i, :, :, 256:384] = acc.astype(BF16).reshape(4, 64, 128)
        back_start(2, i)
        return jnp.sum(acc, axis=0, keepdims=True)

    bias_v = lax.fori_loop(0, 4, lambda i, acc: acc + values_back(i), jnp.zeros((1, 128), F32))
    products = r.gmixed[...].reshape(1024, 128).astype(F32).T * r.mix_t[...]
    for h in range(2):
        r.delta[h : h + 1, :] = jnp.sum(products[h * 64 : h * 64 + 64], axis=0, keepdims=True)
    keys_t = r.parts[:, :, :, 128:256].reshape(1024, 128).T

    def scores_back(i):
        cols = pl.ds(pick(i, 256), 256)
        values = r.parts[:, :, :, 256:384].reshape(1024, 128)
        gm = r.gmixed[pl.ds(i * 4, 4)].reshape(256, 128)
        for h in range(2):
            grad = dot_nt(values, masked(gm, h)) - r.delta[h : h + 1, cols]
            low = (r.probs[h, :, cols].astype(F32) * grad).astype(BF16)
            r.probs[h, :, cols] = low
            r.gq_t[h * 64 : h * 64 + 64, cols] = dot(keys_t[h * 64 : h * 64 + 64], low)
        gq = r.gq_t[:, cols].T * 0.125
        r.gparts[i, :, :, 0:128] = gq.astype(BF16).reshape(4, 64, 128)
        back_start(0, i)
        return jnp.sum(gq, axis=0, keepdims=True)

    bias_q = lax.fori_loop(0, 4, lambda i, acc: acc + scores_back(i), jnp.zeros((1, 128), F32))

    def keys_back(i):
        queries = r.parts[:, :, :, 0:128].reshape(1024, 128) * jnp.asarray(0.125, BF16)
        rows = pl.ds(pick(i, 256), 256)
        acc = dot(r.probs[0, rows], masked(queries, 0)) + dot(r.probs[1, rows], masked(queries, 1))
        r.gparts[i, :, :, 128:256] = acc.astype(BF16).reshape(4, 64, 128)
        back_start(1, i)

    loop(4, keys_back)
    r.gback[q4] = r.gparts[:, q4]
    wide = lax.broadcasted_iota(jnp.int32, (1, 1024), 1) // 128 == 2 * z + core
    for i, sums in ((4, bias_q), (5, bias_v)):
        r.vec[i : i + 1, :] = jnp.where(wide, jnp.concatenate([sums] * 8, axis=1), 0.0)

    pair_sum(1)
    pair_sum(2)
    first_sum("two")
    total = r.mo_own[...] + r.small_all[7:8, :]
    await_block(r.mo_in.at[1:4], r.mo_r.at[0])
    for k in (1, 3, 2):
        total = total + r.mo_in[k].astype(F32)
    r.w_layer[...] = (valid_of(z) * (r.hidden[...] + total)).astype(BF16)
    results = [pltpu.make_async_copy(r.w_layer, r.layer_out, r.done.at[0])]
    results[0].start()

    await_block(r.gback.at[0:3], r.hb_r.at[0])

    def assemble(origin):
        for t in range(3):
            for j in range(2):
                for p in range(2):
                    r.gqkv[origin, j * 64 : j * 64 + 64, t * 256 + p * 128 : t * 256 + p * 128 + 128] = r.gback[
                        j * 2 + p, origin, :, t * 128 : t * 128 + 128
                    ]

    loop(4, assemble)

    def attn_back(hop):
        origin = lax.rem(z + hop, 4)
        normed, _ = norm_rows(r.tok_all[origin].astype(F32))
        for i in range(4):
            cols = slice(i * 256, i * 256 + 256)
            part = dot_nt(r.gqkv[origin], r.wq_all[2 * i : 2 * i + 2].reshape(256, 768))
            r.ga_out[origin, :, cols] = part.astype(BF16)
            r.vec[6:7, cols] += jnp.sum(part * normed[:, cols], axis=0, keepdims=True)
            r.vec[7:8, cols] += jnp.sum(part, axis=0, keepdims=True)

            @pl.when(hop == 0)
            def _():
                r.ga_own[:, cols] = part

    halves = {1: slice(0, 64), 3: slice(64, 128)}

    def via_to(k):
        return remote(
            r.ga_out.at[lax.rem(z + 2, 4), halves[k]], r.ga_via.at[k], r.ga_s.at[0], r.gv_r.at[k], z_peer(k)
        )

    def via_add(k):
        await_block(r.ga_via.at[k], r.gv_r.at[k])
        target = lax.rem(z + k, 4)
        total = r.ga_out[target, halves[k]].astype(F32) + r.ga_via[k].astype(F32)
        r.ga_out[target, halves[k]] = total.astype(BF16)
        part_to(r.ga_out, r.ga_in, ga_sems, k).start()

    attn_back(2)
    via_to(1).start()
    via_to(3).start()
    outer("qka", r.attn_all, r.gqkv, 384)
    near_to(3).start()
    outer("qkb", r.attn_all, r.gqkv, 384, 384)
    near_to(4).start()
    loop(2, lambda k: attn_back(1 + 2 * k))
    via_add(1)
    via_add(3)
    pair_sum(3)
    pair_sum(4)
    attn_back(0)
    vec_across = remote(r.vec, r.vec_sib, r.vs_s.at[0], r.vs_r.at[0], sib)
    vec_across.start()
    await_block(r.vec_sib, r.vs_r.at[0])
    await_sent(r.vec_sib, r.vs_s.at[0])
    r.vec[...] += r.vec_sib[...]
    chip = c // 2

    def vec_to(k):
        peer = lax.rem(chip + k, 8)
        return remote(r.vec.at[:, columns_of(peer)], r.vec_in.at[k], r.v1_s.at[0], r.v1_r.at[0], (2 * peer + core, s))

    loop(8, lambda k: vec_to(k).start(), 1)

    my_part = pl.ds(pick(lax.rem(x, 2) * 2 + yl, 8), 8)

    def last_to(name, k):
        rows = slice(8 * k, 8 * k + 8)
        sems = ref("last_s_", name), ref("last_r_", name)
        device = (to_z * 4 + q4, 2 * (x // 2 * 2 + k // 2) + k % 2)
        return remote(ref("s_", name).at[rows], ref("r_", name).at[z], sems[0].at[0], sems[1].at[0], device)

    def at_owner(k):
        return at_home & (lax.rem(x, 2) == k // 2) & (yl == k % 2)

    def spread(name):
        for k in range(4):
            not_when(at_owner(k), lambda: last_to(name, k).start())

        @pl.when(at_home)
        def _():
            ref("r_", name)[z] = ref("s_", name)[my_part]

    def two_copy():
        return remote(r.s_two, r.r_two, r.last_s_two.at[0], r.last_r_two.at[0], two_to)

    def finish(which, source, target):
        results.append(pltpu.make_async_copy(source, target, r.done.at[which]))
        results[-1].start()

    first_sum("one")
    second_sum("two")
    not_when(two_stays, lambda: two_copy().start())

    @pl.when(two_stays)
    def _():
        r.r_two[...] = r.s_two[...]

    second_sum("one")
    spread("one")
    first_sum("out")

    await_block(r.vec_in.at[1:8], r.v1_r.at[0])
    sums = r.vec[:, columns_of(chip)]
    for k in range(1, 8):
        sums = sums + r.vec_in[k]
    r.vec_sum[...] = sums

    def vec_rows_to(k):
        return remote(r.vec_sum, r.vec_all.at[s], r.v2_s.at[0], r.v2_r.at[0], (c, lax.rem(s + k, 8)))

    loop(8, lambda k: vec_rows_to(k).start(), 1)
    r.vec_all[s] = sums
    first_sum("qka")
    first_sum("qkb")
    second_sum("out")
    spread("out")

    total = r.ga_own[...]
    await_block(r.ga_in.at[0:2], r.ga_r.at[0])
    for k in (1, 3):
        total = total + r.ga_in[k].astype(F32)
    normed, inverse = norm_rows(r.tok_all[z].astype(F32))
    r.w_input[...] = (
        r.grad_hidden[...] + norm_back(total, normed, inverse, r.small_all[0:1, :])
    ).astype(BF16)
    finish(1, r.w_input, r.input_grad)

    second_sum("qka")
    spread("qka")
    second_sum("qkb")
    spread("qkb")

    def rows_arrived(name):
        into = ref("r_", name)
        not_when(at_home, lambda: await_block(into, ref("last_r_", name).at[0]))
        pl.when(at_home)(lambda: await_block(into.at[0:3], ref("last_r_", name).at[0]))

    not_when(two_stays, lambda: await_block(r.r_two, r.last_r_two.at[0]))
    finish(2, r.r_two, r.o_two)
    rows_arrived("one")
    for i in range(4):
        for t in range(8):
            r.w_one_out[:, t * 512 + i * 128 : t * 512 + i * 128 + 128] = r.r_one[i, :, t * 128 : t * 128 + 128]
    finish(3, r.w_one_out, r.o_one)
    rows_arrived("out")
    r.w_out_out[...] = (r.r_out[0] + r.r_out[1]) + (r.r_out[2] + r.r_out[3])
    finish(4, r.w_out_out, r.o_out)
    await_block(r.vec_all.at[0:7], r.v2_r.at[0])
    total = r.vec_all[0]
    for i in range(1, 8):
        total = total + r.vec_all[i]
    r.w_vec_out[...] = total
    finish(5, r.w_vec_out, r.o_vec)
    rows_arrived("qka")
    rows_arrived("qkb")
    for i in range(4):
        for t in range(6):
            source = r.r_qka if t < 3 else r.r_qkb
            column = t // 2 * 1024 + i * 256 + t % 2 * 128
            r.w_qkv_out[:, column : column + 128] = source[i, :, t % 3 * 128 : t % 3 * 128 + 128]
    finish(6, r.w_qkv_out, r.o_qkv)

    await_sent(r.small_all.at[:, 0:896], r.sm_s.at[0])
    for block, sem in (
        (r.tok_all.at[0:2], r.tk_s), (r.tok_all.at[0], r.tf_s), (r.cot_all.at[0:3], r.ct_s), (r.mlp_all.at[0:2], r.ml_s),
        (r.mlp_all.at[0], r.mg_s), (r.qkv.at[0:3], r.qa_s), (r.mixed.at[0:15], r.mx_s), (r.gm_out.at[0:3], r.gm_s),
        (r.mo_out.at[0:3], r.mo_s), (r.gmixed.at[0:15], r.mf_s), (r.gparts.at[0:3], r.hb_s), (r.ga_out.at[0:3], r.ga_s),
        (r.vec_in.at[0:7], r.v1_s), (r.vec_all.at[0:7], r.v2_s),
    ):
        await_sent(block, sem.at[0])
    for name, _ in WEIGHTS:
        await_sent(ref(name, "_all").at[0:7, 0:64], ref("sent_", name).at[0])
        await_sent(ref(name, "_all").at[:, 0:64], ref("sent_", name).at[1])
    for name, _ in GRADS:
        await_sent(ref("n_", name), ref("near_s_", name).at[0])
        await_sent(ref("a_", name).at[0:3], ref("first_s_", name).at[0])
        await_sent(ref("m_", name).at[0:3], ref("second_s_", name).at[0])
        if name != "two":
            not_when(at_home, lambda: await_sent(ref("r_", name), ref("last_s_", name).at[0]))
            pl.when(at_home)(lambda: await_sent(ref("r_", name).at[0:3], ref("last_s_", name).at[0]))
    not_when(two_stays, lambda: two_copy().wait_send())
    for copy in results:
        copy.wait()


PLAIN = ("layer_out", "input_grad", "o_qkv", "o_out", "o_one", "o_two")


def owner_kernel(*refs):
    c, s, core, x, yl = place()
    vec, outs = refs[6], refs[7:]
    for i in range(6):
        outs[i][...] = refs[i][...]
    mine = pltpu.roll(vec[...], 128 - core * 64 - s * 8, 1)
    for i in range(8):
        outs[6 + i][...] = mine[i : i + 1, 0:8]
    up = pltpu.roll(vec[pl.ds(8 + 2 * core + x // 2, 1), :], 128 - lax.rem(s, 4) * 32, 1)
    outs[14][...] = up[:, 0:32]


def owner_call(f):
    arrays = [getattr(f, name) for name in PLAIN]
    shapes = [jax.ShapeDtypeStruct(a.shape, a.dtype) for a in arrays]
    shapes += [jax.ShapeDtypeStruct((1, 8), F32)] * 8 + [jax.ShapeDtypeStruct((1, 32), F32)]
    return pl.pallas_call(
        owner_kernel,
        name="owner",
        out_shape=shapes,
        in_specs=[pl.BlockSpec(memory_space=VMEM)] * 7,
        out_specs=[pl.BlockSpec(memory_space=VMEM)] * 15,
    )(*arrays, f.o_vec)


def named_call(kernel, name, cid, ins, outs, scratch, operands):
    results = pl.pallas_call(
        kernel,
        name=name,
        out_shape=[jax.ShapeDtypeStruct(shape, dtype) for _, _, shape, dtype in outs],
        in_specs=[pl.BlockSpec(memory_space=space) for _, space in ins],
        out_specs=[pl.BlockSpec(memory_space=space) for _, space, _, _ in outs],
        scratch_shapes=[kind for _, kind in scratch],
        compiler_params=pltpu.CompilerParams(
            collective_id=cid, has_side_effects=True, vmem_limit_bytes=60 << 20
        ),
    )(*[operands[name] for name, _ in ins])
    return SimpleNamespace(**dict(zip([o[0] for o in outs], results, strict=True)))


def shards(
    tokens,
    lengths,
    block_pairs,
    ln1_gain,
    ln1_bias,
    w_qkv,
    query_bias,
    value_bias,
    w_out,
    out_bias,
    ln2_gain,
    ln2_bias,
    w_fc1,
    fc1_bias,
    w_fc2,
    fc2_bias,
    out_cotangent,
):
    f = named_call(
        layer_kernel,
        "layer",
        0,
        LAYER_IN,
        LAYER_OUT,
        LAYER_SCRATCH,
        dict(
            lengths=lengths,
            block_pairs=block_pairs,
            tok=tokens.reshape(128, 1024),
            ln1_gain=ln1_gain.reshape(1, 128),
            ln1_bias=ln1_bias.reshape(1, 128),
            query_bias=query_bias.reshape(1, 128),
            value_bias=value_bias.reshape(1, 128),
            out_bias=out_bias.reshape(1, 128),
            ln2_gain=ln2_gain.reshape(1, 128),
            ln2_bias=ln2_bias.reshape(1, 128),
            fc2_bias=fc2_bias.reshape(1, 128),
            fc1_bias=fc1_bias.reshape(4, 128),
            w_qkv=w_qkv,
            w_out=w_out,
            w_fc1=w_fc1,
            w_fc2=w_fc2,
            cot=out_cotangent.reshape(128, 1024),
        ),
    )
    layer_out, input_grad, g_qkv, g_out, g_one, g_two, *vecs = owner_call(f)
    out_b, gain_two, bias_two, fc2_b, query_b, value_b, gain_one, bias_one, up = [v.reshape(-1) for v in vecs]
    return (
        layer_out.reshape(tokens.shape),
        input_grad.reshape(tokens.shape),
        gain_one,
        bias_one,
        g_qkv,
        query_b,
        value_b,
        g_out,
        out_b,
        gain_two,
        bias_two,
        g_one,
        up,
        g_two,
        fc2_b,
    )


def solution(mesh):
    one, both = P("shard"), P(("ctx", "shard"))
    rows, both_rows = P("shard", None), P(("ctx", "shard"), None)
    whole = P("ctx", "shard", None, None)
    return jax.shard_map(
        shards,
        mesh=mesh,
        in_specs=(
            whole, one, P(), one, one, rows, one, one, rows, one, one, one, rows, one, rows, one, whole,
        ),
        out_specs=(
            whole, whole, both, both, both_rows, both, both, both_rows, both, both, both,
            both_rows, both, both_rows, both,
        ),
        check_vma=False,
    )
```

```python
from types import SimpleNamespace

import jax
import jax.numpy as jnp
from jax import lax
from jax.experimental import pallas as pl
from jax.experimental.pallas import tpu as pltpu
from jax.sharding import PartitionSpec as P

HEADS = 16
HEAD_DIM = 64
MESH = pl.DeviceIdType.MESH
ANY = pl.ANY
VMEM = pltpu.VMEM
F32 = jnp.float32
BF16 = jnp.bfloat16

eps_norm = 1e-05
negative = -1e30


def place():
    c, s = lax.axis_index("ctx"), lax.axis_index("shard")
    return c, s, lax.rem(c, 2), s // 2, lax.rem(s, 2)


def sibling(c):
    return c + 1 - 2 * lax.rem(c, 2)


def norm_back(grad_normed, normed, inverse, gain):
    scaled = grad_normed * gain
    centred = scaled - jnp.mean(scaled, axis=-1, keepdims=True)
    return inverse * (centred - normed * jnp.mean(scaled * normed, axis=-1, keepdims=True))


def dot(left, right):
    return jnp.dot(left, right, preferred_element_type=F32)


def dot_tn(left, right):
    return lax.dot_general(left, right, (((0,), (0,)), ((), ())), preferred_element_type=F32)


def pick(value, unit):
    return pl.multiple_of(value * unit, unit)


def loop(count, body, first=0):
    def step(k, carry):
        body(k)
        return carry

    lax.fori_loop(first, count, step, 0)


def remote(src, dst, send_sem, recv_sem, device):
    return pltpu.make_async_remote_copy(
        src_ref=src,
        dst_ref=dst,
        send_sem=send_sem,
        recv_sem=recv_sem,
        device_id=device,
        device_id_type=MESH,
    )


def not_when(condition, body):
    pl.when(jnp.logical_not(condition))(body)


def norm_rows(rows):
    centre = rows - jnp.mean(rows, axis=-1, keepdims=True)
    inverse = lax.rsqrt(jnp.mean(centre * centre, axis=-1, keepdims=True) + eps_norm)
    return centre * inverse, inverse


def dot_nt(left, right):
    return lax.dot_general(left, right, (((1,), (1,)), ((), ())), preferred_element_type=F32)


VECTORS = (
    "ln1_gain", "ln1_bias", "query_bias", "value_bias", "out_bias", "ln2_gain", "ln2_bias", "fc2_bias",
)

LAYER_IN = (
    ("lengths", VMEM),
    ("block_pairs", VMEM),
    ("tok", ANY),
    *[(name, VMEM) for name in VECTORS],
    ("fc1_bias", VMEM),
    ("w_qkv", ANY),
    ("w_out", ANY),
    ("w_fc1", ANY),
    ("w_fc2", ANY),
    ("cot", ANY),
)

LAYER_OUT = (
    ("layer_out", ANY, (128, 1024), BF16),
    ("input_grad", ANY, (128, 1024), BF16),
    ("o_qkv", ANY, (8, 3072), F32),
    ("o_out", ANY, (8, 1024), F32),
    ("o_one", ANY, (8, 4096), F32),
    ("o_two", ANY, (32, 1024), F32),
    ("o_vec", ANY, (16, 128), F32),
)

WEIGHTS = (("wq", 768), ("wo", 1024), ("w1", 1024), ("w2", 1024))
GRADS = (("two", 1024), ("one", 1024), ("out", 1024), ("qka", 384), ("qkb", 384))

LAYER_SCRATCH = (
    *[(name + "_all", pltpu.VMEM((8, 128, width), BF16)) for name, width in WEIGHTS],
    *[
        (prefix + name, pltpu.VMEM((*shape, width), BF16))
        for name, width in GRADS
        for prefix, shape in (
            ("g_", (8, 2, 64)), ("n_", (8, 64)), ("a_", (4, 4, 32)), ("b_", (4, 4, 32)), ("m_", (4, 32)), ("h_", (4, 32)),
        )
    ],
    *[("s_" + name, pltpu.VMEM((32, width), F32)) for name, width in GRADS],
    *[
        (name, pltpu.VMEM(shape, BF16))
        for name, shape in (
            ("tok_all", (4, 128, 1024)), ("attn_all", (4, 128, 1024)), ("cot_all", (4, 128, 1024)),
            ("qkv", (4, 4, 64, 384)), ("parts", (4, 4, 64, 384)),
            ("probs", (2, 1024, 1024)), ("mixed", (16, 64, 128)), ("mix_rows", (2, 64, 1024)),
            ("mlp_all", (4, 128, 1024)), ("act_all", (4, 128, 1024)), ("gp_all", (4, 128, 1024)),
            ("gm_out", (4, 128, 1024)), ("mo_out", (4, 128, 1024)), ("gm_in", (4, 128, 1024)),
            ("mo_in", (4, 128, 1024)), ("hidden_low", (128, 1024)), ("gmix", (2, 64, 1024)),
            ("gmixed", (16, 64, 128)), ("gparts", (4, 4, 64, 384)), ("gback", (4, 4, 64, 384)),
            ("gqkv", (4, 128, 768)), ("ga_out", (4, 128, 1024)), ("ga_in", (4, 128, 1024)), ("ga_via", (4, 64, 1024)),
            ("w_layer", (128, 1024)), ("w_input", (128, 1024)),
        )
    ],
    *[
        (name, pltpu.VMEM(shape, F32))
        for name, shape in (
            ("small", (16, 128)), ("small_all", (16, 1024)), ("places", (1024, 128)), ("key_places", (1024, 128)), ("mix_t", (128, 1024)),
            ("hidden", (128, 1024)), ("gm_own", (128, 1024)), ("mo_own", (128, 1024)),
            ("grad_hidden", (128, 1024)), ("ga_own", (128, 1024)), ("gq_t", (128, 1024)), ("delta", (2, 1024)),
            ("r_two", (32, 1024)), ("r_one", (4, 8, 1024)), ("r_out", (4, 8, 1024)), ("r_qka", (4, 8, 384)),
            ("r_qkb", (4, 8, 384)), ("w_qkv_out", (8, 3072)), ("w_out_out", (8, 1024)), ("w_one_out", (8, 4096)),
            ("w_vec_out", (16, 128)),
            ("vec", (16, 1024)), ("vec_sib", (16, 1024)), ("vec_in", (8, 16, 128)), ("vec_sum", (16, 128)),
            ("vec_all", (8, 16, 128)),
        )
    ],
    *[
        (prefix + name, pltpu.SemaphoreType.DMA((count,)))
        for name, _ in WEIGHTS
        for prefix, count in (("sent_", 2), ("along_", 4), ("up_", 1), ("cross_", 1))
    ],
    *[
        (prefix + name, pltpu.SemaphoreType.DMA((1,)))
        for name, _ in GRADS
        for prefix in ("near_s_", "near_r_", "first_s_", "first_r_", "second_s_", "second_r_", "last_s_", "last_r_")
    ],
    *[
        (name + end, pltpu.SemaphoreType.DMA((1,)))
        for name in ("sm", "tf", "qa", "mx", "mg", "gm", "mo", "mf", "hb", "ga", "vs", "v1", "v2")
        for end in ("_s", "_r")
    ],
    *[
        (name, pltpu.SemaphoreType.DMA((count,)))
        for name, count in (
            ("local", 7), ("done", 7), ("tk_s", 1), ("tk_r", 4), ("ct_s", 1), ("ct_r", 4), ("ml_s", 1), ("ml_r", 4),
            ("gv_r", 4),
        )
    ],
)


def layer_kernel(*refs):
    names = [n[0] for n in LAYER_IN + LAYER_OUT + LAYER_SCRATCH]
    r = SimpleNamespace(**dict(zip(names, refs, strict=True)))
    ref = lambda *name: getattr(r, "".join(name))
    c, s, core, x, yl = place()
    z, yh, q4 = c // 4, lax.rem(c // 2, 2), lax.rem(c, 4)
    sib = (sibling(c), s)
    mate_s = s + 1 - 2 * yl
    half = lambda which: pl.ds(pick(which, 64), 64)

    pieces = [(r.w_qkv, r.wq_all, t * 1024 + z * 256, t * 256, 256) for t in range(3)]
    pieces += [(r.w_fc1, r.w1_all, t * 512 + z * 128, t * 128, 128) for t in range(8)]
    own = [
        pltpu.make_async_copy(
            weight.at[half(core), pl.ds(pl.multiple_of(source, 128), width)],
            whole.at[s, half(core), target : target + width],
            r.local.at[0 if i < 3 else 1],
        )
        for i, (weight, whole, source, target, width) in enumerate(pieces)
    ]
    own.append(pltpu.make_async_copy(r.w_out.at[half(core)], r.wo_all.at[s, half(core)], r.local.at[2]))
    own.append(
        pltpu.make_async_copy(r.w_fc2.at[half(2 * z + core)], r.w2_all.at[s, half(core)], r.local.at[3])
    )
    own.append(pltpu.make_async_copy(r.cot, r.cot_all.at[z], r.local.at[4]))
    own.append(pltpu.make_async_copy(r.tok, r.tok_all.at[z], r.local.at[5]))

    barrier = pltpu.get_barrier_semaphore()

    def hail(device):
        pl.semaphore_signal(barrier, inc=1, device_id=device, device_id_type=MESH)

    to_z, from_x, from_yl = 2 * yl + lax.rem(x, 2), x // 2 * 2 + lax.rem(z, 2), z // 2
    at_home = to_z == z
    two_to = (to_z * 4 + yh * 2 + z // 2, (lax.rem(z, 2) * 2 + core) * 2 + x // 2)
    two_from = (
        (core * 2 + x // 2) * 4 + yh * 2 + lax.rem(x, 2),
        (yl * 2 + lax.rem(z, 2)) * 2 + z // 2,
    )
    two_stays = (two_to[0] == c) & (two_to[1] == s)
    loop(8, lambda k: hail((c, lax.rem(s + k, 8))), 1)
    loop(16, lambda k: hail((lax.rem(c + k, 16), s)), 1)
    hail((c + 2 - 4 * yh, mate_s))
    loop(4, lambda k: not_when(at_home & (k == z), lambda: hail((k * 4 + q4, 2 * from_x + from_yl))))
    not_when(two_stays, lambda: hail(two_from))
    for copy in own:
        copy.start()

    for i, name in enumerate(VECTORS):
        r.small[i : i + 1, :] = ref(name)[...].astype(F32)
    r.small[8:12, :] = r.fc1_bias[...].astype(F32)
    r.small[12:16, :] = jnp.zeros((4, 128), F32)


    def own_here(whole, sem):
        block = whole.at[s, half(core)]
        pltpu.make_async_copy(block, block, r.local.at[sem]).wait()

    own_here(r.wq_all, 0)
    pl.semaphore_wait(barrier, 28 - at_home.astype(jnp.int32) - two_stays.astype(jnp.int32))

    def await_block(dst, recv_sem):
        remote(dst, dst, r.local.at[6], recv_sem, sib).wait_recv()

    def await_sent(block, send_sem):
        remote(block, block, send_sem, r.local.at[6], sib).wait_send()

    columns_of = lambda which: pl.ds(pick(which, 128), 128)
    z_peer = lambda k: (lax.rem(c + 4 * k, 16), s)
    x_peer = lambda k: (c, 2 * lax.rem(x + k, 4) + yl)

    def small_to(k):
        return remote(
            r.small, r.small_all.at[:, columns_of(s)], r.sm_s.at[0], r.sm_r.at[0], (c, lax.rem(s + k, 8))
        )

    halves = {1: (slice(0, 64), slice(64, 128)), 3: (slice(64, 128), slice(0, 64))}

    def tok_to(k, h):
        rows = halves[k][h]
        return remote(r.tok.at[rows], r.tok_all.at[z, rows], r.tk_s.at[0], r.tk_r.at[k - h], z_peer(k))

    def cot_to(k):
        return remote(r.cot, r.cot_all.at[z], r.ct_s.at[0], r.ct_r.at[k], z_peer(k))

    z_of = lambda hop: lax.rem(z - hop + 4, 4)

    def pass_on(whole, send_sems, recv_sems, k):
        block = whole.at[z_of(k), halves[k][0]]
        return remote(block, block, send_sems.at[0], recv_sems.at[0], z_peer(k))

    def ring_arrived(whole, recv_sems, send_next, recv_next, k):
        @pl.when(k == 1)
        def _():
            for j in (1, 3):
                await_block(whole.at[z_of(j), halves[j][0]], recv_sems.at[j])
                pass_on(whole, send_next, recv_next, j).start()
            for j in (1, 3):
                await_block(whole.at[z_of(j), halves[j][1]], recv_sems.at[j - 1])

        @pl.when(k == 3)
        def _():
            await_block(whole.at[z_of(2)], recv_next.at[0])

    y_next = lambda p: (c + (2 - 4 * yh) * p, mate_s)
    some_rows = lambda p: pl.ds(pick(2 * core + p, 32), 32)

    def weight_along(name, kind, k):
        whole = ref(name, "_all")
        block = whole.at[s if kind == "own_" else mate_s, half(core)]
        return remote(
            block, block, ref("sent_", name).at[0], ref("along_", name).at[0 if name == "wo" else k], x_peer(k)
        )

    def weight_up(name, k, p):
        block = ref(name, "_all").at[2 * lax.rem(x - k + 4, 4) + yl, some_rows(p)]
        return remote(block, block, ref("sent_", name).at[0], ref("up_", name).at[0], y_next(p))

    def weight_cross(name, k, other):
        block = ref(name, "_all").at[2 * lax.rem(x - k + 4, 4) + (1 - yl if other else yl), half(core)]
        return remote(block, block, ref("sent_", name).at[1], ref("cross_", name).at[0], sib)

    def weight_own(name):
        for p in range(2):
            weight_up(name, 0, p).start()
        for k in (1, 3, 2):
            weight_along(name, "own_", k).start()

    def await_along(name, k):
        block = ref(name, "_all").at[2 * lax.rem(x - k + 4, 4) + yl, half(core)]
        await_block(block, ref("along_", name).at[k])

    def weight_far(name):
        if name == "wo":
            await_block(ref(name, "_all").at[mate_s, half(core)], ref("up_", name).at[0])
            for k in (1, 3, 2):
                weight_along(name, "far_", k).start()
        else:
            for k in (1, 3, 2):
                await_along(name, k)
                for p in range(2):
                    weight_up(name, k, p).start()
                weight_cross(name, k, False).start()
            weight_cross(name, 0, False).start()

    def weight_across(name):
        if name == "wo":
            await_block(ref(name, "_all").at[0:6, 0:64], ref("along_", name).at[0])
            for k in range(4):
                weight_cross(name, k, False).start()
        else:
            await_block(ref(name, "_all").at[0:4, 0:64], ref("up_", name).at[0])
        for k in range(4):
            weight_cross(name, k, True).start()

    def weight_ready(name):
        await_block(ref(name, "_all").at[:, half(1 - core)], ref("cross_", name).at[0])

    for h in range(2):
        for k in (1, 3):
            tok_to(k, h).start()
    weight_own("wq")
    loop(8, lambda k: small_to(k).start(), 1)
    r.small_all[:, columns_of(s)] = r.small[...]
    weight_far("wq")

    sub = lax.broadcasted_iota(jnp.int32, (64, 128), 0)

    pair_lane = lax.broadcasted_iota(jnp.int32, (1, 16), 1)

    def set_places(k):
        pair = jnp.sum(jnp.where(pair_lane == k, r.block_pairs[...], 0), axis=1, keepdims=True)
        block = jnp.where(sub < 32, pair, 31 - pair)
        r.places[pl.ds(pick(k, 64), 64), :] = (block * 32 + lax.rem(sub, 32)).astype(F32)

    loop(16, set_places)
    length = jnp.where(yh == 0, r.lengths[:, 0:1], r.lengths[:, 1:2]).astype(F32)
    r.key_places[...] = jnp.where(r.places[...] < length, r.places[...], 2048.0)
    await_block(r.small_all.at[:, 0:896], r.sm_r.at[0])
    weight_across("wq")
    own_here(r.w1_all, 1)
    for copy in own[11:14]:
        copy.wait()
    weight_own("wo")
    weight_own("w1")

    gain_one, bias_one = r.small_all[0:1, :], r.small_all[1:2, :]
    head_cols = pl.ds(pick(z, 256), 256)
    bias_qkv = (r.small_all[2:3, head_cols], None, r.small_all[3:4, head_cols])

    def parts_to(m, origin):
        peer = lax.rem(q4 + m, 4)
        return remote(
            r.qkv.at[peer, origin],
            r.parts.at[origin, q4],
            r.qa_s.at[0],
            r.qa_r.at[0],
            (4 * z + peer, s),
        )

    def norm_block(origin):
        normed, _ = norm_rows(r.tok_all[origin].astype(F32))
        r.attn_all[origin] = (normed * gain_one + bias_one).astype(BF16)

    def hop_of(k):
        return k + (k // 2) * (1 - 2 * lax.rem(k, 2))

    own[14].wait()
    norm_block(z)

    def norm_next(k):
        ring_arrived(r.tok_all, r.tk_r, r.tf_s, r.tf_r, k)
        norm_block(z_of(hop_of(k)))

    loop(4, norm_next, 1)
    weight_ready("wq")

    def qkv_block(k):
        hop = hop_of(k)
        origin = z_of(hop)
        for t in range(3):
            cols = slice(t * 256, t * 256 + 256)
            acc = dot(r.attn_all[origin], r.wq_all[:, :, cols].reshape(1024, 256))
            if bias_qkv[t] is not None:
                acc = acc + bias_qkv[t]
            acc = acc.astype(BF16)
            for j in range(2):
                for p in range(2):
                    r.qkv[j * 2 + p, origin, :, t * 128 : t * 128 + 128] = acc[
                        j * 64 : j * 64 + 64, p * 128 : p * 128 + 128
                    ]
        for m in (1, 2, 3):
            parts_to(m, origin).start()
        r.parts[origin, q4] = r.qkv[q4, origin]

    loop(4, qkv_block)
    weight_far("wo")
    for k in (1, 3, 2):
        cot_to(k).start()
    weight_own("w2")

    await_block(r.parts.at[0:3], r.qa_r.at[0])
    weight_far("w1")

    head_lane = lax.broadcasted_iota(jnp.int32, (1, 128), 1) // 64
    value_t = r.parts[:, :, :, 256:384].reshape(1024, 128).T

    def masked(rows, h):
        return jnp.where(head_lane == h, rows, jnp.zeros_like(rows))

    def pair_columns(which):
        return columns_of(which // 4 * 2 + lax.rem(which, 2))

    def slot_of(which):
        return lax.rem(which // 2, 2)

    def mix_to(peer):
        return remote(
            r.mixed.at[peer], r.mix_rows.at[yh, :, pair_columns(c)], r.mx_s.at[0], r.mx_r.at[0], (peer, s)
        )

    def attend(k):
        i = lax.rem(z + k + 1, 4)
        keys = r.parts[:, :, :, 128:256].reshape(1024, 128)
        query_place = r.places[pl.ds(pick(i, 256), 256), :].T[0:1, :]
        key_place = r.key_places[...]
        allowed = jnp.concatenate([key_place, key_place], axis=1) <= query_place
        queries = r.parts[i, :, :, 0:128].reshape(256, 128) * jnp.asarray(0.125, BF16)
        cols = pl.ds(pick(i, 256), 256)
        for h in range(2):
            scores = jnp.where(allowed, dot_nt(keys, masked(queries, h)), negative)
            powers = jnp.exp(scores - jnp.max(scores, axis=0, keepdims=True))
            low = (powers * (1.0 / jnp.sum(powers, axis=0, keepdims=True))).astype(BF16)
            r.probs[h, :, cols] = low
            r.mix_t[h * 64 : h * 64 + 64, cols] = dot(value_t[h * 64 : h * 64 + 64], low)
        r.mixed[pl.ds(4 * i, 4)] = r.mix_t[:, cols].T.astype(BF16).reshape(4, 64, 128)
        for q in range(4):
            not_when(4 * i + q == c, lambda: mix_to(4 * i + q).start())

    loop(4, attend)

    r.mix_rows[yh, :, pair_columns(c)] = r.mixed[c]
    weight_across("wo")
    weight_far("w2")
    weight_across("w1")
    weight_ready("wo")

    await_block(r.mixed.at[0:15], r.mx_r.at[0])

    mix = r.mix_rows[...].reshape(128, 1024)
    hidden = r.tok_all[z].astype(F32) + (dot(mix, r.wo_all[...].reshape(1024, 1024)) + r.small_all[4:5, :])
    r.hidden[...] = hidden
    normed, _ = norm_rows(hidden)
    r.mlp_all[z] = (normed * r.small_all[5:6, :] + r.small_all[6:7, :]).astype(BF16)

    def mlp_to(k, h):
        block = r.mlp_all.at[z, halves[k][h]]
        return remote(block, block, r.ml_s.at[0], r.ml_r.at[k - h], z_peer(k))

    for h in range(2):
        for k in (1, 3):
            mlp_to(k, h).start()
    weight_across("w2")
    weight_ready("w1")
    weight_ready("w2")

    r.vec[...] = jnp.zeros_like(r.vec)
    up_row = pl.ds(8 + z, 1)
    upper = lax.broadcasted_iota(jnp.int32, (128, 1), 0) < 64
    row_length = jnp.where(upper, r.lengths[:, 0:1], r.lengths[:, 1:2]).astype(F32)

    def valid_of(origin):
        mine = r.places[half(origin * 4 + q4), 0:1]
        return (jnp.concatenate([mine, mine], axis=0) < row_length).astype(F32)

    def part_to(out, into, sems, k):
        return remote(out.at[lax.rem(z + k, 4)], into.at[k], sems[0].at[0], sems[1].at[0], z_peer(k))

    gm_sems, mo_sems = (r.gm_s, r.gm_r), (r.mo_s, r.mo_r)

    def mlp_block(k):
        hop = hop_of(k)
        origin = z_of(hop)
        ring_arrived(r.mlp_all, r.ml_r, r.mg_s, r.mg_r, k)

        @pl.when(k > 0)
        def _():
            await_block(r.cot_all.at[origin], r.ct_r.at[hop])

        r.cot_all[origin] = (r.cot_all[origin].astype(F32) * valid_of(origin)).astype(BF16)
        for i in range(4):
            cols = slice(i * 256, i * 256 + 256)
            pre = dot(r.mlp_all[origin], r.w1_all[:, :, cols].reshape(1024, 256)) + r.small_all[up_row, cols]
            spread = 0.5 * (1.0 + lax.erf(pre * 0.7071067811865476))
            r.act_all[origin, :, cols] = (pre * spread).astype(BF16)
            slope = spread + pre * (0.3989422804014327 * jnp.exp(-0.5 * pre * pre))
            grad = dot_nt(r.cot_all[origin], r.w2_all[2 * i : 2 * i + 2].reshape(256, 1024)) * slope
            r.vec[up_row, cols] += jnp.sum(grad, axis=0, keepdims=True)
            r.gp_all[origin, :, cols] = grad.astype(BF16)
        for i in range(4):
            cols = slice(i * 256, i * 256 + 256)
            part = dot_nt(r.gp_all[origin], r.w1_all[2 * i : 2 * i + 2].reshape(256, 1024))
            r.gm_out[origin, :, cols] = part.astype(BF16)

            @pl.when(k == 0)
            def _():
                r.gm_own[:, cols] = part

        @pl.when(k > 0)
        def _():
            part_to(r.gm_out, r.gm_in, gm_sems, 4 - hop).start()

    loop(4, mlp_block)

    def mlp_out(origin):
        for i in range(4):
            cols = slice(i * 256, i * 256 + 256)
            part = dot(r.act_all[origin], r.w2_all[:, :, cols].reshape(1024, 256))
            r.mo_out[origin, :, cols] = part.astype(BF16)

            @pl.when(origin == z)
            def _():
                r.mo_own[:, cols] = part

    def outer(name, left, right, width, first=0):
        into = ref("g_", name)

        def body(i):
            rows = pl.ds(pick(i, 256), 256)
            part = dot_tn(
                left[:, :, rows].reshape(512, 256), right[:, :, first : first + width].reshape(512, width)
            )
            into[pl.ds(2 * i, 2)] = part.astype(BF16).reshape(2, 2, 64, width)

        loop(4, body)

    def near_to(which):
        name = GRADS[which][0]
        return remote(
            ref("g_", name).at[:, 1 - core], ref("n_", name), ref("near_s_", name).at[0], ref("near_r_", name).at[0], sib
        )

    def y_peer(k):
        yh_to, yl_to = (1 - yh if k // 2 else yh), (1 - yl if k % 2 else yl)
        return (c + 2 * (yh_to - yh), s + yl_to - yl), 2 * yh_to + yl_to

    here = {"x": x, "y": 2 * yh + yl}
    order = {"two": "xy", "one": "yx", "out": "xy", "qka": "xy", "qkb": "yx"}

    def peer_of(axis, k):
        return (x_peer(k), lax.rem(x + k, 4)) if axis == "x" else y_peer(k)

    def first_to(name, k):
        device, index = peer_of(order[name][0], k)
        sems = ref("first_s_", name), ref("first_r_", name)
        return remote(ref("a_", name).at[index], ref("b_", name).at[k], sems[0].at[0], sems[1].at[0], device)

    def second_to(name, k):
        device, index = peer_of(order[name][1], k)
        sems = ref("second_s_", name), ref("second_r_", name)
        return remote(ref("m_", name).at[index], ref("h_", name).at[k], sems[0].at[0], sems[1].at[0], device)

    def pair_sum(which):
        name = GRADS[which][0]
        grad, near, into = ref("g_", name), ref("n_", name), ref("a_", name)
        await_block(near, ref("near_r_", name).at[0])

        def add(j):
            y_to = lax.rem(j, 2) * 2 + j // 4
            for xh in range(2):
                x_to = 2 * xh + lax.rem(j // 2, 2)
                rows = slice(32 * xh, 32 * xh + 32)
                total = near[j, rows].astype(F32) + grad[j, core, rows].astype(F32)
                target = (x_to, y_to) if order[name] == "xy" else (y_to, x_to)
                into[target[0], target[1]] = total.astype(BF16)

        loop(8, add)
        for k in (1, 3, 2):
            first_to(name, k).start()

    def first_sum(name):
        mine, others, into = ref("a_", name), ref("b_", name), ref("m_", name)
        await_block(others.at[1:4], ref("first_r_", name).at[0])

        def add(j):
            total = mine[here[order[name][0]], j].astype(F32)
            for k in (1, 2, 3):
                total = total + others[k, j].astype(F32)
            into[j] = total.astype(BF16)

        loop(4, add)
        for k in (1, 3, 2):
            second_to(name, k).start()

    def second_sum(name):
        mine, others = ref("m_", name), ref("h_", name)
        await_block(others.at[1:4], ref("second_r_", name).at[0])
        total = mine[here[order[name][1]]].astype(F32)
        for k in (1, 2, 3):
            total = total + others[k].astype(F32)
        ref("s_", name)[...] = total

    outer("two", r.act_all, r.cot_all, 1024)
    near_to(0).start()
    outer("one", r.mlp_all, r.gp_all, 1024)
    near_to(1).start()
    loop(4, mlp_out)

    total = r.gm_own[...]
    await_block(r.gm_in.at[1:4], r.gm_r.at[0])
    for k in (1, 3, 2):
        total = total + r.gm_in[k].astype(F32)
    normed, inverse = norm_rows(r.hidden[...])
    grad_out = r.cot_all[z].astype(F32)
    grad_hidden = grad_out + norm_back(total, normed, inverse, r.small_all[5:6, :])
    r.grad_hidden[...] = grad_hidden
    r.hidden_low[...] = grad_hidden.astype(BF16)
    r.gm_own[...] = total
    for i in range(4):
        part = dot_nt(r.hidden_low[...], r.wo_all[2 * i : 2 * i + 2].reshape(256, 1024))
        r.gmix[:, :, i * 256 : i * 256 + 256] = part.astype(BF16).reshape(2, 64, 256)

    def gmix_to(k):
        peer = lax.rem(c + k, 16)
        return remote(
            r.gmix.at[slot_of(peer), :, pair_columns(peer)], r.gmixed.at[c], r.mf_s.at[0], r.mf_r.at[0], (peer, s)
        )

    loop(16, lambda k: gmix_to(k).start(), 1)
    r.gmixed[c] = r.gmix[yh, :, pair_columns(c)]

    def out_rows(i):
        rows = pl.ds(pick(i, 256), 256)
        part = dot_tn(r.mix_rows[:, :, rows].reshape(128, 256), r.hidden_low[...])
        r.g_out[pl.ds(2 * i, 2)] = part.astype(BF16).reshape(2, 2, 64, 1024)

    pair_sum(0)
    total = r.gm_own[...]
    normed, _ = norm_rows(r.hidden[...])
    for i, rows in enumerate((r.grad_hidden[...], total * normed, total, r.cot_all[z].astype(F32))):
        r.vec[i : i + 1, :] = jnp.sum(rows, axis=0, keepdims=True)
    loop(4, out_rows)
    near_to(2).start()
    await_block(r.gmixed.at[0:15], r.mf_r.at[0])
    for k in (1, 3, 2):
        part_to(r.mo_out, r.mo_in, mo_sems, k).start()

    def back_to(m, piece, i):
        peer = lax.rem(q4 + m, 4)
        cols = slice(piece * 128, piece * 128 + 128)
        return remote(
            r.gparts.at[i, peer, :, cols],
            r.gback.at[q4, i, :, cols],
            r.hb_s.at[0],
            r.hb_r.at[0],
            (4 * z + peer, s),
        )

    def back_start(piece, i):
        for m in (1, 2, 3):
            back_to(m, piece, i).start()

    def values_back(i):
        gm = r.gmixed[...].reshape(1024, 128)
        rows = pl.ds(pick(i, 256), 256)
        acc = dot(r.probs[0, rows], masked(gm, 0)) + dot(r.probs[1, rows], masked(gm, 1))
        r.gparts[i, :, :, 256:384] = acc.astype(BF16).reshape(4, 64, 128)
        back_start(2, i)
        return jnp.sum(acc, axis=0, keepdims=True)

    bias_v = lax.fori_loop(0, 4, lambda i, acc: acc + values_back(i), jnp.zeros((1, 128), F32))
    products = r.gmixed[...].reshape(1024, 128).astype(F32).T * r.mix_t[...]
    for h in range(2):
        r.delta[h : h + 1, :] = jnp.sum(products[h * 64 : h * 64 + 64], axis=0, keepdims=True)
    keys_t = r.parts[:, :, :, 128:256].reshape(1024, 128).T

    def scores_back(i):
        cols = pl.ds(pick(i, 256), 256)
        values = r.parts[:, :, :, 256:384].reshape(1024, 128)
        gm = r.gmixed[pl.ds(i * 4, 4)].reshape(256, 128)
        for h in range(2):
            grad = dot_nt(values, masked(gm, h)) - r.delta[h : h + 1, cols]
            low = (r.probs[h, :, cols].astype(F32) * grad).astype(BF16)
            r.probs[h, :, cols] = low
            r.gq_t[h * 64 : h * 64 + 64, cols] = dot(keys_t[h * 64 : h * 64 + 64], low)
        gq = r.gq_t[:, cols].T * 0.125
        r.gparts[i, :, :, 0:128] = gq.astype(BF16).reshape(4, 64, 128)
        back_start(0, i)
        return jnp.sum(gq, axis=0, keepdims=True)

    bias_q = lax.fori_loop(0, 4, lambda i, acc: acc + scores_back(i), jnp.zeros((1, 128), F32))

    def keys_back(i):
        queries = r.parts[:, :, :, 0:128].reshape(1024, 128) * jnp.asarray(0.125, BF16)
        rows = pl.ds(pick(i, 256), 256)
        acc = dot(r.probs[0, rows], masked(queries, 0)) + dot(r.probs[1, rows], masked(queries, 1))
        r.gparts[i, :, :, 128:256] = acc.astype(BF16).reshape(4, 64, 128)
        back_start(1, i)

    pair_sum(2)
    loop(4, keys_back)
    r.gback[q4] = r.gparts[:, q4]
    wide = lax.broadcasted_iota(jnp.int32, (1, 1024), 1) // 128 == 2 * z + core
    for i, sums in ((4, bias_q), (5, bias_v)):
        r.vec[i : i + 1, :] = jnp.where(wide, jnp.concatenate([sums] * 8, axis=1), 0.0)

    pair_sum(1)
    first_sum("two")
    await_block(r.gback.at[0:3], r.hb_r.at[0])

    def assemble(origin):
        for t in range(3):
            for j in range(2):
                for p in range(2):
                    r.gqkv[origin, j * 64 : j * 64 + 64, t * 256 + p * 128 : t * 256 + p * 128 + 128] = r.gback[
                        j * 2 + p, origin, :, t * 128 : t * 128 + 128
                    ]

    loop(4, assemble)

    def attn_back(hop):
        origin = lax.rem(z + hop, 4)
        normed, _ = norm_rows(r.tok_all[origin].astype(F32))
        for i in range(4):
            cols = slice(i * 256, i * 256 + 256)
            part = dot_nt(r.gqkv[origin], r.wq_all[2 * i : 2 * i + 2].reshape(256, 768))
            r.ga_out[origin, :, cols] = part.astype(BF16)
            r.vec[6:7, cols] += jnp.sum(part * normed[:, cols], axis=0, keepdims=True)
            r.vec[7:8, cols] += jnp.sum(part, axis=0, keepdims=True)

            @pl.when(hop == 0)
            def _():
                r.ga_own[:, cols] = part

    def via_to(k):
        return remote(
            r.ga_out.at[lax.rem(z + 2, 4), halves[k][0]], r.ga_via.at[k], r.ga_s.at[0], r.gv_r.at[k], z_peer(k)
        )

    def via_add(k):
        await_block(r.ga_via.at[k], r.gv_r.at[k])
        target, rows = lax.rem(z + k, 4), halves[k][0]
        total = r.ga_out[target, rows].astype(F32) + r.ga_via[k].astype(F32)
        r.ga_out[target, rows] = total.astype(BF16)
        ga_to(k, 0).start()

    def ga_to(k, h):
        rows = halves[k][h]
        return remote(
            r.ga_out.at[lax.rem(z + k, 4), rows], r.ga_in.at[k, rows], r.ga_s.at[0], r.ga_r.at[0], z_peer(k)
        )

    attn_back(2)
    via_to(1).start()
    via_to(3).start()
    loop(2, lambda k: attn_back(1 + 2 * k))
    ga_to(1, 1).start()
    ga_to(3, 1).start()
    attn_back(0)
    vec_across = remote(r.vec, r.vec_sib, r.vs_s.at[0], r.vs_r.at[0], sib)
    vec_across.start()
    outer("qka", r.attn_all, r.gqkv, 384)
    near_to(3).start()
    outer("qkb", r.attn_all, r.gqkv, 384, 384)
    near_to(4).start()
    via_add(1)
    via_add(3)
    await_block(r.vec_sib, r.vs_r.at[0])
    await_sent(r.vec_sib, r.vs_s.at[0])
    r.vec[...] += r.vec_sib[...]
    chip = c // 2

    def vec_to(k):
        peer = lax.rem(chip + k, 8)
        return remote(r.vec.at[:, columns_of(peer)], r.vec_in.at[k], r.v1_s.at[0], r.v1_r.at[0], (2 * peer + core, s))

    loop(8, lambda k: vec_to(k).start(), 1)
    pair_sum(3)
    pair_sum(4)
    total = r.mo_own[...] + r.small_all[7:8, :]
    await_block(r.mo_in.at[1:4], r.mo_r.at[0])
    for k in (1, 3, 2):
        total = total + r.mo_in[k].astype(F32)
    r.w_layer[...] = (valid_of(z) * (r.hidden[...] + total)).astype(BF16)
    results = [pltpu.make_async_copy(r.w_layer, r.layer_out, r.done.at[0])]
    results[0].start()


    my_part = pl.ds(pick(lax.rem(x, 2) * 2 + yl, 8), 8)

    def last_to(name, k):
        rows = slice(8 * k, 8 * k + 8)
        sems = ref("last_s_", name), ref("last_r_", name)
        device = (to_z * 4 + q4, 2 * (x // 2 * 2 + k // 2) + k % 2)
        return remote(ref("s_", name).at[rows], ref("r_", name).at[z], sems[0].at[0], sems[1].at[0], device)

    def at_owner(k):
        return at_home & (lax.rem(x, 2) == k // 2) & (yl == k % 2)

    def spread(name):
        for k in range(4):
            not_when(at_owner(k), lambda: last_to(name, k).start())

        @pl.when(at_home)
        def _():
            ref("r_", name)[z] = ref("s_", name)[my_part]

    def two_copy():
        return remote(r.s_two, r.r_two, r.last_s_two.at[0], r.last_r_two.at[0], two_to)

    def finish(which, source, target):
        results.append(pltpu.make_async_copy(source, target, r.done.at[which]))
        results[-1].start()

    first_sum("one")
    second_sum("two")
    not_when(two_stays, lambda: two_copy().start())

    @pl.when(two_stays)
    def _():
        r.r_two[...] = r.s_two[...]

    second_sum("one")
    spread("one")
    first_sum("out")

    await_block(r.vec_in.at[1:8], r.v1_r.at[0])
    sums = r.vec[:, columns_of(chip)]
    for k in range(1, 8):
        sums = sums + r.vec_in[k]
    r.vec_sum[...] = sums

    def vec_rows_to(k):
        return remote(r.vec_sum, r.vec_all.at[s], r.v2_s.at[0], r.v2_r.at[0], (c, lax.rem(s + k, 8)))

    loop(8, lambda k: vec_rows_to(k).start(), 1)
    r.vec_all[s] = sums
    first_sum("qka")
    first_sum("qkb")
    second_sum("out")
    spread("out")

    total = r.ga_own[...]
    await_block(r.ga_in.at[0:2], r.ga_r.at[0])
    for k in (1, 3):
        total = total + r.ga_in[k].astype(F32)
    normed, inverse = norm_rows(r.tok_all[z].astype(F32))
    r.w_input[...] = (
        r.grad_hidden[...] + norm_back(total, normed, inverse, r.small_all[0:1, :])
    ).astype(BF16)
    finish(1, r.w_input, r.input_grad)

    second_sum("qka")
    spread("qka")
    second_sum("qkb")
    spread("qkb")

    def rows_arrived(name):
        into = ref("r_", name)
        not_when(at_home, lambda: await_block(into, ref("last_r_", name).at[0]))
        pl.when(at_home)(lambda: await_block(into.at[0:3], ref("last_r_", name).at[0]))

    not_when(two_stays, lambda: await_block(r.r_two, r.last_r_two.at[0]))
    finish(2, r.r_two, r.o_two)
    rows_arrived("one")
    for i in range(4):
        for t in range(8):
            r.w_one_out[:, t * 512 + i * 128 : t * 512 + i * 128 + 128] = r.r_one[i, :, t * 128 : t * 128 + 128]
    finish(3, r.w_one_out, r.o_one)
    rows_arrived("out")
    r.w_out_out[...] = (r.r_out[0] + r.r_out[1]) + (r.r_out[2] + r.r_out[3])
    finish(4, r.w_out_out, r.o_out)
    await_block(r.vec_all.at[0:7], r.v2_r.at[0])
    total = r.vec_all[0]
    for i in range(1, 8):
        total = total + r.vec_all[i]
    r.w_vec_out[...] = total
    finish(5, r.w_vec_out, r.o_vec)
    rows_arrived("qka")
    rows_arrived("qkb")
    for i in range(4):
        for t in range(6):
            source = r.r_qka if t < 3 else r.r_qkb
            column = t // 2 * 1024 + i * 256 + t % 2 * 128
            r.w_qkv_out[:, column : column + 128] = source[i, :, t % 3 * 128 : t % 3 * 128 + 128]
    finish(6, r.w_qkv_out, r.o_qkv)

    await_sent(r.small_all.at[:, 0:896], r.sm_s.at[0])
    for block, sem in (
        (r.tok_all.at[0:2], r.tk_s), (r.tok_all.at[0], r.tf_s), (r.cot_all.at[0:3], r.ct_s), (r.mlp_all.at[0:2], r.ml_s),
        (r.mlp_all.at[0], r.mg_s), (r.qkv.at[0:3], r.qa_s), (r.mixed.at[0:15], r.mx_s), (r.gm_out.at[0:3], r.gm_s),
        (r.mo_out.at[0:3], r.mo_s), (r.gmixed.at[0:15], r.mf_s), (r.gparts.at[0:3], r.hb_s), (r.ga_out.at[0:3], r.ga_s),
        (r.vec_in.at[0:7], r.v1_s), (r.vec_all.at[0:7], r.v2_s),
    ):
        await_sent(block, sem.at[0])
    for name, _ in WEIGHTS:
        await_sent(ref(name, "_all").at[0:7, 0:64], ref("sent_", name).at[0])
        await_sent(ref(name, "_all").at[:, 0:64], ref("sent_", name).at[1])
    for name, _ in GRADS:
        await_sent(ref("n_", name), ref("near_s_", name).at[0])
        await_sent(ref("a_", name).at[0:3], ref("first_s_", name).at[0])
        await_sent(ref("m_", name).at[0:3], ref("second_s_", name).at[0])
        if name != "two":
            not_when(at_home, lambda: await_sent(ref("r_", name), ref("last_s_", name).at[0]))
            pl.when(at_home)(lambda: await_sent(ref("r_", name).at[0:3], ref("last_s_", name).at[0]))
    not_when(two_stays, lambda: two_copy().wait_send())
    for copy in results:
        copy.wait()


PLAIN = ("layer_out", "input_grad", "o_qkv", "o_out", "o_one", "o_two")


def owner_kernel(*refs):
    c, s, core, x, yl = place()
    vec, outs = refs[6], refs[7:]
    for i in range(6):
        outs[i][...] = refs[i][...]
    mine = pltpu.roll(vec[...], 128 - core * 64 - s * 8, 1)
    for i in range(8):
        outs[6 + i][...] = mine[i : i + 1, 0:8]
    up = pltpu.roll(vec[pl.ds(8 + 2 * core + x // 2, 1), :], 128 - lax.rem(s, 4) * 32, 1)
    outs[14][...] = up[:, 0:32]


def owner_call(f):
    arrays = [getattr(f, name) for name in PLAIN]
    shapes = [jax.ShapeDtypeStruct(a.shape, a.dtype) for a in arrays]
    shapes += [jax.ShapeDtypeStruct((1, 8), F32)] * 8 + [jax.ShapeDtypeStruct((1, 32), F32)]
    return pl.pallas_call(
        owner_kernel,
        name="owner",
        out_shape=shapes,
        in_specs=[pl.BlockSpec(memory_space=VMEM)] * 7,
        out_specs=[pl.BlockSpec(memory_space=VMEM)] * 15,
    )(*arrays, f.o_vec)


def named_call(kernel, name, cid, ins, outs, scratch, operands):
    results = pl.pallas_call(
        kernel,
        name=name,
        out_shape=[jax.ShapeDtypeStruct(shape, dtype) for _, _, shape, dtype in outs],
        in_specs=[pl.BlockSpec(memory_space=space) for _, space in ins],
        out_specs=[pl.BlockSpec(memory_space=space) for _, space, _, _ in outs],
        scratch_shapes=[kind for _, kind in scratch],
        compiler_params=pltpu.CompilerParams(
            collective_id=cid, has_side_effects=True, vmem_limit_bytes=60 << 20
        ),
    )(*[operands[name] for name, _ in ins])
    return SimpleNamespace(**dict(zip([o[0] for o in outs], results, strict=True)))


def shards(
    tokens,
    lengths,
    block_pairs,
    ln1_gain,
    ln1_bias,
    w_qkv,
    query_bias,
    value_bias,
    w_out,
    out_bias,
    ln2_gain,
    ln2_bias,
    w_fc1,
    fc1_bias,
    w_fc2,
    fc2_bias,
    out_cotangent,
):
    f = named_call(
        layer_kernel,
        "layer",
        0,
        LAYER_IN,
        LAYER_OUT,
        LAYER_SCRATCH,
        dict(
            lengths=lengths.reshape(1, 2),
            block_pairs=block_pairs.reshape(1, 16),
            tok=tokens.reshape(128, 1024),
            ln1_gain=ln1_gain.reshape(1, 128),
            ln1_bias=ln1_bias.reshape(1, 128),
            query_bias=query_bias.reshape(1, 128),
            value_bias=value_bias.reshape(1, 128),
            out_bias=out_bias.reshape(1, 128),
            ln2_gain=ln2_gain.reshape(1, 128),
            ln2_bias=ln2_bias.reshape(1, 128),
            fc2_bias=fc2_bias.reshape(1, 128),
            fc1_bias=fc1_bias.reshape(4, 128),
            w_qkv=w_qkv,
            w_out=w_out,
            w_fc1=w_fc1,
            w_fc2=w_fc2,
            cot=out_cotangent.reshape(128, 1024),
        ),
    )
    layer_out, input_grad, g_qkv, g_out, g_one, g_two, *vecs = owner_call(f)
    out_b, gain_two, bias_two, fc2_b, query_b, value_b, gain_one, bias_one, up = [v.reshape(-1) for v in vecs]
    return (
        layer_out.reshape(tokens.shape),
        input_grad.reshape(tokens.shape),
        gain_one,
        bias_one,
        g_qkv,
        query_b,
        value_b,
        g_out,
        out_b,
        gain_two,
        bias_two,
        g_one,
        up,
        g_two,
        fc2_b,
    )


def solution(mesh):
    one, both = P("shard"), P(("ctx", "shard"))
    rows, both_rows = P("shard", None), P(("ctx", "shard"), None)
    whole = P("ctx", "shard", None, None)
    return jax.shard_map(
        shards,
        mesh=mesh,
        in_specs=(
            whole, one, P(), one, one, rows, one, one, rows, one, one, one, rows, one, rows, one, whole,
        ),
        out_specs=(
            whole, whole, both, both, both_rows, both, both, both_rows, both, both, both,
            both_rows, both, both_rows, both,
        ),
        check_vma=False,
    )
```

```python
from types import SimpleNamespace

import jax
import jax.numpy as jnp
from jax import lax
from jax.experimental import pallas as pl
from jax.experimental.pallas import tpu as pltpu
from jax.sharding import PartitionSpec as P

HEADS = 16
HEAD_DIM = 64
MESH = pl.DeviceIdType.MESH
ANY = pl.ANY
VMEM = pltpu.VMEM
F32 = jnp.float32
BF16 = jnp.bfloat16

eps_norm = 1e-05
negative = -1e30


def place():
    c, s = lax.axis_index("ctx"), lax.axis_index("shard")
    return c, s, lax.rem(c, 2), s // 2, lax.rem(s, 2)


def sibling(c):
    return c + 1 - 2 * lax.rem(c, 2)


def norm_back(grad_normed, normed, inverse, gain):
    scaled = grad_normed * gain
    centred = scaled - jnp.mean(scaled, axis=-1, keepdims=True)
    return inverse * (centred - normed * jnp.mean(scaled * normed, axis=-1, keepdims=True))


def dot(left, right):
    return jnp.dot(left, right, preferred_element_type=F32)


def dot_tn(left, right):
    return lax.dot_general(left, right, (((0,), (0,)), ((), ())), preferred_element_type=F32)


def pick(value, unit):
    return pl.multiple_of(value * unit, unit)


def loop(count, body, first=0):
    def step(k, carry):
        body(k)
        return carry

    lax.fori_loop(first, count, step, 0)


def remote(src, dst, send_sem, recv_sem, device):
    return pltpu.make_async_remote_copy(
        src_ref=src,
        dst_ref=dst,
        send_sem=send_sem,
        recv_sem=recv_sem,
        device_id=device,
        device_id_type=MESH,
    )


def not_when(condition, body):
    pl.when(jnp.logical_not(condition))(body)


def norm_rows(rows):
    centre = rows - jnp.mean(rows, axis=-1, keepdims=True)
    inverse = lax.rsqrt(jnp.mean(centre * centre, axis=-1, keepdims=True) + eps_norm)
    return centre * inverse, inverse


def dot_nt(left, right):
    return lax.dot_general(left, right, (((1,), (1,)), ((), ())), preferred_element_type=F32)


VECTORS = (
    "ln1_gain", "ln1_bias", "query_bias", "value_bias", "out_bias", "ln2_gain", "ln2_bias", "fc2_bias",
)

LAYER_IN = (
    ("lengths", VMEM),
    ("block_pairs", VMEM),
    ("tok", ANY),
    *[(name, VMEM) for name in VECTORS],
    ("fc1_bias", VMEM),
    ("w_qkv", ANY),
    ("w_out", ANY),
    ("w_fc1", ANY),
    ("w_fc2", ANY),
    ("cot", ANY),
)

LAYER_OUT = (
    ("layer_out", ANY, (128, 1024), BF16),
    ("input_grad", ANY, (128, 1024), BF16),
    ("o_qkv", ANY, (8, 3072), F32),
    ("o_out", ANY, (8, 1024), F32),
    ("o_one", ANY, (8, 4096), F32),
    ("o_two", ANY, (32, 1024), F32),
    ("o_vec", ANY, (16, 128), F32),
)

WEIGHTS = (("wq", 768), ("wo", 1024), ("w1", 1024), ("w2", 1024))
GRADS = (("two", 1024), ("one", 1024), ("out", 1024), ("qka", 384), ("qkb", 384))

LAYER_SCRATCH = (
    *[(name + "_all", pltpu.VMEM((8, 128, width), BF16)) for name, width in WEIGHTS],
    *[
        (prefix + name, pltpu.VMEM((*shape, width), BF16))
        for name, width in GRADS
        for prefix, shape in (
            ("g_", (8, 2, 64)), ("n_", (8, 64)), ("a_", (4, 4, 32)), ("b_", (4, 4, 32)), ("m_", (4, 32)), ("h_", (4, 32)),
        )
    ],
    *[("s_" + name, pltpu.VMEM((32, width), F32)) for name, width in GRADS],
    *[
        (name, pltpu.VMEM(shape, BF16))
        for name, shape in (
            ("tok_all", (4, 128, 1024)), ("attn_all", (4, 128, 1024)), ("cot_all", (4, 128, 1024)),
            ("qkv", (4, 4, 64, 384)), ("parts", (4, 4, 64, 384)),
            ("probs", (2, 1024, 1024)), ("mixed", (16, 64, 128)), ("mix_rows", (2, 64, 1024)),
            ("mlp_all", (4, 128, 1024)), ("act_all", (4, 128, 1024)), ("gp_all", (4, 128, 1024)),
            ("gm_out", (4, 128, 1024)), ("mo_out", (4, 128, 1024)), ("gm_in", (4, 128, 1024)),
            ("mo_in", (4, 128, 1024)), ("hidden_low", (128, 1024)), ("gmix", (2, 64, 1024)),
            ("gmixed", (16, 64, 128)), ("gparts", (4, 4, 64, 384)), ("gback", (4, 4, 64, 384)),
            ("gqkv", (4, 128, 768)), ("ga_out", (4, 128, 1024)), ("ga_in", (4, 128, 1024)), ("ga_via", (4, 64, 1024)),
            ("w_layer", (128, 1024)), ("w_input", (128, 1024)),
        )
    ],
    *[
        (name, pltpu.VMEM(shape, F32))
        for name, shape in (
            ("small", (16, 128)), ("small_all", (16, 1024)), ("places", (1024, 128)), ("key_places", (1024, 128)), ("mix_t", (128, 1024)),
            ("hidden", (128, 1024)), ("gm_own", (128, 1024)), ("mo_own", (128, 1024)),
            ("grad_hidden", (128, 1024)), ("ga_own", (128, 1024)), ("gq_t", (128, 1024)), ("delta", (2, 1024)),
            ("r_two", (32, 1024)), ("r_one", (4, 8, 1024)), ("r_out", (4, 8, 1024)), ("r_qka", (4, 8, 384)),
            ("r_qkb", (4, 8, 384)), ("w_qkv_out", (8, 3072)), ("w_out_out", (8, 1024)), ("w_one_out", (8, 4096)),
            ("w_vec_out", (16, 128)),
            ("vec", (16, 1024)), ("vec_sib", (16, 1024)), ("vec_in", (8, 16, 128)), ("vec_sum", (16, 128)),
            ("vec_all", (8, 16, 128)),
        )
    ],
    *[
        (prefix + name, pltpu.SemaphoreType.DMA((count,)))
        for name, _ in WEIGHTS
        for prefix, count in (("sent_", 2), ("along_", 4), ("up_", 1), ("cross_", 1))
    ],
    *[
        (prefix + name, pltpu.SemaphoreType.DMA((1,)))
        for name, _ in GRADS
        for prefix in ("near_s_", "near_r_", "first_s_", "first_r_", "second_s_", "second_r_", "last_s_", "last_r_")
    ],
    *[
        (name + end, pltpu.SemaphoreType.DMA((1,)))
        for name in ("sm", "tf", "qa", "mx", "mg", "gm", "mo", "mf", "hb", "ga", "vs", "v1", "v2")
        for end in ("_s", "_r")
    ],
    *[
        (name, pltpu.SemaphoreType.DMA((count,)))
        for name, count in (
            ("local", 7), ("done", 7), ("tk_s", 1), ("tk_r", 4), ("ct_s", 1), ("ct_r", 4), ("ml_s", 1), ("ml_r", 4),
            ("gv_r", 4),
        )
    ],
)


def layer_kernel(*refs):
    names = [n[0] for n in LAYER_IN + LAYER_OUT + LAYER_SCRATCH]
    r = SimpleNamespace(**dict(zip(names, refs, strict=True)))
    ref = lambda *name: getattr(r, "".join(name))
    c, s, core, x, yl = place()
    z, yh, q4 = c // 4, lax.rem(c // 2, 2), lax.rem(c, 4)
    sib = (sibling(c), s)
    mate_s = s + 1 - 2 * yl
    half = lambda which: pl.ds(pick(which, 64), 64)

    pieces = [(r.w_qkv, r.wq_all, t * 1024 + z * 256, t * 256, 256) for t in range(3)]
    pieces += [(r.w_fc1, r.w1_all, t * 512 + z * 128, t * 128, 128) for t in range(8)]
    own = [
        pltpu.make_async_copy(
            weight.at[half(core), pl.ds(pl.multiple_of(source, 128), width)],
            whole.at[s, half(core), target : target + width],
            r.local.at[0 if i < 3 else 1],
        )
        for i, (weight, whole, source, target, width) in enumerate(pieces)
    ]
    own.append(pltpu.make_async_copy(r.w_out.at[half(core)], r.wo_all.at[s, half(core)], r.local.at[2]))
    own.append(
        pltpu.make_async_copy(r.w_fc2.at[half(2 * z + core)], r.w2_all.at[s, half(core)], r.local.at[3])
    )
    own.append(pltpu.make_async_copy(r.cot, r.cot_all.at[z], r.local.at[4]))
    own.append(pltpu.make_async_copy(r.tok, r.tok_all.at[z], r.local.at[5]))

    barrier = pltpu.get_barrier_semaphore()

    def hail(device):
        pl.semaphore_signal(barrier, inc=1, device_id=device, device_id_type=MESH)

    to_z, from_x, from_yl = 2 * yl + lax.rem(x, 2), x // 2 * 2 + lax.rem(z, 2), z // 2
    at_home = to_z == z
    two_to = (to_z * 4 + yh * 2 + z // 2, (lax.rem(z, 2) * 2 + core) * 2 + x // 2)
    two_from = (
        (core * 2 + x // 2) * 4 + yh * 2 + lax.rem(x, 2),
        (yl * 2 + lax.rem(z, 2)) * 2 + z // 2,
    )
    two_stays = (two_to[0] == c) & (two_to[1] == s)
    loop(8, lambda k: hail((c, lax.rem(s + k, 8))), 1)
    loop(16, lambda k: hail((lax.rem(c + k, 16), s)), 1)
    hail((c + 2 - 4 * yh, mate_s))
    loop(4, lambda k: not_when(at_home & (k == z), lambda: hail((k * 4 + q4, 2 * from_x + from_yl))))
    not_when(two_stays, lambda: hail(two_from))
    for copy in own:
        copy.start()

    for i, name in enumerate(VECTORS):
        r.small[i : i + 1, :] = ref(name)[...].astype(F32)
    r.small[8:12, :] = r.fc1_bias[...].astype(F32)
    r.small[12:16, :] = jnp.zeros((4, 128), F32)


    def own_here(whole, sem):
        block = whole.at[s, half(core)]
        pltpu.make_async_copy(block, block, r.local.at[sem]).wait()

    own_here(r.wq_all, 0)
    pl.semaphore_wait(barrier, 28 - at_home.astype(jnp.int32) - two_stays.astype(jnp.int32))

    def await_block(dst, recv_sem):
        remote(dst, dst, r.local.at[6], recv_sem, sib).wait_recv()

    def await_sent(block, send_sem):
        remote(block, block, send_sem, r.local.at[6], sib).wait_send()

    columns_of = lambda which: pl.ds(pick(which, 128), 128)
    z_peer = lambda k: (lax.rem(c + 4 * k, 16), s)
    x_peer = lambda k: (c, 2 * lax.rem(x + k, 4) + yl)

    def small_to(k):
        return remote(
            r.small, r.small_all.at[:, columns_of(s)], r.sm_s.at[0], r.sm_r.at[0], (c, lax.rem(s + k, 8))
        )

    halves = {1: (slice(0, 64), slice(64, 128)), 3: (slice(64, 128), slice(0, 64))}

    def tok_to(k, h):
        rows = halves[k][h]
        return remote(r.tok.at[rows], r.tok_all.at[z, rows], r.tk_s.at[0], r.tk_r.at[k - h], z_peer(k))

    def cot_to(k):
        return remote(r.cot, r.cot_all.at[z], r.ct_s.at[0], r.ct_r.at[k], z_peer(k))

    z_of = lambda hop: lax.rem(z - hop + 4, 4)

    def pass_on(whole, send_sems, recv_sems, k):
        block = whole.at[z_of(k), halves[k][0]]
        return remote(block, block, send_sems.at[0], recv_sems.at[0], z_peer(k))

    def ring_arrived(whole, recv_sems, send_next, recv_next, k):
        @pl.when(k == 1)
        def _():
            for j in (1, 3):
                await_block(whole.at[z_of(j), halves[j][0]], recv_sems.at[j])
                pass_on(whole, send_next, recv_next, j).start()
            for j in (1, 3):
                await_block(whole.at[z_of(j), halves[j][1]], recv_sems.at[j - 1])

        @pl.when(k == 3)
        def _():
            await_block(whole.at[z_of(2)], recv_next.at[0])

    y_next = lambda p: (c + (2 - 4 * yh) * p, mate_s)
    some_rows = lambda p: pl.ds(pick(2 * core + p, 32), 32)

    def weight_along(name, kind, k):
        whole = ref(name, "_all")
        block = whole.at[s if kind == "own_" else mate_s, half(core)]
        return remote(
            block, block, ref("sent_", name).at[0], ref("along_", name).at[0 if name == "wo" else k], x_peer(k)
        )

    def weight_up(name, k, p):
        block = ref(name, "_all").at[2 * lax.rem(x - k + 4, 4) + yl, some_rows(p)]
        return remote(block, block, ref("sent_", name).at[0], ref("up_", name).at[0], y_next(p))

    def weight_cross(name, k, other):
        block = ref(name, "_all").at[2 * lax.rem(x - k + 4, 4) + (1 - yl if other else yl), half(core)]
        return remote(block, block, ref("sent_", name).at[1], ref("cross_", name).at[0], sib)

    def weight_own(name):
        for p in range(2):
            weight_up(name, 0, p).start()
        for k in (1, 3, 2):
            weight_along(name, "own_", k).start()

    def await_along(name, k):
        block = ref(name, "_all").at[2 * lax.rem(x - k + 4, 4) + yl, half(core)]
        await_block(block, ref("along_", name).at[k])

    def weight_far(name):
        if name == "wo":
            await_block(ref(name, "_all").at[mate_s, half(core)], ref("up_", name).at[0])
            for k in (1, 3, 2):
                weight_along(name, "far_", k).start()
        else:
            for k in (1, 3, 2):
                await_along(name, k)
                for p in range(2):
                    weight_up(name, k, p).start()
                weight_cross(name, k, False).start()
            weight_cross(name, 0, False).start()

    def weight_across(name):
        if name == "wo":
            await_block(ref(name, "_all").at[0:6, 0:64], ref("along_", name).at[0])
            for k in range(4):
                weight_cross(name, k, False).start()
        else:
            await_block(ref(name, "_all").at[0:4, 0:64], ref("up_", name).at[0])
        for k in range(4):
            weight_cross(name, k, True).start()

    def weight_ready(name):
        await_block(ref(name, "_all").at[:, half(1 - core)], ref("cross_", name).at[0])

    for h in range(2):
        for k in (1, 3):
            tok_to(k, h).start()
    weight_own("wq")
    loop(8, lambda k: small_to(k).start(), 1)
    r.small_all[:, columns_of(s)] = r.small[...]
    weight_far("wq")

    sub = lax.broadcasted_iota(jnp.int32, (64, 128), 0)

    pair_lane = lax.broadcasted_iota(jnp.int32, (1, 16), 1)

    def set_places(k):
        pair = jnp.sum(jnp.where(pair_lane == k, r.block_pairs[...], 0), axis=1, keepdims=True)
        block = jnp.where(sub < 32, pair, 31 - pair)
        r.places[pl.ds(pick(k, 64), 64), :] = (block * 32 + lax.rem(sub, 32)).astype(F32)

    loop(16, set_places)
    length = jnp.where(yh == 0, r.lengths[:, 0:1], r.lengths[:, 1:2]).astype(F32)
    r.key_places[...] = jnp.where(r.places[...] < length, r.places[...], 2048.0)
    await_block(r.small_all.at[:, 0:896], r.sm_r.at[0])
    weight_across("wq")
    own_here(r.w1_all, 1)
    for copy in own[11:14]:
        copy.wait()
    weight_own("wo")
    weight_own("w1")

    gain_one, bias_one = r.small_all[0:1, :], r.small_all[1:2, :]
    head_cols = pl.ds(pick(z, 256), 256)
    bias_qkv = (r.small_all[2:3, head_cols], None, r.small_all[3:4, head_cols])

    def parts_to(m, origin):
        peer = lax.rem(q4 + m, 4)
        return remote(
            r.qkv.at[peer, origin],
            r.parts.at[origin, q4],
            r.qa_s.at[0],
            r.qa_r.at[0],
            (4 * z + peer, s),
        )

    def norm_block(origin):
        normed, _ = norm_rows(r.tok_all[origin].astype(F32))
        r.attn_all[origin] = (normed * gain_one + bias_one).astype(BF16)

    def hop_of(k):
        return k + (k // 2) * (1 - 2 * lax.rem(k, 2))

    own[14].wait()
    norm_block(z)

    def norm_next(k):
        ring_arrived(r.tok_all, r.tk_r, r.tf_s, r.tf_r, k)
        norm_block(z_of(hop_of(k)))

    loop(4, norm_next, 1)
    weight_ready("wq")

    def qkv_block(k):
        hop = hop_of(k)
        origin = z_of(hop)
        for t in range(3):
            cols = slice(t * 256, t * 256 + 256)
            acc = dot(r.attn_all[origin], r.wq_all[:, :, cols].reshape(1024, 256))
            if bias_qkv[t] is not None:
                acc = acc + bias_qkv[t]
            acc = acc.astype(BF16)
            for j in range(2):
                for p in range(2):
                    r.qkv[j * 2 + p, origin, :, t * 128 : t * 128 + 128] = acc[
                        j * 64 : j * 64 + 64, p * 128 : p * 128 + 128
                    ]
        for m in (1, 2, 3):
            parts_to(m, origin).start()
        r.parts[origin, q4] = r.qkv[q4, origin]

    loop(4, qkv_block)
    weight_far("wo")
    for k in (1, 3, 2):
        cot_to(k).start()
    weight_own("w2")

    await_block(r.parts.at[0:3], r.qa_r.at[0])
    weight_far("w1")

    head_lane = lax.broadcasted_iota(jnp.int32, (1, 128), 1) // 64
    value_t = r.parts[:, :, :, 256:384].reshape(1024, 128).T

    def masked(rows, h):
        return jnp.where(head_lane == h, rows, jnp.zeros_like(rows))

    def pair_columns(which):
        return columns_of(which // 4 * 2 + lax.rem(which, 2))

    def slot_of(which):
        return lax.rem(which // 2, 2)

    def mix_to(peer):
        return remote(
            r.mixed.at[peer], r.mix_rows.at[yh, :, pair_columns(c)], r.mx_s.at[0], r.mx_r.at[0], (peer, s)
        )

    def attend(k):
        i = lax.rem(z + k + 1, 4)
        keys = r.parts[:, :, :, 128:256].reshape(1024, 128)
        query_place = r.places[pl.ds(pick(i, 256), 256), :].T[0:1, :]
        key_place = r.key_places[...]
        allowed = jnp.concatenate([key_place, key_place], axis=1) <= query_place
        queries = r.parts[i, :, :, 0:128].reshape(256, 128) * jnp.asarray(0.125, BF16)
        cols = pl.ds(pick(i, 256), 256)
        for h in range(2):
            scores = jnp.where(allowed, dot_nt(keys, masked(queries, h)), negative)
            powers = jnp.exp(scores - jnp.max(scores, axis=0, keepdims=True))
            low = (powers * (1.0 / jnp.sum(powers, axis=0, keepdims=True))).astype(BF16)
            r.probs[h, :, cols] = low
            r.mix_t[h * 64 : h * 64 + 64, cols] = dot(value_t[h * 64 : h * 64 + 64], low)
        r.mixed[pl.ds(4 * i, 4)] = r.mix_t[:, cols].T.astype(BF16).reshape(4, 64, 128)
        for q in range(4):
            not_when(4 * i + q == c, lambda: mix_to(4 * i + q).start())

    loop(4, attend)

    r.mix_rows[yh, :, pair_columns(c)] = r.mixed[c]
    weight_across("wo")
    weight_far("w2")
    weight_across("w1")
    weight_ready("wo")

    await_block(r.mixed.at[0:15], r.mx_r.at[0])

    mix = r.mix_rows[...].reshape(128, 1024)
    hidden = r.tok_all[z].astype(F32) + (dot(mix, r.wo_all[...].reshape(1024, 1024)) + r.small_all[4:5, :])
    r.hidden[...] = hidden
    normed, _ = norm_rows(hidden)
    r.mlp_all[z] = (normed * r.small_all[5:6, :] + r.small_all[6:7, :]).astype(BF16)

    def mlp_to(k, h):
        block = r.mlp_all.at[z, halves[k][h]]
        return remote(block, block, r.ml_s.at[0], r.ml_r.at[k - h], z_peer(k))

    for h in range(2):
        for k in (1, 3):
            mlp_to(k, h).start()
    weight_across("w2")
    weight_ready("w1")
    weight_ready("w2")

    r.vec[...] = jnp.zeros_like(r.vec)
    up_row = pl.ds(8 + z, 1)
    upper = lax.broadcasted_iota(jnp.int32, (128, 1), 0) < 64
    row_length = jnp.where(upper, r.lengths[:, 0:1], r.lengths[:, 1:2]).astype(F32)

    def valid_of(origin):
        mine = r.places[half(origin * 4 + q4), 0:1]
        return (jnp.concatenate([mine, mine], axis=0) < row_length).astype(F32)

    def part_to(out, into, sems, k):
        return remote(out.at[lax.rem(z + k, 4)], into.at[k], sems[0].at[0], sems[1].at[0], z_peer(k))

    gm_sems, mo_sems = (r.gm_s, r.gm_r), (r.mo_s, r.mo_r)

    def mlp_block(k):
        hop = hop_of(k)
        origin = z_of(hop)
        ring_arrived(r.mlp_all, r.ml_r, r.mg_s, r.mg_r, k)

        @pl.when(k > 0)
        def _():
            await_block(r.cot_all.at[origin], r.ct_r.at[hop])

        r.cot_all[origin] = (r.cot_all[origin].astype(F32) * valid_of(origin)).astype(BF16)
        for i in range(4):
            cols = slice(i * 256, i * 256 + 256)
            pre = dot(r.mlp_all[origin], r.w1_all[:, :, cols].reshape(1024, 256)) + r.small_all[up_row, cols]
            spread = 0.5 * (1.0 + lax.erf(pre * 0.7071067811865476))
            r.act_all[origin, :, cols] = (pre * spread).astype(BF16)
            slope = spread + pre * (0.3989422804014327 * jnp.exp(-0.5 * pre * pre))
            grad = dot_nt(r.cot_all[origin], r.w2_all[2 * i : 2 * i + 2].reshape(256, 1024)) * slope
            r.vec[up_row, cols] += jnp.sum(grad, axis=0, keepdims=True)
            r.gp_all[origin, :, cols] = grad.astype(BF16)
        for i in range(4):
            cols = slice(i * 256, i * 256 + 256)
            part = dot_nt(r.gp_all[origin], r.w1_all[2 * i : 2 * i + 2].reshape(256, 1024))
            r.gm_out[origin, :, cols] = part.astype(BF16)

            @pl.when(k == 0)
            def _():
                r.gm_own[:, cols] = part

        @pl.when(k > 0)
        def _():
            part_to(r.gm_out, r.gm_in, gm_sems, 4 - hop).start()

    loop(4, mlp_block)

    def mlp_out(origin):
        for i in range(4):
            cols = slice(i * 256, i * 256 + 256)
            part = dot(r.act_all[origin], r.w2_all[:, :, cols].reshape(1024, 256))
            r.mo_out[origin, :, cols] = part.astype(BF16)

            @pl.when(origin == z)
            def _():
                r.mo_own[:, cols] = part

    def outer(name, left, right, width, first=0):
        into = ref("g_", name)

        def body(i):
            rows = pl.ds(pick(i, 256), 256)
            part = dot_tn(
                left[:, :, rows].reshape(512, 256), right[:, :, first : first + width].reshape(512, width)
            )
            into[pl.ds(2 * i, 2)] = part.astype(BF16).reshape(2, 2, 64, width)

        loop(4, body)

    def near_to(which):
        name = GRADS[which][0]
        return remote(
            ref("g_", name).at[:, 1 - core], ref("n_", name), ref("near_s_", name).at[0], ref("near_r_", name).at[0], sib
        )

    def y_peer(k):
        yh_to, yl_to = (1 - yh if k // 2 else yh), (1 - yl if k % 2 else yl)
        return (c + 2 * (yh_to - yh), s + yl_to - yl), 2 * yh_to + yl_to

    here = {"x": x, "y": 2 * yh + yl}
    order = {"two": "xy", "one": "yx", "out": "xy", "qka": "xy", "qkb": "yx"}

    def peer_of(axis, k):
        return (x_peer(k), lax.rem(x + k, 4)) if axis == "x" else y_peer(k)

    def first_to(name, k):
        device, index = peer_of(order[name][0], k)
        sems = ref("first_s_", name), ref("first_r_", name)
        return remote(ref("a_", name).at[index], ref("b_", name).at[k], sems[0].at[0], sems[1].at[0], device)

    def second_to(name, k):
        device, index = peer_of(order[name][1], k)
        sems = ref("second_s_", name), ref("second_r_", name)
        return remote(ref("m_", name).at[index], ref("h_", name).at[k], sems[0].at[0], sems[1].at[0], device)

    def pair_sum(which):
        name = GRADS[which][0]
        grad, near, into = ref("g_", name), ref("n_", name), ref("a_", name)
        await_block(near, ref("near_r_", name).at[0])

        def add(j):
            y_to = lax.rem(j, 2) * 2 + j // 4
            for xh in range(2):
                x_to = 2 * xh + lax.rem(j // 2, 2)
                rows = slice(32 * xh, 32 * xh + 32)
                total = near[j, rows].astype(F32) + grad[j, core, rows].astype(F32)
                target = (x_to, y_to) if order[name] == "xy" else (y_to, x_to)
                into[target[0], target[1]] = total.astype(BF16)

        loop(8, add)
        for k in (1, 3, 2):
            first_to(name, k).start()

    def first_sum(name):
        mine, others, into = ref("a_", name), ref("b_", name), ref("m_", name)
        await_block(others.at[1:4], ref("first_r_", name).at[0])

        def add(j):
            total = mine[here[order[name][0]], j].astype(F32)
            for k in (1, 2, 3):
                total = total + others[k, j].astype(F32)
            into[j] = total.astype(BF16)

        loop(4, add)
        for k in (1, 3, 2):
            second_to(name, k).start()

    def second_sum(name):
        mine, others = ref("m_", name), ref("h_", name)
        await_block(others.at[1:4], ref("second_r_", name).at[0])
        total = mine[here[order[name][1]]].astype(F32)
        for k in (1, 2, 3):
            total = total + others[k].astype(F32)
        ref("s_", name)[...] = total

    outer("two", r.act_all, r.cot_all, 1024)
    near_to(0).start()
    outer("one", r.mlp_all, r.gp_all, 1024)
    near_to(1).start()
    loop(4, mlp_out)

    total = r.gm_own[...]
    await_block(r.gm_in.at[1:4], r.gm_r.at[0])
    for k in (1, 3, 2):
        total = total + r.gm_in[k].astype(F32)
    normed, inverse = norm_rows(r.hidden[...])
    grad_out = r.cot_all[z].astype(F32)
    grad_hidden = grad_out + norm_back(total, normed, inverse, r.small_all[5:6, :])
    r.grad_hidden[...] = grad_hidden
    r.hidden_low[...] = grad_hidden.astype(BF16)
    r.gm_own[...] = total
    for i in range(4):
        part = dot_nt(r.hidden_low[...], r.wo_all[2 * i : 2 * i + 2].reshape(256, 1024))
        r.gmix[:, :, i * 256 : i * 256 + 256] = part.astype(BF16).reshape(2, 64, 256)

    def gmix_to(k):
        peer = lax.rem(c + k, 16)
        return remote(
            r.gmix.at[slot_of(peer), :, pair_columns(peer)], r.gmixed.at[c], r.mf_s.at[0], r.mf_r.at[0], (peer, s)
        )

    loop(16, lambda k: gmix_to(k).start(), 1)
    r.gmixed[c] = r.gmix[yh, :, pair_columns(c)]

    def out_rows(i):
        rows = pl.ds(pick(i, 256), 256)
        part = dot_tn(r.mix_rows[:, :, rows].reshape(128, 256), r.hidden_low[...])
        r.g_out[pl.ds(2 * i, 2)] = part.astype(BF16).reshape(2, 2, 64, 1024)

    pair_sum(0)
    total = r.gm_own[...]
    normed, _ = norm_rows(r.hidden[...])
    for i, rows in enumerate((r.grad_hidden[...], total * normed, total, r.cot_all[z].astype(F32))):
        r.vec[i : i + 1, :] = jnp.sum(rows, axis=0, keepdims=True)
    loop(4, out_rows)
    near_to(2).start()
    await_block(r.gmixed.at[0:15], r.mf_r.at[0])

    def back_to(m, piece, i):
        peer = lax.rem(q4 + m, 4)
        cols = slice(piece * 128, piece * 128 + 128)
        return remote(
            r.gparts.at[i, peer, :, cols],
            r.gback.at[q4, i, :, cols],
            r.hb_s.at[0],
            r.hb_r.at[0],
            (4 * z + peer, s),
        )

    def back_start(piece, i):
        for m in (1, 2, 3):
            back_to(m, piece, i).start()

    def values_back(i):
        gm = r.gmixed[...].reshape(1024, 128)
        rows = pl.ds(pick(i, 256), 256)
        acc = dot(r.probs[0, rows], masked(gm, 0)) + dot(r.probs[1, rows], masked(gm, 1))
        r.gparts[i, :, :, 256:384] = acc.astype(BF16).reshape(4, 64, 128)
        back_start(2, i)
        return jnp.sum(acc, axis=0, keepdims=True)

    bias_v = lax.fori_loop(0, 4, lambda i, acc: acc + values_back(i), jnp.zeros((1, 128), F32))
    products = r.gmixed[...].reshape(1024, 128).astype(F32).T * r.mix_t[...]
    for h in range(2):
        r.delta[h : h + 1, :] = jnp.sum(products[h * 64 : h * 64 + 64], axis=0, keepdims=True)
    keys_t = r.parts[:, :, :, 128:256].reshape(1024, 128).T

    def scores_back(i):
        cols = pl.ds(pick(i, 256), 256)
        values = r.parts[:, :, :, 256:384].reshape(1024, 128)
        gm = r.gmixed[pl.ds(i * 4, 4)].reshape(256, 128)
        for h in range(2):
            grad = dot_nt(values, masked(gm, h)) - r.delta[h : h + 1, cols]
            low = (r.probs[h, :, cols].astype(F32) * grad).astype(BF16)
            r.probs[h, :, cols] = low
            r.gq_t[h * 64 : h * 64 + 64, cols] = dot(keys_t[h * 64 : h * 64 + 64], low)
        gq = r.gq_t[:, cols].T * 0.125
        r.gparts[i, :, :, 0:128] = gq.astype(BF16).reshape(4, 64, 128)
        back_start(0, i)
        return jnp.sum(gq, axis=0, keepdims=True)

    for k in (1, 3, 2):
        part_to(r.mo_out, r.mo_in, mo_sems, k).start()
    bias_q = lax.fori_loop(0, 4, lambda i, acc: acc + scores_back(i), jnp.zeros((1, 128), F32))

    def keys_back(i):
        queries = r.parts[:, :, :, 0:128].reshape(1024, 128) * jnp.asarray(0.125, BF16)
        rows = pl.ds(pick(i, 256), 256)
        acc = dot(r.probs[0, rows], masked(queries, 0)) + dot(r.probs[1, rows], masked(queries, 1))
        r.gparts[i, :, :, 128:256] = acc.astype(BF16).reshape(4, 64, 128)
        back_start(1, i)

    pair_sum(2)
    loop(4, keys_back)
    r.gback[q4] = r.gparts[:, q4]
    wide = lax.broadcasted_iota(jnp.int32, (1, 1024), 1) // 128 == 2 * z + core
    for i, sums in ((4, bias_q), (5, bias_v)):
        r.vec[i : i + 1, :] = jnp.where(wide, jnp.concatenate([sums] * 8, axis=1), 0.0)

    pair_sum(1)
    first_sum("two")
    await_block(r.gback.at[0:3], r.hb_r.at[0])

    def assemble(origin):
        for t in range(3):
            for j in range(2):
                for p in range(2):
                    r.gqkv[origin, j * 64 : j * 64 + 64, t * 256 + p * 128 : t * 256 + p * 128 + 128] = r.gback[
                        j * 2 + p, origin, :, t * 128 : t * 128 + 128
                    ]

    loop(4, assemble)

    def attn_back(hop):
        origin = lax.rem(z + hop, 4)
        normed, _ = norm_rows(r.tok_all[origin].astype(F32))
        for i in range(4):
            cols = slice(i * 256, i * 256 + 256)
            part = dot_nt(r.gqkv[origin], r.wq_all[2 * i : 2 * i + 2].reshape(256, 768))
            r.ga_out[origin, :, cols] = part.astype(BF16)
            r.vec[6:7, cols] += jnp.sum(part * normed[:, cols], axis=0, keepdims=True)
            r.vec[7:8, cols] += jnp.sum(part, axis=0, keepdims=True)

            @pl.when(hop == 0)
            def _():
                r.ga_own[:, cols] = part

    def via_to(k):
        return remote(
            r.ga_out.at[lax.rem(z + 2, 4), halves[k][0]], r.ga_via.at[k], r.ga_s.at[0], r.gv_r.at[k], z_peer(k)
        )

    def via_add(k):
        await_block(r.ga_via.at[k], r.gv_r.at[k])
        target, rows = lax.rem(z + k, 4), halves[k][0]
        total = r.ga_out[target, rows].astype(F32) + r.ga_via[k].astype(F32)
        r.ga_out[target, rows] = total.astype(BF16)
        ga_to(k, 0).start()

    def ga_to(k, h):
        rows = halves[k][h]
        return remote(
            r.ga_out.at[lax.rem(z + k, 4), rows], r.ga_in.at[k, rows], r.ga_s.at[0], r.ga_r.at[0], z_peer(k)
        )

    attn_back(2)
    via_to(1).start()
    via_to(3).start()
    outer("qka", r.attn_all, r.gqkv, 384)
    near_to(3).start()
    outer("qkb", r.attn_all, r.gqkv, 384, 384)
    near_to(4).start()
    loop(2, lambda k: attn_back(1 + 2 * k))
    ga_to(1, 1).start()
    ga_to(3, 1).start()
    attn_back(0)
    vec_across = remote(r.vec, r.vec_sib, r.vs_s.at[0], r.vs_r.at[0], sib)
    vec_across.start()
    via_add(1)
    via_add(3)
    await_block(r.vec_sib, r.vs_r.at[0])
    await_sent(r.vec_sib, r.vs_s.at[0])
    r.vec[...] += r.vec_sib[...]
    chip = c // 2

    def vec_to(k):
        peer = lax.rem(chip + k, 8)
        return remote(r.vec.at[:, columns_of(peer)], r.vec_in.at[k], r.v1_s.at[0], r.v1_r.at[0], (2 * peer + core, s))

    loop(8, lambda k: vec_to(k).start(), 1)
    pair_sum(3)
    pair_sum(4)
    total = r.mo_own[...] + r.small_all[7:8, :]
    await_block(r.mo_in.at[1:4], r.mo_r.at[0])
    for k in (1, 3, 2):
        total = total + r.mo_in[k].astype(F32)
    r.w_layer[...] = (valid_of(z) * (r.hidden[...] + total)).astype(BF16)
    results = [pltpu.make_async_copy(r.w_layer, r.layer_out, r.done.at[0])]
    results[0].start()


    my_part = pl.ds(pick(lax.rem(x, 2) * 2 + yl, 8), 8)

    def last_to(name, k):
        rows = slice(8 * k, 8 * k + 8)
        sems = ref("last_s_", name), ref("last_r_", name)
        device = (to_z * 4 + q4, 2 * (x // 2 * 2 + k // 2) + k % 2)
        return remote(ref("s_", name).at[rows], ref("r_", name).at[z], sems[0].at[0], sems[1].at[0], device)

    def at_owner(k):
        return at_home & (lax.rem(x, 2) == k // 2) & (yl == k % 2)

    def spread(name):
        for k in range(4):
            not_when(at_owner(k), lambda: last_to(name, k).start())

        @pl.when(at_home)
        def _():
            ref("r_", name)[z] = ref("s_", name)[my_part]

    def two_copy():
        return remote(r.s_two, r.r_two, r.last_s_two.at[0], r.last_r_two.at[0], two_to)

    def finish(which, source, target):
        results.append(pltpu.make_async_copy(source, target, r.done.at[which]))
        results[-1].start()

    first_sum("one")
    second_sum("two")
    not_when(two_stays, lambda: two_copy().start())

    @pl.when(two_stays)
    def _():
        r.r_two[...] = r.s_two[...]

    second_sum("one")
    spread("one")
    first_sum("out")

    await_block(r.vec_in.at[1:8], r.v1_r.at[0])
    sums = r.vec[:, columns_of(chip)]
    for k in range(1, 8):
        sums = sums + r.vec_in[k]
    r.vec_sum[...] = sums

    def vec_rows_to(k):
        return remote(r.vec_sum, r.vec_all.at[s], r.v2_s.at[0], r.v2_r.at[0], (c, lax.rem(s + k, 8)))

    loop(8, lambda k: vec_rows_to(k).start(), 1)
    r.vec_all[s] = sums
    first_sum("qka")
    first_sum("qkb")
    second_sum("out")
    spread("out")

    total = r.ga_own[...]
    await_block(r.ga_in.at[0:2], r.ga_r.at[0])
    for k in (1, 3):
        total = total + r.ga_in[k].astype(F32)
    normed, inverse = norm_rows(r.tok_all[z].astype(F32))
    r.w_input[...] = (
        r.grad_hidden[...] + norm_back(total, normed, inverse, r.small_all[0:1, :])
    ).astype(BF16)
    finish(1, r.w_input, r.input_grad)

    second_sum("qka")
    spread("qka")
    second_sum("qkb")
    spread("qkb")

    def rows_arrived(name):
        into = ref("r_", name)
        not_when(at_home, lambda: await_block(into, ref("last_r_", name).at[0]))
        pl.when(at_home)(lambda: await_block(into.at[0:3], ref("last_r_", name).at[0]))

    not_when(two_stays, lambda: await_block(r.r_two, r.last_r_two.at[0]))
    finish(2, r.r_two, r.o_two)
    rows_arrived("one")
    for i in range(4):
        for t in range(8):
            r.w_one_out[:, t * 512 + i * 128 : t * 512 + i * 128 + 128] = r.r_one[i, :, t * 128 : t * 128 + 128]
    finish(3, r.w_one_out, r.o_one)
    rows_arrived("out")
    r.w_out_out[...] = (r.r_out[0] + r.r_out[1]) + (r.r_out[2] + r.r_out[3])
    finish(4, r.w_out_out, r.o_out)
    await_block(r.vec_all.at[0:7], r.v2_r.at[0])
    total = r.vec_all[0]
    for i in range(1, 8):
        total = total + r.vec_all[i]
    r.w_vec_out[...] = total
    finish(5, r.w_vec_out, r.o_vec)
    rows_arrived("qka")
    rows_arrived("qkb")
    for i in range(4):
        for t in range(6):
            source = r.r_qka if t < 3 else r.r_qkb
            column = t // 2 * 1024 + i * 256 + t % 2 * 128
            r.w_qkv_out[:, column : column + 128] = source[i, :, t % 3 * 128 : t % 3 * 128 + 128]
    finish(6, r.w_qkv_out, r.o_qkv)

    await_sent(r.small_all.at[:, 0:896], r.sm_s.at[0])
    for block, sem in (
        (r.tok_all.at[0:2], r.tk_s), (r.tok_all.at[0], r.tf_s), (r.cot_all.at[0:3], r.ct_s), (r.mlp_all.at[0:2], r.ml_s),
        (r.mlp_all.at[0], r.mg_s), (r.qkv.at[0:3], r.qa_s), (r.mixed.at[0:15], r.mx_s), (r.gm_out.at[0:3], r.gm_s),
        (r.mo_out.at[0:3], r.mo_s), (r.gmixed.at[0:15], r.mf_s), (r.gparts.at[0:3], r.hb_s), (r.ga_out.at[0:3], r.ga_s),
        (r.vec_in.at[0:7], r.v1_s), (r.vec_all.at[0:7], r.v2_s),
    ):
        await_sent(block, sem.at[0])
    for name, _ in WEIGHTS:
        await_sent(ref(name, "_all").at[0:7, 0:64], ref("sent_", name).at[0])
        await_sent(ref(name, "_all").at[:, 0:64], ref("sent_", name).at[1])
    for name, _ in GRADS:
        await_sent(ref("n_", name), ref("near_s_", name).at[0])
        await_sent(ref("a_", name).at[0:3], ref("first_s_", name).at[0])
        await_sent(ref("m_", name).at[0:3], ref("second_s_", name).at[0])
        if name != "two":
            not_when(at_home, lambda: await_sent(ref("r_", name), ref("last_s_", name).at[0]))
            pl.when(at_home)(lambda: await_sent(ref("r_", name).at[0:3], ref("last_s_", name).at[0]))
    not_when(two_stays, lambda: two_copy().wait_send())
    for copy in results:
        copy.wait()


PLAIN = ("layer_out", "input_grad", "o_qkv", "o_out", "o_one", "o_two")


def owner_kernel(*refs):
    c, s, core, x, yl = place()
    vec, outs = refs[6], refs[7:]
    for i in range(6):
        outs[i][...] = refs[i][...]
    mine = pltpu.roll(vec[...], 128 - core * 64 - s * 8, 1)
    for i in range(8):
        outs[6 + i][...] = mine[i : i + 1, 0:8]
    up = pltpu.roll(vec[pl.ds(8 + 2 * core + x // 2, 1), :], 128 - lax.rem(s, 4) * 32, 1)
    outs[14][...] = up[:, 0:32]


def owner_call(f):
    arrays = [getattr(f, name) for name in PLAIN]
    shapes = [jax.ShapeDtypeStruct(a.shape, a.dtype) for a in arrays]
    shapes += [jax.ShapeDtypeStruct((1, 8), F32)] * 8 + [jax.ShapeDtypeStruct((1, 32), F32)]
    return pl.pallas_call(
        owner_kernel,
        name="owner",
        out_shape=shapes,
        in_specs=[pl.BlockSpec(memory_space=VMEM)] * 7,
        out_specs=[pl.BlockSpec(memory_space=VMEM)] * 15,
    )(*arrays, f.o_vec)


def named_call(kernel, name, cid, ins, outs, scratch, operands):
    results = pl.pallas_call(
        kernel,
        name=name,
        out_shape=[jax.ShapeDtypeStruct(shape, dtype) for _, _, shape, dtype in outs],
        in_specs=[pl.BlockSpec(memory_space=space) for _, space in ins],
        out_specs=[pl.BlockSpec(memory_space=space) for _, space, _, _ in outs],
        scratch_shapes=[kind for _, kind in scratch],
        compiler_params=pltpu.CompilerParams(
            collective_id=cid, has_side_effects=True, vmem_limit_bytes=60 << 20
        ),
    )(*[operands[name] for name, _ in ins])
    return SimpleNamespace(**dict(zip([o[0] for o in outs], results, strict=True)))


def shards(
    tokens,
    lengths,
    block_pairs,
    ln1_gain,
    ln1_bias,
    w_qkv,
    query_bias,
    value_bias,
    w_out,
    out_bias,
    ln2_gain,
    ln2_bias,
    w_fc1,
    fc1_bias,
    w_fc2,
    fc2_bias,
    out_cotangent,
):
    f = named_call(
        layer_kernel,
        "layer",
        0,
        LAYER_IN,
        LAYER_OUT,
        LAYER_SCRATCH,
        dict(
            lengths=lengths.reshape(1, 2),
            block_pairs=block_pairs.reshape(1, 16),
            tok=tokens.reshape(128, 1024),
            ln1_gain=ln1_gain.reshape(1, 128),
            ln1_bias=ln1_bias.reshape(1, 128),
            query_bias=query_bias.reshape(1, 128),
            value_bias=value_bias.reshape(1, 128),
            out_bias=out_bias.reshape(1, 128),
            ln2_gain=ln2_gain.reshape(1, 128),
            ln2_bias=ln2_bias.reshape(1, 128),
            fc2_bias=fc2_bias.reshape(1, 128),
            fc1_bias=fc1_bias.reshape(4, 128),
            w_qkv=w_qkv,
            w_out=w_out,
            w_fc1=w_fc1,
            w_fc2=w_fc2,
            cot=out_cotangent.reshape(128, 1024),
        ),
    )
    layer_out, input_grad, g_qkv, g_out, g_one, g_two, *vecs = owner_call(f)
    out_b, gain_two, bias_two, fc2_b, query_b, value_b, gain_one, bias_one, up = [v.reshape(-1) for v in vecs]
    return (
        layer_out.reshape(tokens.shape),
        input_grad.reshape(tokens.shape),
        gain_one,
        bias_one,
        g_qkv,
        query_b,
        value_b,
        g_out,
        out_b,
        gain_two,
        bias_two,
        g_one,
        up,
        g_two,
        fc2_b,
    )


def solution(mesh):
    one, both = P("shard"), P(("ctx", "shard"))
    rows, both_rows = P("shard", None), P(("ctx", "shard"), None)
    whole = P("ctx", "shard", None, None)
    return jax.shard_map(
        shards,
        mesh=mesh,
        in_specs=(
            whole, one, P(), one, one, rows, one, one, rows, one, one, one, rows, one, rows, one, whole,
        ),
        out_specs=(
            whole, whole, both, both, both_rows, both, both, both_rows, both, both, both,
            both_rows, both, both_rows, both,
        ),
        check_vma=False,
    )
```
